256 devices in a mesh: src: 8 (over z_hi, core), tile: 32 (over y, x, z_lo).
Axes of the slice: x: 4, y: 4, z: 8 (z_hi: 4, z_lo: 2; z = z_hi * 2 + z_lo), core: 2. Of those that a mesh axis runs over, the one named last changes fastest.
Arguments:
- mask_tiles: float32 [32, 512, 512], P('tile'), may hold values from -1 to 1
- target: float32 [32, 512, 512], P('tile'), may hold values from 0 to 0.4
- pupil_gain: float32 [128, 128], replicated, may hold values from 0.5 to 1.5
- weights: float32 [32], P('src'), may hold values from 0.1 to 1
- freq_index: int32 [32, 2, 128], P('src'), may hold values from 0 to 639, as said below
Outputs:
- mask_grad: float32 [32, 512, 512], P('tile', 'src')
- weight_grad: float32 [32], P('src')
The draws below stay inside these ranges and needn't reach their ends.
Inputs may be any that keep to these rules, and one draw needn't show every extreme that they name: freq_index[s, c, k] = (k - 64 - o) mod 640 for k = 0..127, with one integer offset o of -64 to 63 for each source s and coordinate c.
All inputs are finite; a program needn't handle non-finite values.
Results may differ from the reference program's by a relative error of at most 0.0003.
Values sent between devices are 32-bit elements; how exact they have to be, the bound alone decides.
No kernel may reach another device: no remote copies, remote signals or barrier semaphores. Data moves between devices by JAX's collectives and lax.ppermute only.
A program may use at most 128 MiB of HBM per device.

```python
import math
import jax
import jax.numpy as jnp
from jax import lax

P_SIZE = 512
A = 64
K = 128
TCOLS = 8
N = 640
NTILE = 32
TROWS = 4
SRC = 32


def draw_freq_index(key, part):
    key = jax.random.fold_in(key, 7)
    offsets = jax.random.randint(key, (SRC, 2, 1), -(K // 2), K // 2)
    freq_ranks = jnp.arange(K, dtype=jnp.int32)[None, None, :]
    return jnp.mod(freq_ranks - K // 2 - offsets, N).astype(jnp.int32)


def level_of(own_key, shape, shards, smallest, top_value):
    def one(position, parts):
        draws = jax.random.uniform(jax.random.fold_in(jax.random.fold_in(own_key, 6), position), (parts,), jnp.float32, smallest / len(shards), top_value / len(shards))
        return jnp.repeat(jnp.exp(draws), shape[position] // parts).reshape((-1,) + (1,) * (len(shape) - position - 1))

    gain = one(*shards[0])
    for cut in shards[1:]:
        gain = gain * one(*cut)
    return gain


def setup_inputs(seed: int = 0) -> dict:
    arg_keys = jax.random.split(jax.random.key(seed), 6)
    return {
        "mask_tiles": jnp.clip(jax.random.uniform(arg_keys[0], (NTILE, P_SIZE, P_SIZE), jnp.float32, -1.0, 1.0) * level_of(arg_keys[0], (NTILE, P_SIZE, P_SIZE), ((0, 32),), -0.4, 0.0), -1.0, 1.0),
        "target": jnp.clip(0.4 * jax.random.uniform(arg_keys[1], (NTILE, P_SIZE, P_SIZE), jnp.float32) ** level_of(arg_keys[1], (NTILE, P_SIZE, P_SIZE), ((0, 32),), -0.2, 0.2), 0.0, 0.4),
        "pupil_gain": jnp.clip(jax.random.uniform(arg_keys[2], (K, K), jnp.float32, 0.5, 1.5), 0.5, 1.5),
        "weights": jnp.clip(jnp.exp(math.log(1.0) - 2.3025851 * jax.random.uniform(arg_keys[3], (SRC,), jnp.float32) ** level_of(arg_keys[3], (SRC,), ((0, 8),), -0.2, 0.2)), 0.1, 1.0),
        "freq_index": draw_freq_index(jax.random.fold_in(arg_keys[5], 71), 0),
    }


HIGHEST = lax.Precision.HIGHEST

def phase_table(indices, positions, factor, orient):
    phases = jnp.mod(indices.astype(jnp.int32)[:, None] * positions.astype(jnp.int32)[None, :], N)
    angles = phases.astype(jnp.float32) * (2.0 * math.pi / N)
    return (jnp.cos(angles) * factor, orient * jnp.sin(angles) * factor)

def contract(form, first_op, second_op):
    return jnp.einsum(form, first_op, second_op, precision=HIGHEST)

def extend(mask_tiles):
    picture = mask_tiles.reshape(TROWS, TCOLS, P_SIZE, P_SIZE).transpose(0, 2, 1, 3).reshape(TROWS * P_SIZE, TCOLS * P_SIZE)
    padded = jnp.pad(picture, A)
    pieces = [padded[row_at * P_SIZE:row_at * P_SIZE + N, col_at * P_SIZE:col_at * P_SIZE + N] for row_at in range(TROWS) for col_at in range(TCOLS)]
    return jnp.stack(pieces)

def fields(extended, indices, pupil_disc, down_real, down_imag):
    spread = jnp.arange(N, dtype=jnp.int32)
    row_real, row_imag = phase_table(indices[0], spread, 1.0 / math.sqrt(N), -1.0)
    col_real, col_imag = phase_table(indices[1], spread, 1.0 / math.sqrt(N), -1.0)
    upper_real = contract('tpq,kq->tpk', extended, col_real)
    upper_imag = contract('tpq,kq->tpk', extended, col_imag)
    spec_real = contract('kp,tpl->tkl', row_real, upper_real) - contract('kp,tpl->tkl', row_imag, upper_imag)
    spec_imag = contract('kp,tpl->tkl', row_real, upper_imag) + contract('kp,tpl->tkl', row_imag, upper_real)
    spec_real = spec_real * pupil_disc
    spec_imag = spec_imag * pupil_disc
    half_real = contract('tkl,lq->tkq', spec_real, down_real) - contract('tkl,lq->tkq', spec_imag, down_imag)
    half_imag = contract('tkl,lq->tkq', spec_real, down_imag) + contract('tkl,lq->tkq', spec_imag, down_real)
    out_real = contract('kp,tkq->tpq', down_real, half_real) - contract('kp,tkq->tpq', down_imag, half_imag)
    out_imag = contract('kp,tkq->tpq', down_real, half_imag) + contract('kp,tkq->tpq', down_imag, half_real)
    return (out_real, out_imag)

def reference(mask_tiles, target, pupil_gain, weights, freq_index):
    freq_ranks = jnp.arange(K, dtype=jnp.int32) - K // 2
    inside = freq_ranks[:, None] ** 2 + freq_ranks[None, :] ** 2 <= (K // 2) ** 2
    pupil_disc = jnp.where(inside, pupil_gain, jnp.zeros_like(pupil_gain))
    down_real, down_imag = phase_table(jnp.mod(freq_ranks, N), jnp.arange(P_SIZE, dtype=jnp.int32) + A, 1.0 / math.sqrt(K), 1.0)
    extended = extend(mask_tiles)

    def bright(total, source):
        out_real, out_imag = fields(extended, freq_index[source], pupil_disc, down_real, down_imag)
        return (total + weights[source] * (out_real * out_real + out_imag * out_imag), None)
    total, _ = lax.scan(bright, jnp.zeros((NTILE, P_SIZE, P_SIZE), jnp.float32), jnp.arange(SRC, dtype=jnp.int32))
    residual = total / SRC - target

    def adjoint(carry, source):

        def mapping(tiles):
            return fields(extend(tiles), freq_index[source], pupil_disc, down_real, down_imag)
        (out_real, out_imag), pullback = jax.vjp(mapping, mask_tiles)
        factor = 2.0 * weights[source] * residual
        gradient, = pullback((factor * out_real, factor * out_imag))
        energy_sum = jnp.sum(residual * (out_real * out_real + out_imag * out_imag))
        return (carry + gradient, energy_sum)
    grad_total, energy_sums = lax.scan(adjoint, jnp.zeros_like(mask_tiles), jnp.arange(SRC, dtype=jnp.int32))
    return (grad_total, energy_sums * (16.0 / (NTILE * P_SIZE * P_SIZE)))
```

```python
import functools
import math

import jax
import jax.numpy as jnp
import ml_dtypes
import numpy as np
from jax import lax
from jax.experimental import pallas as pl
from jax.experimental.pallas import tpu as pltpu
from jax.sharding import PartitionSpec as P

A = 64
TROWS = 4
TCOLS = 8
PIX = 512
N = PIX + 2 * A
K = 128
W = 256
SOURCES = 4
BF = jnp.bfloat16
F32 = jnp.float32
BOTH = ("src", "tile")


def two_terms(table):
    first = table.astype(np.float32).astype(ml_dtypes.bfloat16)
    rest = (table - first.astype(np.float64)).astype(np.float32)
    return np.stack([first, rest.astype(ml_dtypes.bfloat16)])


def real_basis():
    angles = 2.0 * np.pi / N * np.mod(np.outer(np.arange(N), np.arange(K)), N)
    return np.concatenate([np.cos(angles), np.sin(angles)], axis=1) / math.sqrt(N)


def fold_table():
    ranks = np.arange(W) - K
    parts = np.arange(K)
    same = np.abs(ranks)[None, :] == parts[:, None]
    return np.concatenate([same * 1.0, same * np.sign(ranks)[None, :]], axis=0)


def coarse_table():
    ranks = np.arange(K) - K // 2
    angles = 2.0 * np.pi / W * np.mod(np.outer(ranks, np.arange(W)), W)
    down_real, down_imag = np.cos(angles) / math.sqrt(K), np.sin(angles) / math.sqrt(K)
    return np.block([[down_real, down_imag], [-down_imag, down_real]])


def interpolation():
    ranks = np.arange(1, K)
    shift = (np.arange(PIX) + A)[:, None] / N - np.arange(W)[None, :] / W
    return (1.0 + 2.0 * np.cos(2.0 * np.pi * shift[..., None] * ranks).sum(-1)) / W


def make_tables():
    basis = real_basis()
    fold = fold_table()
    coarse = coarse_table()
    spread = interpolation()
    rims = np.concatenate([basis[:A], basis[N - A :]])
    bf16 = ml_dtypes.bfloat16
    return {
        "mid": two_terms(basis[A : N - A]),
        "mid_t": two_terms(basis[A : N - A].T),
        "all_t": two_terms(basis.T),
        "rims": two_terms(rims),
        "rims_t": two_terms(rims.T),
        "fold": fold.astype(bf16),
        "fold_t": np.ascontiguousarray(fold.T).astype(bf16),
        "coarse": two_terms(coarse),
        "coarse_t": two_terms(coarse.T),
        "spread": two_terms(spread),
        "spread_t": two_terms(spread.T),
        "gram": two_terms(spread.T @ spread),
        "blocks": np.ascontiguousarray(two_terms(basis[A : N - A]).reshape(2, 4, K, W).swapaxes(0, 1)),
        "outer": np.stack([two_terms(basis[N - A :])] * 2 + [two_terms(basis[:A])] * 2),
        "sides_t": np.stack([two_terms(basis[:A].T), two_terms(basis[N - A :].T)]),
    }


def terms(value):
    first = value.astype(BF)
    return first, (value - first.astype(F32)).astype(BF)


def dot(first_op, second_op):
    return jnp.dot(first_op, second_op, preferred_element_type=F32)


def product(first_op, second_op):
    first_hi, first_lo = first_op
    second_hi, second_lo = second_op
    return dot(first_hi, second_hi) + (dot(first_hi, second_lo) + dot(first_lo, second_hi))


def pair_of(ref):
    return ref[0], ref[1]


def exact_left(table, value):
    high, low = terms(value)
    return dot(table, high) + dot(table, low)


def exact_right(value, table):
    high, low = terms(value)
    return dot(high, table) + dot(low, table)


def call(kernel, outs, ins, name, flops, scratch=(), smem=()):
    specs = [
        pl.BlockSpec(memory_space=pltpu.SMEM if at in smem else pltpu.VMEM) for at in range(len(ins))
    ]
    shapes = [jax.ShapeDtypeStruct(shape, F32) for shape in outs]
    moved = 4 * sum(math.prod(shape) for shape in outs) + sum(one.size * one.dtype.itemsize for one in ins)
    return pl.pallas_call(
        kernel,
        out_shape=shapes,
        in_specs=specs,
        out_specs=[pl.BlockSpec(memory_space=pltpu.VMEM) for _ in outs],
        scratch_shapes=list(scratch),
        compiler_params=pltpu.CompilerParams(vmem_limit_bytes=40 * 1024 * 1024),
        cost_estimate=pl.CostEstimate(flops=flops, bytes_accessed=moved, transcendentals=0),
        name=name,
    )(*ins)


def own_kernel(tile_ref, target_ref, mid_ref, mid_t_ref, spread_ref, spread_t_ref, basis_ref, wanted_ref):
    upper = product(terms(tile_ref[0]), pair_of(mid_ref))
    basis_ref[...] = product(pair_of(mid_t_ref), terms(upper))
    upper = product(terms(target_ref[0]), pair_of(spread_ref))
    wanted_ref[...] = product(pair_of(spread_t_ref), terms(upper))


def pack_kernel(at_ref, left_ref, right_ref, mine_ref, other_ref, out_ref):
    first = at_ref[1] == 0
    mine, other = mine_ref[...], other_ref[...]
    up = jnp.where(first, mine, other)
    down = jnp.where(first, other, mine)

    def chosen(left, right):
        return jnp.where(first, right[:, K - A :], left[:, :A])

    up_part = chosen(up[:, :K], up[:, PIX - K :])
    down_part = chosen(down[:, :K], down[:, PIX - K :])
    middle = chosen(left_ref[0], right_ref[0])
    half = N // 2
    top = jnp.concatenate([up_part, middle[: half - A]], axis=0)
    bottom = jnp.concatenate([middle[half - A :], down_part], axis=0)
    out_ref[...] = jnp.concatenate([top, bottom], axis=1)


def rows_kernel(at_ref, basis_ref, mine_ref, other_ref, mid_ref, rims_t_ref, out_ref):
    first = at_ref[1] == 0
    mine, other = mine_ref[...], other_ref[...]
    rim = jnp.concatenate([jnp.where(first, mine, other), jnp.where(first, other, mine)], axis=0)
    upper = product(terms(rim), pair_of(mid_ref))
    out_ref[...] = basis_ref[...] + product(pair_of(rims_t_ref), terms(upper))


def halves(value, core):
    top, bottom = value[:K], value[K:]
    return jnp.where(core == 0, top, bottom), jnp.where(core == 0, bottom, top)


def joined(mine, other, core):
    return jnp.concatenate(
        [jnp.where(core == 0, mine, other), jnp.where(core == 0, other, mine)], axis=0
    )


def disc_of(gain):
    rows = lax.broadcasted_iota(jnp.int32, (K, K), 0) - K // 2
    columns = lax.broadcasted_iota(jnp.int32, (K, K), 1) - K // 2
    return jnp.where(rows * rows + columns * columns <= (K // 2) ** 2, gain, 0.0)


def window_starts(index_ref, source):
    def start(coordinate):
        return jnp.clip(lax.rem(index_ref[source, coordinate, 0] + K, N), 0, K)

    return start(0), start(1)


def image_kernel(
    at_ref,
    index_ref,
    weights_ref,
    basis_ref,
    mine_ref,
    other_ref,
    gain_ref,
    rims_ref,
    all_t_ref,
    fold_ref,
    fold_t_ref,
    coarse_ref,
    coarse_t_ref,
    field_ref,
    keep_ref,
    send_ref,
    real_ref,
    imag_ref,
):
    core = at_ref[1]
    first = core == 0
    mine, other = mine_ref[...], other_ref[...]
    left = jnp.where(first, mine, other)
    right = jnp.where(first, other, mine)
    rim = jnp.concatenate(
        [
            jnp.concatenate([left[:, :A], right[:, :A]], axis=1),
            jnp.concatenate([left[:, A:], right[:, A:]], axis=1),
        ],
        axis=0,
    )
    upper = product(terms(rim), pair_of(rims_ref))
    basis = basis_ref[...] + product(pair_of(all_t_ref), terms(upper))
    zero = jnp.zeros((K, K), F32)
    even = jnp.concatenate(
        [
            jnp.concatenate([basis[:K, :K], zero], axis=1),
            jnp.concatenate([zero, -basis[K:, K:]], axis=1),
        ],
        axis=0,
    )
    odd = jnp.concatenate(
        [
            jnp.concatenate([zero, -basis[:K, K:]], axis=1),
            jnp.concatenate([-basis[K:, :K], zero], axis=1),
        ],
        axis=0,
    )
    fold, fold_t = fold_ref[...], fold_t_ref[...]
    for ref, part in ((real_ref, even), (imag_ref, odd)):
        plane = exact_right(exact_left(fold_t, part), fold)
        ref[0] = plane[:, :K]
        ref[1] = plane[:, K:]
    disc = disc_of(gain_ref[...])
    total = jnp.zeros((W, W), F32)
    for source in range(SOURCES):
        row, column = window_starts(index_ref, source)

        def window(ref):
            rows = jnp.concatenate([ref[0, pl.ds(row, K), :], ref[1, pl.ds(row, K), :]], axis=1)
            return pltpu.roll(rows, lax.rem(W - column, W), 1)[:, :K] * disc

        spec = jnp.concatenate([window(real_ref), window(imag_ref)], axis=1)
        half = product(terms(spec), pair_of(coarse_ref))
        half = jnp.concatenate([half[:, :W], half[:, W:]], axis=0)
        field = product(pair_of(coarse_t_ref), terms(half))
        field_ref[source] = field
        real, imag = field[:W], field[W:]
        total = total + weights_ref[source] * (real * real + imag * imag)
    keep, send = halves(total, core)
    keep_ref[...] = keep
    send_ref[...] = send


def adjoint_kernel(
    at_ref,
    index_ref,
    weights_ref,
    mine_ref,
    other_ref,
    wanted_ref,
    field_ref,
    gain_ref,
    gram_ref,
    fold_ref,
    fold_t_ref,
    coarse_ref,
    coarse_t_ref,
    keep_ref,
    send_ref,
    energy_ref,
    real_ref,
    imag_ref,
):
    core = at_ref[1]
    bright = joined(mine_ref[...], other_ref[...], core)
    gram = pair_of(gram_ref)
    value = product(terms(product(gram, terms(bright))), gram)
    residual = value * (1.0 / (8 * SOURCES)) - wanted_ref[...]
    disc = disc_of(gain_ref[...])
    sides = []
    lanes = lax.broadcasted_iota(jnp.int32, (8, K), 1)
    energies = jnp.zeros((8, K), F32)
    for source in range(SOURCES):
        field = field_ref[source]
        real, imag = field[:W], field[W:]
        scaled = jnp.concatenate([residual * real, residual * imag], axis=1)
        energy = jnp.sum(scaled[:, :W] * real + scaled[:, W:] * imag)
        energies = jnp.where(lanes == source, energy, energies)
        back = product(terms(scaled), pair_of(coarse_t_ref))
        sides.append(jnp.concatenate([back[:, :K], back[:, K:]], axis=0))
    energy_ref[...] = energies
    real_ref[...] = jnp.zeros((2, W, K), F32)
    imag_ref[...] = jnp.zeros((2, W, K), F32)
    pad = jnp.zeros((K, K), F32)
    for couple in range(SOURCES // 2):
        spec = product(pair_of(coarse_ref), terms(jnp.concatenate(sides[2 * couple : 2 * couple + 2], axis=1)))
        for place in range(2):
            source = 2 * couple + place
            row, column = window_starts(index_ref, source)
            scale = disc * (2.0 * weights_ref[source])
            for ref, part in ((real_ref, spec[:K]), (imag_ref, spec[K:])):
                part = part[:, place * K : place * K + K] * scale
                wide = pltpu.roll(jnp.concatenate([part, pad], axis=1), column, 1)
                for side in range(2):
                    ref[side, pl.ds(row, K), :] += wide[:, side * K : side * K + K]
    fold, fold_t = fold_ref[...], fold_t_ref[...]

    def folded(ref):
        return exact_right(exact_left(fold, jnp.concatenate([ref[0], ref[1]], axis=1)), fold_t)

    even, odd = folded(real_ref), folded(imag_ref)
    top = jnp.concatenate([even[:K, :K], -odd[:K, K:]], axis=1)
    bottom = jnp.concatenate([-odd[K:, :K], -even[K:, K:]], axis=1)
    keep_ref[...] = jnp.where(core == 0, top, bottom)
    send_ref[...] = jnp.where(core == 0, bottom, top)


def lines_kernel(at_ref, mine_ref, other_ref, block_ref, outer_ref, lines_ref, rim_ref):
    spectrum = terms(joined(mine_ref[...], other_ref[...], at_ref[1]))
    lines_ref[...] = product((block_ref[0, 0], block_ref[0, 1]), spectrum)
    rim_ref[...] = product((outer_ref[0, 0], outer_ref[0, 1]), spectrum)


def pixels_kernel(at_ref, lines_ref, rim_ref, mid_t_ref, sides_ref, inner_ref, side_ref):
    place, core = at_ref[0], at_ref[1]
    rim = rim_ref[...]
    lines = lines_ref[...]
    top = lines[:A] + jnp.where(place == 0, rim, 0.0)
    bottom = lines[A:] + jnp.where(place == 3, rim, 0.0)
    table = (sides_ref[0, 0], sides_ref[0, 1])
    side_ref[...] = jnp.concatenate([product(terms(top), table), product(terms(bottom), table)], axis=1)
    own = jnp.where(core == 0, top, bottom)
    inner_ref[...] = product(terms(own), pair_of(mid_t_ref))


def join_kernel(at_ref, inner_ref, mine_ref, other_ref, out_ref):
    first = at_ref[1] == 0
    mine, other = mine_ref[...], other_ref[...]
    left = jnp.where(first, other[:, :A], mine[:, A:])
    right = jnp.where(first, mine[:, :A], other[:, A:])
    inner = inner_ref[...]
    pad = jnp.zeros((A, A), F32)
    out_ref[0, :, :K] = inner[:, :K] + jnp.concatenate([left, pad], axis=1)
    out_ref[0, :, K : PIX - K] = inner[:, K : PIX - K]
    out_ref[0, :, PIX - K :] = inner[:, PIX - K :] + jnp.concatenate([pad, right], axis=1)


def swap_cores(value):
    return lax.ppermute(value, "src", [(at, at ^ 1) for at in range(8)])


def swap_chips(value, partner):
    return lax.ppermute(value, "src", [(at, 2 * partner(at // 2) + at % 2) for at in range(8)])


def all_sum(keep, send):
    value = keep + swap_cores(send)
    value = value + swap_chips(value, lambda chip: chip ^ 1)
    value = value + swap_chips(value, lambda chip: 3 - chip)
    return value, swap_cores(value)


def tile_move(value, shift_of):
    pairs = []
    for source in range(8):
        shift = shift_of(source)
        if shift is None:
            continue
        for row in range(TROWS):
            for column in range(TCOLS):
                to_row, to_column = row + shift[0], column + shift[1]
                if 0 <= to_row < TROWS and 0 <= to_column < TCOLS:
                    pairs.append(
                        (source * 32 + row * TCOLS + column, source * 32 + to_row * TCOLS + to_column)
                    )
    return lax.ppermute(value, BOTH, pairs)


def tile_sum(value):
    for bit in (1, 2, 4, 8, 16):
        value = value + lax.ppermute(value, "tile", [(at, at ^ bit) for at in range(TROWS * TCOLS)])
    return value


def body(tables, mask_tiles, target, pupil_gain, weights, freq_index):
    group = lax.axis_index("src").astype(jnp.int32)
    chip, core = group // 2, group % 2
    at = jnp.stack([chip, core])

    edge = jnp.where(core == 0, mask_tiles[0, PIX - A :], mask_tiles[0, :A])
    mine = tile_move(edge, lambda source: (1, 0) if source % 2 == 0 else (-1, 0))
    basis, wanted = call(
        own_kernel,
        [(W, W), (W, W)],
        [mask_tiles, target, tables["mid"], tables["mid_t"], tables["spread"], tables["spread_t"]],
        "own",
        2 * 3 * 2 * (PIX * PIX * W + W * PIX * W),
    )
    other = swap_cores(mine)
    whole = pl.BlockSpec(memory_space=pltpu.VMEM)
    packed = pl.pallas_call(
        pack_kernel,
        out_shape=jax.ShapeDtypeStruct((N // 2, K), F32),
        grid=(1,),
        in_specs=[
            pl.BlockSpec(memory_space=pltpu.SMEM),
            pl.BlockSpec((1, PIX, K), lambda step: (0, 0, 0)),
            pl.BlockSpec((1, PIX, K), lambda step: (0, 0, PIX // K - 1)),
            whole,
            whole,
        ],
        out_specs=whole,
        name="pack",
    )(at, mask_tiles, mask_tiles, mine, other)
    my_side = tile_move(packed, lambda source: (0, 1) if source % 2 == 0 else (0, -1))
    (basis,) = call(
        rows_kernel,
        [(W, W)],
        [at, basis, mine, other, tables["mid"], tables["rims_t"]],
        "rows",
        3 * 2 * (K * PIX * W + W * K * W),
        smem=(0,),
    )
    other_side = swap_cores(my_side)
    plane = pltpu.VMEM((2, W, K), F32)
    field, keep, send = call(
        image_kernel,
        [(SOURCES, 2 * W, W), (K, W), (K, W)],
        [
            at,
            freq_index,
            weights,
            basis,
            my_side,
            other_side,
            pupil_gain,
            tables["rims"],
            tables["all_t"],
            tables["fold"],
            tables["fold_t"],
            tables["coarse"],
            tables["coarse_t"],
        ],
        "image",
        1_500_000_000,
        scratch=(plane, plane),
        smem=(0, 1, 2),
    )
    mine, other = all_sum(keep, send)
    keep, send, energies = call(
        adjoint_kernel,
        [(K, W), (K, W), (8, K)],
        [
            at,
            freq_index,
            weights,
            mine,
            other,
            wanted,
            field,
            pupil_gain,
            tables["gram"],
            tables["fold"],
            tables["fold_t"],
            tables["coarse"],
            tables["coarse_t"],
        ],
        "adjoint",
        1_700_000_000,
        scratch=(plane, plane),
        smem=(0, 1, 2),
    )
    energies = tile_sum(energies)
    mine, other = all_sum(keep, send)
    lines, rim = pl.pallas_call(
        lines_kernel,
        out_shape=[jax.ShapeDtypeStruct((K, W), F32), jax.ShapeDtypeStruct((A, W), F32)],
        grid_spec=pltpu.PrefetchScalarGridSpec(
            num_scalar_prefetch=1,
            grid=(1,),
            in_specs=[
                whole,
                whole,
                pl.BlockSpec((1, 2, K, W), lambda step, at: (at[0], 0, 0, 0)),
                pl.BlockSpec((1, 2, A, W), lambda step, at: (at[0], 0, 0, 0)),
            ],
            out_specs=[whole, whole],
        ),
        name="lines",
    )(at, mine, other, tables["blocks"], tables["outer"])
    from_rows = tile_move(rim, lambda source: {0: (1, 0), 3: (-1, 0)}.get(source // 2))
    inner, side = pl.pallas_call(
        pixels_kernel,
        out_shape=[jax.ShapeDtypeStruct((A, PIX), F32), jax.ShapeDtypeStruct((A, K), F32)],
        grid_spec=pltpu.PrefetchScalarGridSpec(
            num_scalar_prefetch=1,
            grid=(1,),
            in_specs=[
                whole,
                whole,
                whole,
                pl.BlockSpec((1, 2, W, A), lambda step, at: (at[1], 0, 0, 0)),
            ],
            out_specs=[whole, whole],
        ),
        name="pixels",
    )(at, lines, from_rows, tables["mid_t"], tables["sides_t"])
    my_side = tile_move(side, lambda source: (0, -1) if source % 2 == 0 else (0, 1))
    other_side = swap_cores(my_side)
    (mask_grad,) = call(
        join_kernel,
        [(1, A, PIX)],
        [at, inner, my_side, other_side],
        "join",
        A * PIX,
        smem=(0,),
    )
    weight_grad = energies[0, :SOURCES] * (16.0 / (TROWS * TCOLS * PIX * PIX))
    return mask_grad, weight_grad


def solution(mesh):
    placed = (P("tile", None, None), P("tile", None, None), P(), P("src"), P("src", None, None))
    return jax.shard_map(
        functools.partial(body, make_tables()),
        mesh=mesh,
        in_specs=placed,
        out_specs=(P("tile", "src", None), P("src")),
        check_vma=False,
    )
```

```python
import functools
import math

import jax
import jax.numpy as jnp
import ml_dtypes
import numpy as np
from jax import lax
from jax.experimental import pallas as pl
from jax.experimental.pallas import tpu as pltpu
from jax.sharding import PartitionSpec as P

A = 64
TROWS = 4
TCOLS = 8
PIX = 512
N = PIX + 2 * A
K = 128
W = 256
SOURCES = 4
BF = jnp.bfloat16
F32 = jnp.float32
BOTH = ("src", "tile")


def two_terms(table):
    first = table.astype(np.float32).astype(ml_dtypes.bfloat16)
    rest = (table - first.astype(np.float64)).astype(np.float32)
    return np.stack([first, rest.astype(ml_dtypes.bfloat16)])


def real_basis():
    angles = 2.0 * np.pi / N * np.mod(np.outer(np.arange(N), np.arange(K)), N)
    return np.concatenate([np.cos(angles), np.sin(angles)], axis=1) / math.sqrt(N)


def fold_table():
    ranks = np.arange(W) - K
    parts = np.arange(K)
    same = np.abs(ranks)[None, :] == parts[:, None]
    return np.concatenate([same * 1.0, same * np.sign(ranks)[None, :]], axis=0)


def coarse_table():
    ranks = np.arange(K) - K // 2
    angles = 2.0 * np.pi / W * np.mod(np.outer(ranks, np.arange(W)), W)
    down_real, down_imag = np.cos(angles) / math.sqrt(K), np.sin(angles) / math.sqrt(K)
    return np.block([[down_real, down_imag], [-down_imag, down_real]])


def interpolation():
    ranks = np.arange(1, K)
    shift = (np.arange(PIX) + A)[:, None] / N - np.arange(W)[None, :] / W
    return (1.0 + 2.0 * np.cos(2.0 * np.pi * shift[..., None] * ranks).sum(-1)) / W


def make_tables():
    basis = real_basis()
    fold = fold_table()
    coarse = coarse_table()
    spread = interpolation()
    rims = np.concatenate([basis[:A], basis[N - A :]])
    bf16 = ml_dtypes.bfloat16
    return {
        "mid": two_terms(basis[A : N - A]),
        "mid_t": two_terms(basis[A : N - A].T),
        "rims": two_terms(rims),
        "rims_t": two_terms(rims.T),
        "fold": fold.astype(bf16),
        "fold_t": np.ascontiguousarray(fold.T).astype(bf16),
        "coarse": two_terms(coarse),
        "coarse_t": two_terms(coarse.T),
        "spread": two_terms(spread),
        "spread_t": two_terms(spread.T),
        "gram": two_terms(spread.T @ spread),
        "blocks": np.ascontiguousarray(two_terms(basis[A : N - A]).reshape(2, 4, K, W).swapaxes(0, 1)),
        "outer": np.stack([two_terms(basis[N - A :]), two_terms(basis[:A])]),
        "sides_t": np.stack([two_terms(basis[:A].T), two_terms(basis[N - A :].T)]),
    }


def terms(value):
    first = value.astype(BF)
    return first, (value - first.astype(F32)).astype(BF)


def dot(first_op, second_op):
    return jnp.dot(first_op, second_op, preferred_element_type=F32)


def product(first_op, second_op):
    first_hi, first_lo = first_op
    second_hi, second_lo = second_op
    return dot(first_hi, second_hi) + (dot(first_hi, second_lo) + dot(first_lo, second_hi))


def pair_of(ref):
    return ref[0], ref[1]


def exact_left(table, value):
    high, low = terms(value)
    return dot(table, high) + dot(table, low)


def exact_right(value, table):
    high, low = terms(value)
    return dot(high, table) + dot(low, table)


def call(kernel, outs, ins, name, flops, scratch=(), smem=(), hbm=()):
    spaces = dict.fromkeys(smem, pltpu.SMEM) | dict.fromkeys(hbm, pltpu.HBM)
    specs = [pl.BlockSpec(memory_space=spaces.get(at, pltpu.VMEM)) for at in range(len(ins))]
    shapes = [jax.ShapeDtypeStruct(shape, F32) for shape in outs]
    moved = 4 * sum(math.prod(shape) for shape in outs) + sum(one.size * one.dtype.itemsize for one in ins)
    return pl.pallas_call(
        kernel,
        out_shape=shapes,
        in_specs=specs,
        out_specs=[pl.BlockSpec(memory_space=pltpu.VMEM) for _ in outs],
        scratch_shapes=list(scratch),
        compiler_params=pltpu.CompilerParams(vmem_limit_bytes=40 * 1024 * 1024),
        cost_estimate=pl.CostEstimate(flops=flops, bytes_accessed=moved, transcendentals=0),
        name=name,
    )(*ins)


def my_place():
    group = lax.axis_index("src")
    return group // 2, group % 2


def own_kernel(tile_hbm, table_hbm, rows_ref, tile_ref, table_ref, done_ref):
    table_copy = pltpu.make_async_copy(table_hbm, table_ref, done_ref.at[0])
    table_copy.start()
    chunks = []
    for chunk in range(PIX // K):
        part = pl.ds(chunk * K, K)
        chunks.append(pltpu.make_async_copy(tile_hbm.at[0, part], tile_ref.at[part], done_ref.at[1 + chunk]))
        chunks[-1].start()
    table_copy.wait()
    total = jnp.zeros((W, PIX), F32)
    for chunk, copy in enumerate(chunks):
        copy.wait()
        part = slice(chunk * K, chunk * K + K)
        total = total + product((table_ref[0, :, part], table_ref[1, :, part]), terms(tile_ref[part]))
    rows_ref[...] = total


def wanted_kernel(
    target_hbm, spread_hbm, spread_t_hbm, wanted_ref, target_ref, spread_ref, spread_t_ref, done_ref
):
    copies = [
        pltpu.make_async_copy(spread_hbm, spread_ref, done_ref.at[0]),
        pltpu.make_async_copy(target_hbm.at[0], target_ref, done_ref.at[1]),
        pltpu.make_async_copy(spread_t_hbm, spread_t_ref, done_ref.at[2]),
    ]
    for copy in copies:
        copy.start()
    for copy in copies:
        copy.wait()
    upper = product(terms(target_ref[...]), pair_of(spread_ref))
    wanted_ref[...] = product(pair_of(spread_t_ref), terms(upper))


def rows_kernel(rows_ref, mine_ref, other_ref, rims_t_ref, all_ref, side_ref):
    _, core = my_place()
    first = core == 0
    mine, other = mine_ref[...], other_ref[...]
    rim = jnp.concatenate([jnp.where(first, mine, other), jnp.where(first, other, mine)], axis=0)
    rows = rows_ref[...] + product(pair_of(rims_t_ref), terms(rim))
    all_ref[...] = rows
    side = jnp.where(first, rows[:, PIX - A :], rows[:, :A])
    side_ref[...] = jnp.concatenate([side[:K], side[K:]], axis=1)


def columns_kernel(rows_ref, mid_ref, basis_ref):
    basis_ref[...] = product(terms(rows_ref[...]), pair_of(mid_ref))


def halves(value, core):
    top, bottom = value[:K], value[K:]
    return jnp.where(core == 0, top, bottom), jnp.where(core == 0, bottom, top)


def joined(mine, other, core):
    return jnp.concatenate(
        [jnp.where(core == 0, mine, other), jnp.where(core == 0, other, mine)], axis=0
    )


def disc_of(gain):
    rows = lax.broadcasted_iota(jnp.int32, (K, K), 0) - K // 2
    columns = lax.broadcasted_iota(jnp.int32, (K, K), 1) - K // 2
    return jnp.where(rows * rows + columns * columns <= (K // 2) ** 2, gain, 0.0)


def window_starts(index_ref, source):
    def start(coordinate):
        return jnp.clip(lax.rem(index_ref[source, coordinate, 0] + K, N), 0, K)

    return start(0), start(1)


def image_kernel(
    index_ref,
    weights_ref,
    basis_ref,
    mine_ref,
    other_ref,
    gain_ref,
    rims_ref,
    fold_ref,
    fold_t_ref,
    coarse_ref,
    coarse_t_ref,
    field_ref,
    keep_ref,
    send_ref,
    real_ref,
    imag_ref,
):
    _, core = my_place()
    first = core == 0
    mine, other = mine_ref[...], other_ref[...]
    left = jnp.where(first, mine, other)
    right = jnp.where(first, other, mine)
    rim = jnp.concatenate(
        [
            jnp.concatenate([left[:, :A], right[:, :A]], axis=1),
            jnp.concatenate([left[:, A:], right[:, A:]], axis=1),
        ],
        axis=0,
    )
    basis = basis_ref[...] + product(terms(rim), pair_of(rims_ref))
    zero = jnp.zeros((K, K), F32)
    even = jnp.concatenate(
        [
            jnp.concatenate([basis[:K, :K], zero], axis=1),
            jnp.concatenate([zero, -basis[K:, K:]], axis=1),
        ],
        axis=0,
    )
    odd = jnp.concatenate(
        [
            jnp.concatenate([zero, -basis[:K, K:]], axis=1),
            jnp.concatenate([-basis[K:, :K], zero], axis=1),
        ],
        axis=0,
    )
    fold, fold_t = fold_ref[...], fold_t_ref[...]
    for ref, part in ((real_ref, even), (imag_ref, odd)):
        plane = exact_right(exact_left(fold_t, part), fold)
        ref[0] = plane[:, :K]
        ref[1] = plane[:, K:]
    disc = disc_of(gain_ref[...])
    total = jnp.zeros((W, W), F32)
    for source in range(SOURCES):
        row, column = window_starts(index_ref, source)

        def window(ref):
            rows = jnp.concatenate([ref[0, pl.ds(row, K), :], ref[1, pl.ds(row, K), :]], axis=1)
            return pltpu.roll(rows, lax.rem(W - column, W), 1)[:, :K] * disc

        spec = jnp.concatenate([window(real_ref), window(imag_ref)], axis=1)
        half = product(terms(spec), pair_of(coarse_ref))
        half = jnp.concatenate([half[:, :W], half[:, W:]], axis=0)
        field = product(pair_of(coarse_t_ref), terms(half))
        field_ref[source] = field
        real, imag = field[:W], field[W:]
        total = total + weights_ref[source] * (real * real + imag * imag)
    keep, send = halves(total, core)
    keep_ref[...] = keep
    send_ref[...] = send


def residual_kernel(mine_ref, other_ref, wanted_ref, field_ref, gram_ref, residual_ref, energy_ref):
    _, core = my_place()
    bright = joined(mine_ref[...], other_ref[...], core)
    gram = pair_of(gram_ref)
    value = product(terms(product(gram, terms(bright))), gram)
    residual = value * (1.0 / (8 * SOURCES)) - wanted_ref[...]
    residual_ref[...] = residual
    lanes = lax.broadcasted_iota(jnp.int32, (8, K), 1)
    energies = jnp.zeros((8, K), F32)
    for source in range(SOURCES):
        real, imag = field_ref[source, :W], field_ref[source, W:]
        energy = jnp.sum(residual * (real * real + imag * imag))
        energies = jnp.where(lanes == source, energy, energies)
    energy_ref[...] = energies


def adjoint_kernel(
    index_ref,
    weights_ref,
    residual_ref,
    field_ref,
    gain_ref,
    fold_ref,
    fold_t_ref,
    coarse_ref,
    coarse_t_ref,
    keep_ref,
    send_ref,
    real_ref,
    imag_ref,
):
    _, core = my_place()
    residual = residual_ref[...]
    disc = disc_of(gain_ref[...])
    sides = []
    for source in range(SOURCES):
        field = field_ref[source]
        real, imag = field[:W], field[W:]
        scaled = jnp.concatenate([residual * real, residual * imag], axis=1)
        back = product(terms(scaled), pair_of(coarse_t_ref))
        sides.append(jnp.concatenate([back[:, :K], back[:, K:]], axis=0))
    real_ref[...] = jnp.zeros((2, W, K), F32)
    imag_ref[...] = jnp.zeros((2, W, K), F32)
    pad = jnp.zeros((K, K), F32)
    for couple in range(SOURCES // 2):
        spec = product(pair_of(coarse_ref), terms(jnp.concatenate(sides[2 * couple : 2 * couple + 2], axis=1)))
        for place in range(2):
            source = 2 * couple + place
            row, column = window_starts(index_ref, source)
            scale = disc * (2.0 * weights_ref[source])
            for ref, part in ((real_ref, spec[:K]), (imag_ref, spec[K:])):
                part = part[:, place * K : place * K + K] * scale
                wide = pltpu.roll(jnp.concatenate([part, pad], axis=1), column, 1)
                for side in range(2):
                    ref[side, pl.ds(row, K), :] += wide[:, side * K : side * K + K]
    fold, fold_t = fold_ref[...], fold_t_ref[...]

    def folded(ref):
        return exact_right(exact_left(fold, jnp.concatenate([ref[0], ref[1]], axis=1)), fold_t)

    even, odd = folded(real_ref), folded(imag_ref)
    top = jnp.concatenate([even[:K, :K], -odd[:K, K:]], axis=1)
    bottom = jnp.concatenate([-odd[K:, :K], -even[K:, K:]], axis=1)
    keep_ref[...] = jnp.where(core == 0, top, bottom)
    send_ref[...] = jnp.where(core == 0, bottom, top)


def lines_kernel(mine_ref, other_ref, block_ref, outer_ref, lines_ref, rim_ref):
    chip, core = my_place()
    spectrum = terms(joined(mine_ref[...], other_ref[...], core))
    lines_ref[...] = product((block_ref[chip, 0], block_ref[chip, 1]), spectrum)
    rim_ref[...] = product((outer_ref[chip // 2, 0], outer_ref[chip // 2, 1]), spectrum)


def pixels_kernel(lines_ref, rim_ref, mid_t_ref, sides_ref, inner_ref, side_ref):
    chip, core = my_place()
    rim = rim_ref[...]
    lines = lines_ref[...]
    top = lines[:A] + jnp.where(chip == 0, rim, 0.0)
    bottom = lines[A:] + jnp.where(chip == 3, rim, 0.0)
    table = (sides_ref[core, 0], sides_ref[core, 1])
    side_ref[...] = jnp.concatenate([product(terms(top), table), product(terms(bottom), table)], axis=1)
    own = jnp.where(core == 0, top, bottom)
    inner_ref[...] = product(terms(own), pair_of(mid_t_ref))


def join_kernel(inner_ref, mine_ref, other_ref, out_ref):
    _, core = my_place()
    first = core == 0
    mine, other = mine_ref[...], other_ref[...]
    left = jnp.where(first, other[:, :A], mine[:, A:])
    right = jnp.where(first, mine[:, :A], other[:, A:])
    inner = inner_ref[...]
    pad = jnp.zeros((A, A), F32)
    out_ref[0, :, :K] = inner[:, :K] + jnp.concatenate([left, pad], axis=1)
    out_ref[0, :, K : PIX - K] = inner[:, K : PIX - K]
    out_ref[0, :, PIX - K :] = inner[:, PIX - K :] + jnp.concatenate([pad, right], axis=1)


def swap_cores(value):
    return lax.ppermute(value, "src", [(at, at ^ 1) for at in range(8)])


def swap_chips(value, turn):
    def partner(at):
        chip, core = at // 2, at % 2
        return 2 * (chip ^ 1 if core == turn else 3 - chip) + core

    return lax.ppermute(value, "src", [(at, partner(at)) for at in range(8)])


def tile_move(value, shift_of):
    pairs = []
    for source in range(8):
        shift = shift_of(source)
        if shift is None:
            continue
        for row in range(TROWS):
            for column in range(TCOLS):
                to_row, to_column = row + shift[0], column + shift[1]
                if 0 <= to_row < TROWS and 0 <= to_column < TCOLS:
                    pairs.append(
                        (source * 32 + row * TCOLS + column, source * 32 + to_row * TCOLS + to_column)
                    )
    return lax.ppermute(value, BOTH, pairs)


def tile_move_all(value, step):
    def partner(at):
        y, x, z = at // TCOLS, at // 2 % 4, at % 2
        if step == 0:
            z = 1 - z
        elif step < 3:
            x = x ^ 1 if step == 1 else 3 - x
        else:
            y = y ^ 1 if step == 3 else 3 - y
        return y * TCOLS + x * 2 + z

    return lax.ppermute(value, "tile", [(at, partner(at)) for at in range(TROWS * TCOLS)])


def tile_pass(value, step):
    return value + tile_move_all(value, step)


def tied(*values):
    return lax.optimization_barrier(values)


def body(tables, mask_tiles, target, pupil_gain, weights, freq_index):
    core = lax.axis_index("src") % 2
    edge = jnp.where(core == 0, mask_tiles[0, PIX - A :], mask_tiles[0, :A])
    mine = tile_move(edge, lambda source: (1, 0) if source % 2 == 0 else (-1, 0))
    (rows,) = call(
        own_kernel,
        [(W, PIX)],
        [mask_tiles, tables["mid_t"]],
        "own",
        400_000_000,
        scratch=(
            pltpu.VMEM((PIX, PIX), F32),
            pltpu.VMEM((2, W, PIX), BF),
            pltpu.SemaphoreType.DMA((1 + PIX // K,)),
        ),
        hbm=(0, 1),
    )
    mine, rows = tied(mine, rows)
    other = swap_cores(mine)
    rows, side = call(
        rows_kernel, [(W, PIX), (K, K)], [rows, mine, other, tables["rims_t"]], "rows", 100_000_000
    )
    my_side = tile_move(side, lambda source: (0, 1) if source % 2 == 0 else (0, -1))
    (basis,) = call(columns_kernel, [(W, W)], [rows, tables["mid"]], "columns", 200_000_000)
    my_side, basis = tied(my_side, basis)
    other_side = swap_cores(my_side)
    plane = pltpu.VMEM((2, W, K), F32)
    field, keep, send = call(
        image_kernel,
        [(SOURCES, 2 * W, W), (K, W), (K, W)],
        [
            freq_index,
            weights,
            basis,
            my_side,
            other_side,
            pupil_gain,
            tables["rims"],
            tables["fold"],
            tables["fold_t"],
            tables["coarse"],
            tables["coarse_t"],
        ],
        "image",
        1_500_000_000,
        scratch=(plane, plane),
        smem=(0, 1),
    )
    value = keep + swap_cores(send)
    moved = swap_chips(value, 0)
    (wanted,) = call(
        wanted_kernel,
        [(W, W)],
        [target, tables["spread"], tables["spread_t"]],
        "wanted",
        600_000_000,
        scratch=(
            pltpu.VMEM((PIX, PIX), F32),
            pltpu.VMEM((2, PIX, W), BF),
            pltpu.VMEM((2, W, PIX), BF),
            pltpu.SemaphoreType.DMA((3,)),
        ),
        hbm=(0, 1, 2),
    )
    value, wanted = tied(value + moved, wanted)
    mine = value + swap_chips(value, 1)
    other = swap_cores(mine)
    residual, energies = call(
        residual_kernel, [(W, W), (8, K)], [mine, other, wanted, field, tables["gram"]], "residual", 300_000_000
    )
    arrived = tile_move_all(energies, 3)
    keep, send = call(
        adjoint_kernel,
        [(K, W), (K, W)],
        [
            freq_index,
            weights,
            residual,
            field,
            pupil_gain,
            tables["fold"],
            tables["fold_t"],
            tables["coarse"],
            tables["coarse_t"],
        ],
        "adjoint",
        1_500_000_000,
        scratch=(plane, plane),
        smem=(0, 1),
    )
    keep, send, energies = tied(keep, send, energies + arrived)
    value = keep + swap_cores(send)
    moved = swap_chips(value, 0)
    energies = tile_pass(energies, 1)
    value, energies = tied(value + moved, energies)
    moved = swap_chips(value, 1)
    energies = tile_pass(energies, 4)
    mine, energies = tied(value + moved, energies)
    other = swap_cores(mine)
    lines, rim = call(
        lines_kernel,
        [(K, W), (A, W)],
        [mine, other, tables["blocks"], tables["outer"]],
        "lines",
        100_000_000,
    )
    from_rows = tile_move(rim, lambda source: {0: (1, 0), 3: (-1, 0)}.get(source // 2))
    energies = tile_pass(energies, 0)
    from_rows, energies = tied(from_rows, energies)
    inner, side = call(
        pixels_kernel,
        [(A, PIX), (A, K)],
        [lines, from_rows, tables["mid_t"], tables["sides_t"]],
        "pixels",
        100_000_000,
    )
    my_side = tile_move(side, lambda source: (0, -1) if source % 2 == 0 else (0, 1))
    energies = tile_pass(energies, 2)
    my_side, energies = tied(my_side, energies)
    other_side = swap_cores(my_side)
    (mask_grad,) = call(join_kernel, [(1, A, PIX)], [inner, my_side, other_side], "join", A * PIX)
    weight_grad = energies[0, :SOURCES] * (16.0 / (TROWS * TCOLS * PIX * PIX))
    return mask_grad, weight_grad


def solution(mesh):
    placed = (P("tile", None, None), P("tile", None, None), P(), P("src"), P("src", None, None))
    return jax.shard_map(
        functools.partial(body, make_tables()),
        mesh=mesh,
        in_specs=placed,
        out_specs=(P("tile", "src", None), P("src")),
        check_vma=False,
    )
```

```python
import functools
import math

import jax
import jax.numpy as jnp
import ml_dtypes
import numpy as np
from jax import lax
from jax.experimental import pallas as pl
from jax.experimental.pallas import tpu as pltpu
from jax.sharding import PartitionSpec as P

A = 64
TROWS = 4
TCOLS = 8
PIX = 512
N = PIX + 2 * A
K = 128
W = 256
SOURCES = 4
CHIPS = 4
BF = jnp.bfloat16
F32 = jnp.float32
BOTH = ("src", "tile")


def two_terms(table):
    first = table.astype(np.float32).astype(ml_dtypes.bfloat16)
    rest = (table - first.astype(np.float64)).astype(np.float32)
    return np.stack([first, rest.astype(ml_dtypes.bfloat16)])


def real_basis():
    angles = 2.0 * np.pi / N * np.mod(np.outer(np.arange(N), np.arange(K)), N)
    return np.concatenate([np.cos(angles), np.sin(angles)], axis=1) / math.sqrt(N)


def fold_table():
    ranks = np.arange(W) - K
    parts = np.arange(K)
    same = np.abs(ranks)[None, :] == parts[:, None]
    return np.concatenate([same * 1.0, same * np.sign(ranks)[None, :]], axis=0)


def coarse_table():
    ranks = np.arange(K) - K // 2
    angles = 2.0 * np.pi / W * np.mod(np.outer(ranks, np.arange(W)), W)
    down_real, down_imag = np.cos(angles) / math.sqrt(K), np.sin(angles) / math.sqrt(K)
    return np.block([[down_real, down_imag], [-down_imag, down_real]])


def interpolation():
    ranks = np.arange(1, K)
    shift = (np.arange(PIX) + A)[:, None] / N - np.arange(W)[None, :] / W
    return (1.0 + 2.0 * np.cos(2.0 * np.pi * shift[..., None] * ranks).sum(-1)) / W


ROWS = 64


def packed(entries):
    spots, pieces, at = {}, [], 0
    for name, tables in entries.items():
        spots[name] = []
        for table in tables:
            count = table.shape[0] // ROWS
            spots[name].append((at, count))
            pieces.append(table.reshape(count, ROWS, W))
            at += count
    return np.concatenate(pieces), spots


def two_halves(table):
    return [half for term in two_terms(table) for half in (term[:, :W], term[:, W:])]


def make_tables():
    basis = real_basis()
    coarse = coarse_table()
    spread = interpolation()
    fold = fold_table().astype(ml_dtypes.bfloat16)
    middle = basis[A : N - A]
    rims = np.concatenate([basis[:A], basis[N - A :]])
    sides = [two_terms(basis[:A].T), two_terms(basis[N - A :].T)]
    early = packed(
        {
            "mid": two_terms(middle),
            "mid_t": two_halves(middle.T),
            "rims": two_terms(rims),
            "rims_t": [np.concatenate(list(two_terms(rims.T)), axis=1)],
            "sides": [np.concatenate([term for pair in sides for term in pair], axis=1)],
        }
    )
    late = packed(
        {
            "coarse": two_halves(coarse),
            "coarse_t": two_terms(coarse.T),
            "fold": [fold],
            "fold_t": [np.ascontiguousarray(fold.T)],
            "spread": two_terms(spread),
            "spread_t": two_halves(spread.T),
            "gram": two_terms(spread.T @ spread),
        }
    )
    return early, late


(EARLY, EARLY_AT), (LATE, LATE_AT) = make_tables()
SPOTS = EARLY_AT | LATE_AT


def stored(ref, name, at=0):
    start, count = SPOTS[name][at]
    return ref[start : start + count].reshape(count * ROWS, W)


def narrow(ref, name):
    return stored(ref, name, 0), stored(ref, name, 1)


def wide(ref, name):
    return tuple(
        jnp.concatenate([stored(ref, name, at), stored(ref, name, at + 1)], axis=1) for at in (0, 2)
    )


def terms(value):
    first = value.astype(BF)
    return first, (value - first.astype(F32)).astype(BF)


def dot(first_op, second_op):
    return jnp.dot(first_op, second_op, preferred_element_type=F32)


def product(first_op, second_op):
    first_hi, first_lo = first_op
    second_hi, second_lo = second_op
    return dot(
        jnp.concatenate([first_hi, first_hi, first_lo], axis=1),
        jnp.concatenate([second_hi, second_lo, second_hi], axis=0),
    )


def exact_left(table, value):
    high, low = terms(value)
    return dot(table, high) + dot(table, low)


def exact_right(value, table):
    high, low = terms(value)
    return dot(high, table) + dot(low, table)


def call(kernel, outs, ins, name, flops, scratch=(), smem=(), bf16=(), grant=20):
    specs = [
        pl.BlockSpec(memory_space=pltpu.SMEM if at in smem else pltpu.VMEM) for at in range(len(ins))
    ]
    shapes = [jax.ShapeDtypeStruct(shape, BF if at in bf16 else F32) for at, shape in enumerate(outs)]
    moved = 4 * sum(math.prod(shape) for shape in outs) + sum(one.size * one.dtype.itemsize for one in ins)
    return pl.pallas_call(
        kernel,
        out_shape=shapes,
        in_specs=specs,
        out_specs=[pl.BlockSpec(memory_space=pltpu.VMEM) for _ in outs],
        scratch_shapes=list(scratch),
        compiler_params=pltpu.CompilerParams(vmem_limit_bytes=40 * 1024 * 1024),
        cost_estimate=pl.CostEstimate(flops=flops, bytes_accessed=moved, transcendentals=0),
        name=name,
    )(*ins)


def my_place():
    group = lax.axis_index("src")
    return group // 2, group % 2


def own_kernel(tile_ref, early_ref, rows_ref, table_ref):
    rows_ref[...] = product(wide(early_ref, "mid_t"), terms(tile_ref[0]))
    table_ref[...] = stored(early_ref, "rims_t")


def wanted_kernel(target_ref, late_ref, wanted_ref):
    upper = product(terms(target_ref[0]), narrow(late_ref, "spread"))
    wanted_ref[...] = product(wide(late_ref, "spread_t"), terms(upper))


def rows_kernel(rows_ref, mine_ref, other_ref, table_ref, all_ref, side_ref):
    _, core = my_place()
    first = core == 0
    mine, other = mine_ref[...], other_ref[...]
    rim = jnp.concatenate([jnp.where(first, mine, other), jnp.where(first, other, mine)], axis=0)
    table = table_ref[...]
    rows = rows_ref[...] + product((table[:, :K], table[:, K:]), terms(rim))
    all_ref[...] = rows
    side = jnp.where(first, rows[:, PIX - A :], rows[:, :A])
    side_ref[...] = jnp.concatenate([side[:K], side[K:]], axis=1)


def columns_kernel(rows_ref, early_ref, _, basis_ref):
    basis_ref[...] = product(terms(rows_ref[...]), narrow(early_ref, "mid"))


def disc_of(gain):
    rows = lax.broadcasted_iota(jnp.int32, (K, K), 0) - K // 2
    columns = lax.broadcasted_iota(jnp.int32, (K, K), 1) - K // 2
    return jnp.where(rows * rows + columns * columns <= (K // 2) ** 2, gain, 0.0)


def window_starts(info_refs, source):
    ref = info_refs[min(source // SOURCES, 2)]
    at = source % SOURCES + (SOURCES if source // SOURCES == 3 else 0)

    def start(coordinate):
        index = ref[at, coordinate, 0].astype(jnp.int32)
        return jnp.clip(lax.rem(index + K, N), 0, K)

    return start(0), start(1)


def weight_of(info_refs, source):
    ref = info_refs[min(source // SOURCES, 2)]
    return ref[source % SOURCES + (SOURCES if source // SOURCES == 3 else 0), 0, 1]


def image_of(info_refs, chips, planes, disc, late_ref, field_ref):
    coarse, coarse_t = wide(late_ref, "coarse"), narrow(late_ref, "coarse_t")
    total = jnp.zeros((W, W), F32)
    for chip in chips:
        specs = []
        for source in range(chip * SOURCES, chip * SOURCES + SOURCES):
            row, column = window_starts(info_refs, source)

            def window(ref):
                rows = jnp.concatenate([ref[0, pl.ds(row, K), :], ref[1, pl.ds(row, K), :]], axis=1)
                return pltpu.roll(rows, lax.rem(W - column, W), 1)[:, :K] * disc

            specs.append(jnp.concatenate([window(ref) for ref in planes], axis=1))
        stacked = product(terms(jnp.concatenate(specs, axis=0)), coarse)
        for at in range(SOURCES):
            half = stacked[at * K : at * K + K]
            half = jnp.concatenate([half[:, :W], half[:, W:]], axis=0)
            field = product(coarse_t, terms(half))
            field_ref[(chip - chips[0]) * SOURCES + at] = field
            real, imag = field[:W], field[W:]
            weight = weight_of(info_refs, chip * SOURCES + at)
            total = total + weight * (real * real + imag * imag)
    return total


def image_kernel(
    info_ref,
    basis_ref,
    mine_ref,
    other_ref,
    gain_ref,
    early_ref,
    late_ref,
    field_ref,
    total_ref,
    real_ref,
    imag_ref,
):
    _, core = my_place()
    first = core == 0
    mine, other = mine_ref[...], other_ref[...]
    left = jnp.where(first, mine, other)
    right = jnp.where(first, other, mine)
    rim = jnp.concatenate(
        [
            jnp.concatenate([left[:, :A], right[:, :A]], axis=1),
            jnp.concatenate([left[:, A:], right[:, A:]], axis=1),
        ],
        axis=0,
    )
    basis = basis_ref[...] + product(terms(rim), narrow(early_ref, "rims"))
    zero = jnp.zeros((K, K), F32)
    even = jnp.concatenate(
        [
            jnp.concatenate([basis[:K, :K], zero], axis=1),
            jnp.concatenate([zero, -basis[K:, K:]], axis=1),
        ],
        axis=0,
    )
    odd = jnp.concatenate(
        [
            jnp.concatenate([zero, -basis[:K, K:]], axis=1),
            jnp.concatenate([-basis[K:, :K], zero], axis=1),
        ],
        axis=0,
    )
    fold, fold_t = stored(late_ref, "fold"), stored(late_ref, "fold_t")
    for ref, part in ((real_ref, even), (imag_ref, odd)):
        plane = exact_right(exact_left(fold_t, part), fold)
        ref[0] = plane[:, :K]
        ref[1] = plane[:, K:]
    disc = disc_of(gain_ref[...])
    total_ref[...] = image_of((info_ref,), (0,), (real_ref, imag_ref), disc, late_ref, field_ref)


def others_kernel(
    near_ref, far_ref, gain_ref, late_ref, real_ref, imag_ref, before_ref, field_ref, total_ref
):
    info_refs = (None, near_ref, far_ref)
    disc = disc_of(gain_ref[...])
    total_ref[...] = before_ref[...] + image_of(
        info_refs, (1, 2, 3), (real_ref, imag_ref), disc, late_ref, field_ref
    )


def residual_kernel(mine_ref, other_ref, wanted_ref, field_ref, late_ref, residual_ref, energy_ref):
    bright = mine_ref[...] + other_ref[...]
    gram = narrow(late_ref, "gram")
    value = product(terms(product(gram, terms(bright))), gram)
    residual = value * (1.0 / (8 * SOURCES)) - wanted_ref[...]
    residual_ref[...] = residual
    lanes = lax.broadcasted_iota(jnp.int32, (8, K), 1)
    energies = jnp.zeros((8, K), F32)
    for source in range(SOURCES):
        real, imag = field_ref[source, :W], field_ref[source, W:]
        energy = jnp.sum(residual * (real * real + imag * imag))
        energies = jnp.where(lanes == source, energy, energies)
    energy_ref[...] = energies


def adjoint_kernel(
    chip,
    info_ref,
    residual_ref,
    field_ref,
    gain_ref,
    late_ref,
    real_in,
    imag_in,
    *outs,
):
    info_refs = (info_ref,) * 3
    first_field = SOURCES if chip else 0
    coarse, coarse_t = wide(late_ref, "coarse"), narrow(late_ref, "coarse_t")
    _, core = my_place()
    last = chip == CHIPS - 1
    real_ref, imag_ref = outs[2:] if last else outs
    residual = residual_ref[...]
    disc = disc_of(gain_ref[...])
    real_ref[...] = jnp.zeros((2, W, K), F32) if chip == 0 else real_in[...]
    imag_ref[...] = jnp.zeros((2, W, K), F32) if chip == 0 else imag_in[...]
    pad = jnp.zeros((K, K), F32)
    for couple in range(chip * SOURCES, chip * SOURCES + SOURCES, 2):
        sides = []
        for source in (couple, couple + 1):
            field = field_ref.at[source - first_field]
            real, imag = field[:W], field[W:]
            scaled = jnp.concatenate([residual * real, residual * imag], axis=1)
            back = product(terms(scaled), coarse_t)
            sides.append(jnp.concatenate([back[:, :K], back[:, K:]], axis=0))
        spec = product(coarse, terms(jnp.concatenate(sides, axis=1)))
        for place in range(2):
            source = couple + place
            row, column = window_starts(info_refs, source)
            scale = disc * (2.0 * weight_of(info_refs, source))
            for ref, part in ((real_ref, spec[:K]), (imag_ref, spec[K:])):
                part = part[:, place * K : place * K + K] * scale
                spread = pltpu.roll(jnp.concatenate([part, pad], axis=1), column, 1)
                for side in range(2):
                    ref[side, pl.ds(row, K), :] += spread[:, side * K : side * K + K]
    if not last:
        return
    keep_ref, send_ref = outs[:2]
    fold, fold_t = stored(late_ref, "fold"), stored(late_ref, "fold_t")

    def folded(ref):
        return exact_right(exact_left(fold, jnp.concatenate([ref[0], ref[1]], axis=1)), fold_t)

    even, odd = folded(real_ref), folded(imag_ref)
    left = jnp.concatenate([even[:K, :K], -odd[K:, :K]], axis=0)
    right = jnp.concatenate([-odd[:K, K:], -even[K:, K:]], axis=0)
    keep_ref[...] = jnp.where(core == 0, left, right)
    send_ref[...] = jnp.where(core == 0, right, left)


def lines_kernel(mine_ref, early_ref, lines_ref, rim_ref):
    chip, _ = my_place()
    spectrum = terms(mine_ref[...])
    lines = [early_ref[pl.ds(SPOTS["mid"][at][0] + 2 * chip, 2)].reshape(K, W) for at in range(2)]
    lines_ref[...] = product(lines, spectrum)
    outer = [early_ref[SPOTS["rims"][at][0] + 1 - chip // 2] for at in range(2)]
    rim_ref[...] = product(outer, spectrum)


def rim_kernel(lines_ref, rim_ref, energy_ref, out_ref):
    chip, _ = my_place()
    rim = rim_ref[...]
    out_ref[:A] = lines_ref[:A] + jnp.where(chip == 0, rim, 0.0)
    out_ref[A:K] = lines_ref[A:] + jnp.where(chip == 3, rim, 0.0)
    out_ref[K:] = energy_ref[...]


def pixels_kernel(mine_ref, other_ref, early_ref, inner_ref, side_ref):
    _, core = my_place()
    first = core == 0
    mine, other = mine_ref[...], other_ref[...]
    lines = jnp.concatenate([jnp.where(first, mine, other), jnp.where(first, other, mine)], axis=1)
    top, bottom = lines[:A], lines[A:K]
    table = stored(early_ref, "sides")
    table = jnp.where(first, table[:, :K], table[:, K:])
    table = (table[:, :A], table[:, A:])
    side_ref[:A] = jnp.concatenate([product(terms(top), table), product(terms(bottom), table)], axis=1)
    lanes = lax.broadcasted_iota(jnp.int32, (8, K), 1)
    side_ref[A:] = jnp.where(lanes < A, lines[K:, :K], pltpu.roll(lines[K:, K:], A, 1))
    own = jnp.where(first, top, bottom)
    inner_ref[...] = product(terms(own), wide(early_ref, "mid_t"))


def join_kernel(inner_ref, before_ref, mine_ref, other_ref, out_ref, energy_ref):
    _, core = my_place()
    first = core == 0
    mine, other = mine_ref[...], other_ref[...]
    left = jnp.where(first, other[:A, :A], mine[:A, A:])
    right = jnp.where(first, mine[:A, :A], other[:A, A:])
    inner = inner_ref[...]
    pad = jnp.zeros((A, A), F32)
    out_ref[0, :, :K] = inner[:, :K] + jnp.concatenate([left, pad], axis=1)
    out_ref[0, :, K : PIX - K] = inner[:, K : PIX - K]
    out_ref[0, :, PIX - K :] = inner[:, PIX - K :] + jnp.concatenate([pad, right], axis=1)
    odd = lax.rem(lax.axis_index("tile"), 2)
    total = before_ref[A : A + 1] + jnp.where(core == odd, mine[A : A + 1], other[A : A + 1])
    total = pltpu.roll(total, core * A, 1) * (16.0 / (TROWS * TCOLS * PIX * PIX))
    energy_ref[...] = total[0, :SOURCES]


def swap_cores(value):
    return lax.ppermute(value, "src", [(at, at ^ 1) for at in range(8)])


def next_chip(value, steps):
    return lax.ppermute(
        value, "src", [(at, (at // 2 + steps) % CHIPS * 2 + at % 2) for at in range(2 * CHIPS)]
    )


def tile_move(value, shift_of):
    pairs = []
    for source in range(8):
        shift = shift_of(source)
        if shift is None:
            continue
        for row in range(TROWS):
            for column in range(TCOLS):
                to_row, to_column = row + shift[0], column + shift[1]
                if 0 <= to_row < TROWS and 0 <= to_column < TCOLS:
                    pairs.append(
                        (source * 32 + row * TCOLS + column, source * 32 + to_row * TCOLS + to_column)
                    )
    return lax.ppermute(value, BOTH, pairs)


def tile_swap(value, step):
    def partner(at):
        y, x, z = at // TCOLS, at // 2 % 4, at % 2
        if step == 0:
            z = 1 - z
        elif step < 3:
            x = x ^ 1 if step == 1 else 3 - x
        else:
            y = y ^ 1 if step == 3 else 3 - y
        return y * TCOLS + x * 2 + z

    return lax.ppermute(value, "tile", [(at, partner(at)) for at in range(TROWS * TCOLS)])


def tied(*values):
    return lax.optimization_barrier(values)


def body(mask_tiles, target, pupil_gain, weights, freq_index):
    core = lax.axis_index("src") % 2
    edge = jnp.where(core == 0, mask_tiles[0, PIX - A :], mask_tiles[0, :A])
    mine = tile_move(edge, lambda source: (1, 0) if source % 2 == 0 else (-1, 0))
    rows, rim_table = call(own_kernel, [(W, PIX), (W, W)], [mask_tiles, EARLY], "own", 400_000_000, bf16=(1,))
    mine, rows, weights, freq_index = tied(mine, rows, weights, freq_index)
    other = swap_cores(mine)
    lanes = lax.broadcasted_iota(jnp.int32, freq_index.shape, 2)
    info = jnp.where(lanes == 1, weights[:, None, None], freq_index.astype(F32))
    near = next_chip(info, 1)
    rows, side = call(
        rows_kernel, [(W, PIX), (K, K)], [rows, mine, other, rim_table], "rows", 100_000_000
    )
    my_side = tile_move(side, lambda source: (0, 1) if source % 2 == 0 else (0, -1))
    (basis,) = call(columns_kernel, [(W, W)], [rows, EARLY, LATE], "columns", 200_000_000)
    far = next_chip(jnp.concatenate([info, near]), 2)
    my_side, basis = tied(my_side, basis)
    other_side = swap_cores(my_side)
    own_field, total, real, imag = call(
        image_kernel,
        [(SOURCES, 2 * W, W), (W, W), (2, W, K), (2, W, K)],
        [info, basis, my_side, other_side, pupil_gain, EARLY, LATE],
        "image",
        2_000_000_000,
        smem=(0,),
    )
    field, mine = call(
        others_kernel,
        [((CHIPS - 1) * SOURCES, 2 * W, W), (W, W)],
        [near, far, pupil_gain, LATE, real, imag, total],
        "others",
        5_000_000_000,
        smem=(0, 1),
    )
    other = swap_cores(mine)
    (wanted,) = call(wanted_kernel, [(W, W)], [target, LATE], "wanted", 600_000_000)
    other, wanted = tied(other, wanted)
    residual, energies = call(
        residual_kernel, [(W, W), (8, K)], [mine, other, wanted, own_field, LATE], "residual", 300_000_000
    )
    plane = pltpu.VMEM((2, W, K), F32)
    planes = (jnp.zeros((8, K), F32),) * 2
    for chip in range(CHIPS):
        arrived = tile_swap(energies, (3, 1, 4, 2)[chip])
        last = chip == CHIPS - 1
        outs = call(
            functools.partial(adjoint_kernel, chip),
            [(W, K), (W, K)] if last else [(2, W, K), (2, W, K)],
            [(info, near, far, far)[chip], residual, field if chip else own_field, pupil_gain, LATE, *planes],
            "adjoint",
            1_500_000_000,
            scratch=(plane, plane) if last else (),
            smem=(0,),
        )
        planes = outs[:2]
        *planes, energies = tied(*planes, energies + arrived)
    keep, send = planes
    mine = keep + swap_cores(send)
    lines, rim = call(
        lines_kernel,
        [(K, K), (A, K)],
        [mine, EARLY],
        "lines",
        100_000_000,
    )
    from_rows = tile_move(rim, lambda source: {0: (1, 0), 3: (-1, 0)}.get(source // 2))
    (mine,) = call(rim_kernel, [(K + 8, K)], [lines, from_rows, energies], "rim", K * K)
    other = swap_cores(mine)
    inner, side = call(
        pixels_kernel,
        [(A, PIX), (A + 8, K)],
        [mine, other, EARLY],
        "pixels",
        100_000_000,
    )
    my_side = tile_move(side, lambda source: (0, -1) if source % 2 == 0 else (0, 1))
    other_side = swap_cores(my_side)
    mask_grad, weight_grad = call(
        join_kernel, [(1, A, PIX), (SOURCES,)], [inner, side, my_side, other_side], "join", A * PIX
    )
    return mask_grad, weight_grad


def solution(mesh):
    placed = (P("tile", None, None), P("tile", None, None), P(), P("src"), P("src", None, None))
    return jax.shard_map(
        body,
        mesh=mesh,
        in_specs=placed,
        out_specs=(P("tile", "src", None), P("src")),
        check_vma=False,
    )
```

```python
import functools
import math

import jax
import jax.numpy as jnp
import ml_dtypes
import numpy as np
from jax import lax
from jax.experimental import pallas as pl
from jax.experimental.pallas import tpu as pltpu
from jax.sharding import PartitionSpec as P

A = 64
TROWS = 4
TCOLS = 8
PIX = 512
N = PIX + 2 * A
K = 128
W = 256
SOURCES = 4
CHIPS = 4
BF = jnp.bfloat16
F32 = jnp.float32
BOTH = ("src", "tile")


def two_terms(table):
    first = table.astype(np.float32).astype(ml_dtypes.bfloat16)
    rest = (table - first.astype(np.float64)).astype(np.float32)
    return np.stack([first, rest.astype(ml_dtypes.bfloat16)])


def real_basis():
    angles = 2.0 * np.pi / N * np.mod(np.outer(np.arange(N), np.arange(K)), N)
    return np.concatenate([np.cos(angles), np.sin(angles)], axis=1) / math.sqrt(N)


def fold_table():
    ranks = np.arange(W) - K
    parts = np.arange(K)
    same = np.abs(ranks)[None, :] == parts[:, None]
    return np.concatenate([same * 1.0, same * np.sign(ranks)[None, :]], axis=0)


def coarse_table():
    ranks = np.arange(K) - K // 2
    angles = 2.0 * np.pi / W * np.mod(np.outer(ranks, np.arange(W)), W)
    down_real, down_imag = np.cos(angles) / math.sqrt(K), np.sin(angles) / math.sqrt(K)
    return np.block([[down_real, down_imag], [-down_imag, down_real]])


def interpolation():
    ranks = np.arange(1, K)
    shift = (np.arange(PIX) + A)[:, None] / N - np.arange(W)[None, :] / W
    return (1.0 + 2.0 * np.cos(2.0 * np.pi * shift[..., None] * ranks).sum(-1)) / W


ROWS = 64


def packed(entries):
    spots, pieces, at = {}, [], 0
    for name, tables in entries.items():
        spots[name] = []
        for table in tables:
            count = table.shape[0] // ROWS
            spots[name].append((at, count))
            pieces.append(table.reshape(count, ROWS, W))
            at += count
    return np.concatenate(pieces), spots


def two_halves(table):
    return [half for term in two_terms(table) for half in (term[:, :W], term[:, W:])]


def make_tables():
    basis = real_basis()
    coarse = coarse_table()
    spread = interpolation()
    fold = fold_table().astype(ml_dtypes.bfloat16)
    middle = basis[A : N - A]
    rims = np.concatenate([basis[:A], basis[N - A :]])
    sides = [two_terms(basis[:A].T), two_terms(basis[N - A :].T)]
    return packed(
        {
            "mid": two_terms(middle),
            "mid_t": two_halves(middle.T),
            "rims": two_terms(rims),
            "rims_t": [np.concatenate(list(two_terms(rims.T)), axis=1)],
            "sides": [np.concatenate([term for pair in sides for term in pair], axis=1)],
            "coarse": two_halves(coarse),
            "coarse_t": two_terms(coarse.T),
            "fold": [fold],
            "fold_t": [np.ascontiguousarray(fold.T)],
            "spread": two_terms(spread),
            "spread_t": two_halves(spread.T),
            "gram": two_terms(spread.T @ spread),
        }
    )


TABLES, SPOTS = make_tables()


def stored(ref, name, at=0):
    start, count = SPOTS[name][at]
    return ref[start : start + count].reshape(count * ROWS, W)


def narrow(ref, name):
    return stored(ref, name, 0), stored(ref, name, 1)


def wide(ref, name):
    return tuple(
        jnp.concatenate([stored(ref, name, at), stored(ref, name, at + 1)], axis=1) for at in (0, 2)
    )


def terms(value):
    first = value.astype(BF)
    return first, (value - first.astype(F32)).astype(BF)


def dot(first_op, second_op):
    return jnp.dot(first_op, second_op, preferred_element_type=F32)


def product(first_op, second_op):
    first_hi, first_lo = first_op
    second_hi, second_lo = second_op
    return dot(
        jnp.concatenate([first_hi, first_hi, first_lo], axis=1),
        jnp.concatenate([second_hi, second_lo, second_hi], axis=0),
    )


def exact_left(table, value):
    high, low = terms(value)
    return dot(table, high) + dot(table, low)


def exact_right(value, table):
    high, low = terms(value)
    return dot(high, table) + dot(low, table)


def call(kernel, outs, ins, name, flops, scratch=(), smem=(), bf16=(), grant=20):
    specs = [
        pl.BlockSpec(memory_space=pltpu.SMEM if at in smem else pltpu.VMEM) for at in range(len(ins))
    ]
    shapes = [jax.ShapeDtypeStruct(shape, BF if at in bf16 else F32) for at, shape in enumerate(outs)]
    moved = 4 * sum(math.prod(shape) for shape in outs) + sum(one.size * one.dtype.itemsize for one in ins)
    return pl.pallas_call(
        kernel,
        out_shape=shapes,
        in_specs=specs,
        out_specs=[pl.BlockSpec(memory_space=pltpu.VMEM) for _ in outs],
        scratch_shapes=list(scratch),
        compiler_params=pltpu.CompilerParams(vmem_limit_bytes=40 * 1024 * 1024),
        cost_estimate=pl.CostEstimate(flops=flops, bytes_accessed=moved, transcendentals=0),
        name=name,
    )(*ins)


def my_place():
    group = lax.axis_index("src")
    return group // 2, group % 2


def own_kernel(tile_ref, table_ref, rows_ref, rims_ref):
    rows_ref[...] = product(wide(table_ref, "mid_t"), terms(tile_ref[0]))
    rims_ref[...] = stored(table_ref, "rims_t")


def wanted_kernel(target_ref, table_ref, wanted_ref):
    upper = product(terms(target_ref[0]), narrow(table_ref, "spread"))
    wanted_ref[...] = product(wide(table_ref, "spread_t"), terms(upper)).T


def rows_kernel(rows_ref, mine_ref, other_ref, table_ref, all_ref, side_ref):
    _, core = my_place()
    first = core == 0
    mine, other = mine_ref[...], other_ref[...]
    rim = jnp.concatenate([jnp.where(first, mine, other), jnp.where(first, other, mine)], axis=0)
    table = table_ref[...]
    rows = rows_ref[...] + product((table[:, :K], table[:, K:]), terms(rim))
    all_ref[...] = rows
    side = jnp.where(first, rows[:, PIX - A :], rows[:, :A])
    side_ref[...] = jnp.concatenate([side[:K], side[K:]], axis=1)


def columns_kernel(rows_ref, table_ref, basis_ref):
    basis_ref[...] = product(terms(rows_ref[...]), narrow(table_ref, "mid"))


def disc_of(gain):
    rows = lax.broadcasted_iota(jnp.int32, (K, K), 0) - K // 2
    columns = lax.broadcasted_iota(jnp.int32, (K, K), 1) - K // 2
    return jnp.where(rows * rows + columns * columns <= (K // 2) ** 2, gain, 0.0)


def window_starts(info_refs, source):
    ref = info_refs[min(source // SOURCES, 2)]
    at = source % SOURCES + (SOURCES if source // SOURCES == 3 else 0)

    def start(coordinate):
        index = ref[at, coordinate, 0].astype(jnp.int32)
        return jnp.clip(lax.rem(index + K, N), 0, K)

    return start(0), start(1)


def weight_of(info_refs, source):
    ref = info_refs[min(source // SOURCES, 2)]
    return ref[source % SOURCES + (SOURCES if source // SOURCES == 3 else 0), 0, 1]


def image_of(info_refs, chips, planes, disc, table_ref, field_ref):
    coarse = wide(table_ref, "coarse")
    total = jnp.zeros((W, W), F32)
    for chip in chips:
        specs = []
        for source in range(chip * SOURCES, chip * SOURCES + SOURCES):
            row, column = window_starts(info_refs, source)

            def window(ref):
                rows = jnp.concatenate([ref[0, pl.ds(row, K), :], ref[1, pl.ds(row, K), :]], axis=1)
                return pltpu.roll(rows, lax.rem(W - column, W), 1)[:, :K] * disc

            specs.append(jnp.concatenate([window(ref) for ref in planes], axis=1))
        stacked = product(terms(jnp.concatenate(specs, axis=0)), coarse)
        for at in range(SOURCES):
            half = stacked[at * K : at * K + K].T
            half = jnp.concatenate([half[:W], half[W:]], axis=1)
            field = product(terms(half), coarse)
            field_ref[(chip - chips[0]) * SOURCES + at] = field
            real, imag = field[:, :W], field[:, W:]
            weight = weight_of(info_refs, chip * SOURCES + at)
            total = total + weight * (real * real + imag * imag)
    return total


def image_kernel(
    info_ref,
    basis_ref,
    mine_ref,
    other_ref,
    gain_ref,
    table_ref,
    field_ref,
    total_ref,
    real_ref,
    imag_ref,
):
    _, core = my_place()
    first = core == 0
    mine, other = mine_ref[...], other_ref[...]
    left = jnp.where(first, mine, other)
    right = jnp.where(first, other, mine)
    rim = jnp.concatenate(
        [
            jnp.concatenate([left[:, :A], right[:, :A]], axis=1),
            jnp.concatenate([left[:, A:], right[:, A:]], axis=1),
        ],
        axis=0,
    )
    basis = basis_ref[...] + product(terms(rim), narrow(table_ref, "rims"))
    zero = jnp.zeros((K, K), F32)
    even = jnp.concatenate(
        [
            jnp.concatenate([basis[:K, :K], zero], axis=1),
            jnp.concatenate([zero, -basis[K:, K:]], axis=1),
        ],
        axis=0,
    )
    odd = jnp.concatenate(
        [
            jnp.concatenate([zero, -basis[:K, K:]], axis=1),
            jnp.concatenate([-basis[K:, :K], zero], axis=1),
        ],
        axis=0,
    )
    fold, fold_t = stored(table_ref, "fold"), stored(table_ref, "fold_t")
    for ref, part in ((real_ref, even), (imag_ref, odd)):
        plane = exact_right(exact_left(fold_t, part), fold)
        ref[0] = plane[:, :K]
        ref[1] = plane[:, K:]
    disc = disc_of(gain_ref[...])
    total_ref[...] = image_of((info_ref,), (0,), (real_ref, imag_ref), disc, table_ref, field_ref)


def others_kernel(
    near_ref, far_ref, gain_ref, table_ref, real_ref, imag_ref, before_ref, field_ref, total_ref
):
    info_refs = (None, near_ref, far_ref)
    disc = disc_of(gain_ref[...])
    total_ref[...] = before_ref[...] + image_of(
        info_refs, (1, 2, 3), (real_ref, imag_ref), disc, table_ref, field_ref
    )


def residual_kernel(mine_ref, other_ref, wanted_ref, field_ref, table_ref, residual_ref, energy_ref):
    bright = mine_ref[...] + other_ref[...]
    gram = narrow(table_ref, "gram")
    value = product(terms(product(gram, terms(bright))), gram)
    residual = value * (1.0 / (8 * SOURCES)) - wanted_ref[...]
    residual_ref[...] = residual
    lanes = lax.broadcasted_iota(jnp.int32, (8, K), 1)
    energies = jnp.zeros((8, K), F32)
    for source in range(SOURCES):
        real, imag = field_ref[source, :, :W], field_ref[source, :, W:]
        energy = jnp.sum(residual * (real * real + imag * imag))
        energies = jnp.where(lanes == source, energy, energies)
    energy_ref[...] = energies


def adjoint_kernel(
    chip,
    info_ref,
    residual_ref,
    field_ref,
    gain_ref,
    table_ref,
    real_in,
    imag_in,
    *outs,
):
    info_refs = (info_ref,) * 3
    first_field = SOURCES if chip else 0
    coarse_t = narrow(table_ref, "coarse_t")
    last = chip == CHIPS - 1
    real_ref, imag_ref = outs[1:] if last else outs
    residual = residual_ref[...]
    disc = disc_of(gain_ref[...])
    real_ref[...] = jnp.zeros((2, W, K), F32) if chip == 0 else real_in[...]
    imag_ref[...] = jnp.zeros((2, W, K), F32) if chip == 0 else imag_in[...]
    pad = jnp.zeros((K, K), F32)
    first = chip * SOURCES
    halves = []
    for source in range(first, first + SOURCES):
        field = field_ref.at[source - first_field]
        scaled = jnp.concatenate([residual * field[:, :W], residual * field[:, W:]], axis=1)
        half = product(terms(scaled), coarse_t).T
        halves.append(jnp.concatenate([half[:K], half[K:]], axis=1))
    spec = product(terms(jnp.concatenate(halves, axis=0)), coarse_t)
    for source in range(first, first + SOURCES):
        row, column = window_starts(info_refs, source)
        scale = disc * (2.0 * weight_of(info_refs, source))
        own = spec[(source - first) * K : (source - first) * K + K]
        for ref, part in ((real_ref, own[:, :K]), (imag_ref, own[:, K:])):
            spread = pltpu.roll(jnp.concatenate([part * scale, pad], axis=1), column, 1)
            for side in range(2):
                ref[side, pl.ds(row, K), :] += spread[:, side * K : side * K + K]
    if not last:
        return
    fold, fold_t = stored(table_ref, "fold"), stored(table_ref, "fold_t")

    def folded(ref):
        return exact_right(exact_left(fold, jnp.concatenate([ref[0], ref[1]], axis=1)), fold_t)

    even, odd = folded(real_ref), folded(imag_ref)
    outs[0][:K] = jnp.concatenate([even[:K, :K], -odd[:K, K:]], axis=1)
    outs[0][K:] = jnp.concatenate([-odd[K:, :K], -even[K:, K:]], axis=1)


def lines_kernel(mine_ref, table_ref, lines_ref, rim_ref):
    chip, _ = my_place()
    spectrum = terms(mine_ref[...])
    lines = [table_ref[pl.ds(SPOTS["mid"][at][0] + 2 * chip, 2)].reshape(K, W) for at in range(2)]
    lines_ref[...] = product(lines, spectrum)
    outer = [table_ref[SPOTS["rims"][at][0] + 1 - chip // 2] for at in range(2)]
    rim_ref[...] = product(outer, spectrum)


def rim_kernel(lines_ref, rim_ref, energy_ref, out_ref):
    chip, core = my_place()
    rim = rim_ref[...]
    out_ref[:A] = lines_ref[:A] + jnp.where(chip == 0, rim, 0.0)
    out_ref[A:K] = lines_ref[A:] + jnp.where(chip == 3, rim, 0.0)
    energy = energy_ref[...]
    out_ref[K:] = jnp.concatenate([jnp.where(core == at, energy, 0.0) for at in range(2)], axis=1)


def pixels_kernel(mine_ref, other_ref, table_ref, inner_ref, side_ref):
    _, core = my_place()
    first = core == 0
    lines = mine_ref[...] + other_ref[...]
    top, bottom = lines[:A], lines[A:K]
    table = stored(table_ref, "sides")
    table = jnp.where(first, table[:, :K], table[:, K:])
    table = (table[:, :A], table[:, A:])
    side_ref[:A] = jnp.concatenate([product(terms(top), table), product(terms(bottom), table)], axis=1)
    lanes = lax.broadcasted_iota(jnp.int32, (8, K), 1)
    side_ref[A:] = jnp.where(lanes < A, lines[K:, :K], pltpu.roll(lines[K:, K:], A, 1))
    own = jnp.where(first, top, bottom)
    inner_ref[...] = product(terms(own), wide(table_ref, "mid_t"))


def join_kernel(inner_ref, before_ref, mine_ref, other_ref, out_ref, energy_ref):
    _, core = my_place()
    first = core == 0
    mine, other = mine_ref[...], other_ref[...]
    left = jnp.where(first, other[:A, :A], mine[:A, A:])
    right = jnp.where(first, mine[:A, :A], other[:A, A:])
    inner = inner_ref[...]
    pad = jnp.zeros((A, A), F32)
    out_ref[0, :, :K] = inner[:, :K] + jnp.concatenate([left, pad], axis=1)
    out_ref[0, :, K : PIX - K] = inner[:, K : PIX - K]
    out_ref[0, :, PIX - K :] = inner[:, PIX - K :] + jnp.concatenate([pad, right], axis=1)
    odd = lax.rem(lax.axis_index("tile"), 2)
    total = before_ref[A : A + 1] + jnp.where(core == odd, mine[A : A + 1], other[A : A + 1])
    total = pltpu.roll(total, core * A, 1) * (16.0 / (TROWS * TCOLS * PIX * PIX))
    energy_ref[...] = total[0, :SOURCES]


def swap_cores(value):
    return lax.ppermute(value, "src", [(at, at ^ 1) for at in range(8)])


def chip_swap(value, low):
    pairs = []
    for source in range(2 * CHIPS):
        for tile in range(TROWS * TCOLS):
            step = 1 if tile % 2 == low else -1
            partner = (source // 2 + step) % CHIPS * 2 + source % 2
            pairs.append((source * 32 + tile, partner * 32 + (tile ^ 1)))
    return lax.ppermute(value, BOTH, pairs)


def tile_move(value, shift_of):
    pairs = []
    for source in range(8):
        shift = shift_of(source)
        if shift is None:
            continue
        for row in range(TROWS):
            for column in range(TCOLS):
                to_row, to_column = row + shift[0], column + shift[1]
                if 0 <= to_row < TROWS and 0 <= to_column < TCOLS:
                    pairs.append(
                        (source * 32 + row * TCOLS + column, source * 32 + to_row * TCOLS + to_column)
                    )
    return lax.ppermute(value, BOTH, pairs)


def tile_swap(value, step):
    def partner(at):
        y, x, z = at // TCOLS, at // 2 % 4, at % 2
        if step == 0:
            z = 1 - z
        elif step < 3:
            x = x ^ 1 if step == 1 else 3 - x
        else:
            y = y ^ 1 if step == 3 else 3 - y
        return y * TCOLS + x * 2 + z

    return lax.ppermute(value, "tile", [(at, partner(at)) for at in range(TROWS * TCOLS)])


def tied(*values):
    return lax.optimization_barrier(values)


def body(mask_tiles, target, pupil_gain, weights, freq_index):
    core = lax.axis_index("src") % 2
    edge = jnp.where(core == 0, mask_tiles[0, PIX - A :], mask_tiles[0, :A])
    mine = tile_move(edge, lambda source: (1, 0) if source % 2 == 0 else (-1, 0))
    rows, rim_table = call(own_kernel, [(W, PIX), (W, W)], [mask_tiles, TABLES], "own", 400_000_000, bf16=(1,))
    rows, weights, freq_index = tied(rows, weights, freq_index)
    mine, rows = tied(mine, rows)
    other = swap_cores(mine)
    lanes = lax.broadcasted_iota(jnp.int32, freq_index.shape, 2)
    info = jnp.where(lanes == 1, weights[:, None, None], freq_index.astype(F32))
    near = chip_swap(info, 1)
    rows, side = call(
        rows_kernel, [(W, PIX), (K, K)], [rows, mine, other, rim_table], "rows", 100_000_000
    )
    my_side = tile_move(side, lambda source: (0, 1) if source % 2 == 0 else (0, -1))
    (basis,) = call(columns_kernel, [(W, W)], [rows, TABLES], "columns", 200_000_000)
    far = chip_swap(jnp.concatenate([info, near]), 0)
    my_side, basis = tied(my_side, basis)
    other_side = swap_cores(my_side)
    own_field, total, real, imag = call(
        image_kernel,
        [(SOURCES, W, 2 * W), (W, W), (2, W, K), (2, W, K)],
        [info, basis, my_side, other_side, pupil_gain, TABLES],
        "image",
        2_000_000_000,
        smem=(0,),
    )
    field, mine = call(
        others_kernel,
        [((CHIPS - 1) * SOURCES, W, 2 * W), (W, W)],
        [near, far, pupil_gain, TABLES, real, imag, total],
        "others",
        5_000_000_000,
        smem=(0, 1),
    )
    other = swap_cores(mine)
    (wanted,) = call(wanted_kernel, [(W, W)], [target, TABLES], "wanted", 600_000_000)
    other, wanted = tied(other, wanted)
    residual, energies = call(
        residual_kernel, [(W, W), (8, K)], [mine, other, wanted, own_field, TABLES], "residual", 300_000_000
    )
    plane = pltpu.VMEM((2, W, K), F32)
    planes = (jnp.zeros((8, K), F32),) * 2
    for chip in range(CHIPS):
        arrived = tile_swap(energies, (3, 1, 4, 2)[chip])
        last = chip == CHIPS - 1
        outs = call(
            functools.partial(adjoint_kernel, chip),
            [(W, W)] if last else [(2, W, K), (2, W, K)],
            [(info, near, far, far)[chip], residual, field if chip else own_field, pupil_gain, TABLES, *planes],
            "adjoint",
            1_500_000_000,
            scratch=(plane, plane) if last else (),
            smem=(0,),
        )
        planes = outs
        *planes, energies = tied(*planes, energies + arrived)
    lines, rim = call(
        lines_kernel,
        [(K, W), (A, W)],
        [planes[0], TABLES],
        "lines",
        100_000_000,
    )
    from_rows = tile_move(rim, lambda source: {0: (1, 0), 3: (-1, 0)}.get(source // 2))
    (mine,) = call(rim_kernel, [(K + 8, W)], [lines, from_rows, energies], "rim", K * K)
    other = swap_cores(mine)
    inner, side = call(
        pixels_kernel,
        [(A, PIX), (A + 8, K)],
        [mine, other, TABLES],
        "pixels",
        100_000_000,
    )
    my_side = tile_move(side, lambda source: (0, -1) if source % 2 == 0 else (0, 1))
    other_side = swap_cores(my_side)
    mask_grad, weight_grad = call(
        join_kernel, [(1, A, PIX), (SOURCES,)], [inner, side, my_side, other_side], "join", A * PIX
    )
    return mask_grad, weight_grad


def solution(mesh):
    placed = (P("tile", None, None), P("tile", None, None), P(), P("src"), P("src", None, None))
    return jax.shard_map(
        body,
        mesh=mesh,
        in_specs=placed,
        out_specs=(P("tile", "src", None), P("src")),
        check_vma=False,
    )
```

```python
import functools
import math

import jax
import jax.numpy as jnp
import ml_dtypes
import numpy as np
from jax import lax
from jax.experimental import pallas as pl
from jax.experimental.pallas import tpu as pltpu
from jax.sharding import PartitionSpec as P

A = 64
TROWS = 4
TCOLS = 8
PIX = 512
N = PIX + 2 * A
K = 128
W = 256
SOURCES = 4
CHIPS = 4
BF = jnp.bfloat16
F32 = jnp.float32
BOTH = ("src", "tile")


def two_terms(table):
    first = table.astype(np.float32).astype(ml_dtypes.bfloat16)
    rest = (table - first.astype(np.float64)).astype(np.float32)
    return np.stack([first, rest.astype(ml_dtypes.bfloat16)])


def real_basis():
    angles = 2.0 * np.pi / N * np.mod(np.outer(np.arange(N), np.arange(K)), N)
    return np.concatenate([np.cos(angles), np.sin(angles)], axis=1) / math.sqrt(N)


def fold_table():
    ranks = np.arange(W) - K
    parts = np.arange(K)
    same = np.abs(ranks)[None, :] == parts[:, None]
    return np.concatenate([same * 1.0, same * np.sign(ranks)[None, :]], axis=0)


def coarse_table():
    ranks = np.arange(K) - K // 2
    angles = 2.0 * np.pi / W * np.mod(np.outer(ranks, np.arange(W)), W)
    down_real, down_imag = np.cos(angles) / math.sqrt(K), np.sin(angles) / math.sqrt(K)
    return np.block([[down_real, down_imag], [-down_imag, down_real]])


def interpolation():
    ranks = np.arange(1, K)
    shift = (np.arange(PIX) + A)[:, None] / N - np.arange(W)[None, :] / W
    return (1.0 + 2.0 * np.cos(2.0 * np.pi * shift[..., None] * ranks).sum(-1)) / W


ROWS = 64


def packed(entries):
    spots, pieces, at = {}, [], 0
    for name, tables in entries.items():
        spots[name] = []
        for table in tables:
            count = table.shape[0] // ROWS
            spots[name].append((at, count))
            pieces.append(table.reshape(count, ROWS, W))
            at += count
    return np.concatenate(pieces), spots


def two_halves(table):
    return [half for term in two_terms(table) for half in (term[:, :W], term[:, W:])]


def make_tables():
    basis = real_basis()
    coarse = coarse_table()
    spread = interpolation()
    fold = fold_table().astype(ml_dtypes.bfloat16)
    middle = basis[A : N - A]
    rims = np.concatenate([basis[:A], basis[N - A :]])
    sides = [two_terms(basis[:A].T), two_terms(basis[N - A :].T)]
    return packed(
        {
            "mid": two_terms(middle),
            "mid_t": two_halves(middle.T),
            "rims": two_terms(rims),
            "rims_t": [np.concatenate(list(two_terms(rims.T)), axis=1)],
            "sides": [np.concatenate([term for pair in sides for term in pair], axis=1)],
            "coarse": two_halves(coarse),
            "coarse_t": two_terms(coarse.T),
            "fold": [fold],
            "fold_t": [np.ascontiguousarray(fold.T)],
            "spread": two_terms(spread),
            "spread_t": two_halves(spread.T),
            "gram": two_terms(spread.T @ spread),
        }
    )


TABLES, SPOTS = make_tables()


def stored(ref, name, at=0):
    start, count = SPOTS[name][at]
    return ref[start : start + count].reshape(count * ROWS, W)


def narrow(ref, name):
    return stored(ref, name, 0), stored(ref, name, 1)


def wide(ref, name):
    return tuple(
        jnp.concatenate([stored(ref, name, at), stored(ref, name, at + 1)], axis=1) for at in (0, 2)
    )


def terms(value):
    first = value.astype(BF)
    return first, (value - first.astype(F32)).astype(BF)


def dot(first_op, second_op):
    return jnp.dot(first_op, second_op, preferred_element_type=F32)


def product(first_op, second_op):
    first_hi, first_lo = first_op
    second_hi, second_lo = second_op
    return dot(
        jnp.concatenate([first_hi, first_hi, first_lo], axis=1),
        jnp.concatenate([second_hi, second_lo, second_hi], axis=0),
    )


def exact_left(table, value):
    high, low = terms(value)
    return dot(table, high) + dot(table, low)


def exact_right(value, table):
    high, low = terms(value)
    return dot(high, table) + dot(low, table)


def call(kernel, outs, ins, name, flops, scratch=(), smem=(), bf16=(), grant=20):
    specs = [
        pl.BlockSpec(memory_space=pltpu.SMEM if at in smem else pltpu.VMEM) for at in range(len(ins))
    ]
    shapes = [jax.ShapeDtypeStruct(shape, BF if at in bf16 else F32) for at, shape in enumerate(outs)]
    moved = 4 * sum(math.prod(shape) for shape in outs) + sum(one.size * one.dtype.itemsize for one in ins)
    return pl.pallas_call(
        kernel,
        out_shape=shapes,
        in_specs=specs,
        out_specs=[pl.BlockSpec(memory_space=pltpu.VMEM) for _ in outs],
        scratch_shapes=list(scratch),
        compiler_params=pltpu.CompilerParams(vmem_limit_bytes=40 * 1024 * 1024),
        cost_estimate=pl.CostEstimate(flops=flops, bytes_accessed=moved, transcendentals=0),
        name=name,
    )(*ins)


def my_place():
    group = lax.axis_index("src")
    return group // 2, group % 2


def my_tile():
    tile = lax.axis_index("tile")
    return tile // TCOLS, lax.rem(tile, TCOLS)


def own_kernel(tile_ref, table_ref, rows_ref, rims_ref):
    rows_ref[...] = product(wide(table_ref, "mid_t"), terms(tile_ref[0]))
    rims_ref[...] = stored(table_ref, "rims_t")


def wanted_kernel(target_ref, table_ref, wanted_ref):
    upper = product(terms(target_ref[0]), narrow(table_ref, "spread"))
    wanted_ref[...] = product(wide(table_ref, "spread_t"), terms(upper)).T


def rows_kernel(rows_ref, mine_ref, other_ref, table_ref, all_ref, side_ref):
    _, core = my_place()
    first = core == 0
    mine, other = mine_ref[...], other_ref[...]
    row, _ = my_tile()
    upper = jnp.where(row > 0, jnp.where(first, mine, other), 0.0)
    lower = jnp.where(row < TROWS - 1, jnp.where(first, other, mine), 0.0)
    rim = jnp.concatenate([upper, lower], axis=0)
    table = table_ref[...]
    rows = rows_ref[...] + product((table[:, :K], table[:, K:]), terms(rim))
    all_ref[...] = rows
    side = jnp.where(first, rows[:, PIX - A :], rows[:, :A])
    side_ref[...] = jnp.concatenate([side[:K], side[K:]], axis=1)


def columns_kernel(rows_ref, table_ref, basis_ref):
    basis_ref[...] = product(terms(rows_ref[...]), narrow(table_ref, "mid"))


def disc_of(gain):
    rows = lax.broadcasted_iota(jnp.int32, (K, K), 0) - K // 2
    columns = lax.broadcasted_iota(jnp.int32, (K, K), 1) - K // 2
    return jnp.where(rows * rows + columns * columns <= (K // 2) ** 2, gain, 0.0)


def window_starts(info_refs, source):
    ref = info_refs[min(source // SOURCES, 2)]
    at = source % SOURCES + (SOURCES if source // SOURCES == 3 else 0)

    def start(coordinate):
        index = ref[at, coordinate, 0].astype(jnp.int32)
        return jnp.clip(lax.rem(index + K, N), 0, K)

    return start(0), start(1)


def weight_of(info_refs, source):
    ref = info_refs[min(source // SOURCES, 2)]
    return ref[source % SOURCES + (SOURCES if source // SOURCES == 3 else 0), 0, 1]


def image_of(info_refs, chips, planes, disc, table_ref, field_ref):
    coarse = wide(table_ref, "coarse")
    total = jnp.zeros((W, W), F32)
    for chip in chips:
        specs = []
        for source in range(chip * SOURCES, chip * SOURCES + SOURCES):
            row, column = window_starts(info_refs, source)

            def window(ref):
                rows = jnp.concatenate([ref[0, pl.ds(row, K), :], ref[1, pl.ds(row, K), :]], axis=1)
                return pltpu.roll(rows, lax.rem(W - column, W), 1)[:, :K] * disc

            specs.append(jnp.concatenate([window(ref) for ref in planes], axis=1))
        stacked = product(terms(jnp.concatenate(specs, axis=0)), coarse)
        for at in range(SOURCES):
            half = stacked[at * K : at * K + K].T
            half = jnp.concatenate([half[:W], half[W:]], axis=1)
            field = product(terms(half), coarse)
            field_ref[(chip - chips[0]) * SOURCES + at] = field
            real, imag = field[:, :W], field[:, W:]
            weight = weight_of(info_refs, chip * SOURCES + at)
            total = total + weight * (real * real + imag * imag)
    return total


def image_kernel(
    info_ref,
    basis_ref,
    mine_ref,
    other_ref,
    gain_ref,
    table_ref,
    field_ref,
    total_ref,
    real_ref,
    imag_ref,
):
    _, core = my_place()
    first = core == 0
    mine, other = mine_ref[...], other_ref[...]
    _, column = my_tile()
    left = jnp.where(column > 0, jnp.where(first, mine, other), 0.0)
    right = jnp.where(column < TCOLS - 1, jnp.where(first, other, mine), 0.0)
    rim = jnp.concatenate(
        [
            jnp.concatenate([left[:, :A], right[:, :A]], axis=1),
            jnp.concatenate([left[:, A:], right[:, A:]], axis=1),
        ],
        axis=0,
    )
    basis = basis_ref[...] + product(terms(rim), narrow(table_ref, "rims"))
    zero = jnp.zeros((K, K), F32)
    even = jnp.concatenate(
        [
            jnp.concatenate([basis[:K, :K], zero], axis=1),
            jnp.concatenate([zero, -basis[K:, K:]], axis=1),
        ],
        axis=0,
    )
    odd = jnp.concatenate(
        [
            jnp.concatenate([zero, -basis[:K, K:]], axis=1),
            jnp.concatenate([-basis[K:, :K], zero], axis=1),
        ],
        axis=0,
    )
    fold, fold_t = stored(table_ref, "fold"), stored(table_ref, "fold_t")
    for ref, part in ((real_ref, even), (imag_ref, odd)):
        plane = exact_right(exact_left(fold_t, part), fold)
        ref[0] = plane[:, :K]
        ref[1] = plane[:, K:]
    disc = disc_of(gain_ref[...])
    total_ref[...] = image_of((info_ref,), (0,), (real_ref, imag_ref), disc, table_ref, field_ref)


def others_kernel(
    near_ref, far_ref, gain_ref, table_ref, real_ref, imag_ref, before_ref, field_ref, total_ref
):
    info_refs = (None, near_ref, far_ref)
    disc = disc_of(gain_ref[...])
    total_ref[...] = before_ref[...] + image_of(
        info_refs, (1, 2, 3), (real_ref, imag_ref), disc, table_ref, field_ref
    )


def residual_kernel(mine_ref, other_ref, wanted_ref, field_ref, table_ref, residual_ref, energy_ref):
    bright = mine_ref[...] + other_ref[...]
    gram = narrow(table_ref, "gram")
    value = product(terms(product(gram, terms(bright))), gram)
    residual = value * (1.0 / (8 * SOURCES)) - wanted_ref[...]
    residual_ref[...] = residual
    lanes = lax.broadcasted_iota(jnp.int32, (8, K), 1)
    energies = jnp.zeros((8, K), F32)
    for source in range(SOURCES):
        real, imag = field_ref[source, :, :W], field_ref[source, :, W:]
        energy = jnp.sum(residual * (real * real + imag * imag))
        energies = jnp.where(lanes == source, energy, energies)
    energy_ref[...] = energies


def adjoint_kernel(
    chip,
    info_ref,
    residual_ref,
    field_ref,
    gain_ref,
    table_ref,
    real_in,
    imag_in,
    *outs,
):
    info_refs = (info_ref,) * 3
    first_field = SOURCES if chip else 0
    coarse_t = narrow(table_ref, "coarse_t")
    last = chip == CHIPS - 1
    real_ref, imag_ref = outs[1:] if last else outs
    residual = residual_ref[...]
    disc = disc_of(gain_ref[...])
    real_ref[...] = jnp.zeros((2, W, K), F32) if chip == 0 else real_in[...]
    imag_ref[...] = jnp.zeros((2, W, K), F32) if chip == 0 else imag_in[...]
    pad = jnp.zeros((K, K), F32)
    first = chip * SOURCES
    halves = []
    for source in range(first, first + SOURCES):
        field = field_ref.at[source - first_field]
        scaled = jnp.concatenate([residual * field[:, :W], residual * field[:, W:]], axis=1)
        half = product(terms(scaled), coarse_t).T
        halves.append(jnp.concatenate([half[:K], half[K:]], axis=1))
    spec = product(terms(jnp.concatenate(halves, axis=0)), coarse_t)
    for source in range(first, first + SOURCES):
        row, column = window_starts(info_refs, source)
        scale = disc * (2.0 * weight_of(info_refs, source))
        own = spec[(source - first) * K : (source - first) * K + K]
        for ref, part in ((real_ref, own[:, :K]), (imag_ref, own[:, K:])):
            spread = pltpu.roll(jnp.concatenate([part * scale, pad], axis=1), column, 1)
            for side in range(2):
                ref[side, pl.ds(row, K), :] += spread[:, side * K : side * K + K]
    if not last:
        return
    fold, fold_t = stored(table_ref, "fold"), stored(table_ref, "fold_t")

    def folded(ref):
        return exact_right(exact_left(fold, jnp.concatenate([ref[0], ref[1]], axis=1)), fold_t)

    even, odd = folded(real_ref), folded(imag_ref)
    outs[0][:K] = jnp.concatenate([even[:K, :K], -odd[:K, K:]], axis=1)
    outs[0][K:] = jnp.concatenate([-odd[K:, :K], -even[K:, K:]], axis=1)


def lines_kernel(mine_ref, table_ref, lines_ref, rim_ref):
    chip, _ = my_place()
    spectrum = terms(mine_ref[...])
    lines = [table_ref[pl.ds(SPOTS["mid"][at][0] + 2 * chip, 2)].reshape(K, W) for at in range(2)]
    lines_ref[...] = product(lines, spectrum)
    outer = [table_ref[SPOTS["rims"][at][0] + 1 - chip // 2] for at in range(2)]
    rim_ref[...] = product(outer, spectrum)


def rim_kernel(lines_ref, rim_ref, energy_ref, out_ref):
    chip, core = my_place()
    row, _ = my_tile()
    rim = rim_ref[...]
    out_ref[:A] = lines_ref[:A] + jnp.where((chip == 0) & (row > 0), rim, 0.0)
    out_ref[A:K] = lines_ref[A:] + jnp.where((chip == 3) & (row < TROWS - 1), rim, 0.0)
    energy = energy_ref[...]
    out_ref[K:] = jnp.concatenate([jnp.where(core == at, energy, 0.0) for at in range(2)], axis=1)


def pixels_kernel(mine_ref, other_ref, table_ref, inner_ref, side_ref):
    _, core = my_place()
    first = core == 0
    lines = mine_ref[...] + other_ref[...]
    top, bottom = lines[:A], lines[A:K]
    table = stored(table_ref, "sides")
    table = jnp.where(first, table[:, :K], table[:, K:])
    table = (table[:, :A], table[:, A:])
    side_ref[:A] = jnp.concatenate([product(terms(top), table), product(terms(bottom), table)], axis=1)
    lanes = lax.broadcasted_iota(jnp.int32, (8, K), 1)
    side_ref[A:] = jnp.where(lanes < A, lines[K:, :K], pltpu.roll(lines[K:, K:], A, 1))
    own = jnp.where(first, top, bottom)
    inner_ref[...] = product(terms(own), wide(table_ref, "mid_t"))


def join_kernel(inner_ref, before_ref, mine_ref, other_ref, out_ref, energy_ref):
    _, core = my_place()
    first = core == 0
    mine, other = mine_ref[...], other_ref[...]
    _, column = my_tile()
    left = jnp.where(column > 0, jnp.where(first, other[:A, :A], mine[:A, A:]), 0.0)
    right = jnp.where(column < TCOLS - 1, jnp.where(first, mine[:A, :A], other[:A, A:]), 0.0)
    inner = inner_ref[...]
    pad = jnp.zeros((A, A), F32)
    out_ref[0, :, :K] = inner[:, :K] + jnp.concatenate([left, pad], axis=1)
    out_ref[0, :, K : PIX - K] = inner[:, K : PIX - K]
    out_ref[0, :, PIX - K :] = inner[:, PIX - K :] + jnp.concatenate([pad, right], axis=1)
    odd = lax.rem(column, 2)
    total = before_ref[A : A + 1] + jnp.where(core == odd, mine[A : A + 1], other[A : A + 1])
    total = pltpu.roll(total, core * A, 1) * (16.0 / (TROWS * TCOLS * PIX * PIX))
    energy_ref[...] = total[0, :SOURCES]


def swap_cores(value):
    return lax.ppermute(value, "src", [(at, at ^ 1) for at in range(8)])


def chip_swap(value, low):
    pairs = []
    for source in range(2 * CHIPS):
        for tile in range(TROWS * TCOLS):
            step = 1 if tile % 2 == low else -1
            partner = (source // 2 + step) % CHIPS * 2 + source % 2
            pairs.append((source * 32 + tile, partner * 32 + (tile ^ 1)))
    return lax.ppermute(value, BOTH, pairs)


def tile_move(value, shift_of):
    pairs = []
    for source in range(2 * CHIPS):
        down, right = shift_of(source)
        for row in range(TROWS):
            for column in range(TCOLS):
                to = (row + down) % TROWS * TCOLS + (column + right) % TCOLS
                pairs.append((source * 32 + row * TCOLS + column, source * 32 + to))
    return lax.ppermute(value, BOTH, pairs)


def tile_swap(value, step):
    def partner(at):
        y, x, z = at // TCOLS, at // 2 % 4, at % 2
        if step == 0:
            z = 1 - z
        elif step < 3:
            x = x ^ 1 if step == 1 else 3 - x
        else:
            y = y ^ 1 if step == 3 else 3 - y
        return y * TCOLS + x * 2 + z

    return lax.ppermute(value, "tile", [(at, partner(at)) for at in range(TROWS * TCOLS)])


def tied(*values):
    return lax.optimization_barrier(values)


def body(mask_tiles, target, pupil_gain, weights, freq_index):
    core = lax.axis_index("src") % 2
    edge = jnp.where(core == 0, mask_tiles[0, PIX - A :], mask_tiles[0, :A])
    mine = tile_move(edge, lambda source: (1, 0) if source % 2 == 0 else (-1, 0))
    rows, rim_table = call(own_kernel, [(W, PIX), (W, W)], [mask_tiles, TABLES], "own", 400_000_000, bf16=(1,))
    rows, weights, freq_index = tied(rows, weights, freq_index)
    mine, rows = tied(mine, rows)
    other = swap_cores(mine)
    lanes = lax.broadcasted_iota(jnp.int32, freq_index.shape, 2)
    info = jnp.where(lanes == 1, weights[:, None, None], freq_index.astype(F32))
    near = chip_swap(info, 1)
    rows, side = call(
        rows_kernel, [(W, PIX), (K, K)], [rows, mine, other, rim_table], "rows", 100_000_000
    )
    my_side = tile_move(side, lambda source: (0, 1) if source % 2 == 0 else (0, -1))
    (basis,) = call(columns_kernel, [(W, W)], [rows, TABLES], "columns", 200_000_000)
    far = chip_swap(jnp.concatenate([info, near]), 0)
    my_side, basis = tied(my_side, basis)
    other_side = swap_cores(my_side)
    own_field, total, real, imag = call(
        image_kernel,
        [(SOURCES, W, 2 * W), (W, W), (2, W, K), (2, W, K)],
        [info, basis, my_side, other_side, pupil_gain, TABLES],
        "image",
        2_000_000_000,
        smem=(0,),
    )
    field, mine = call(
        others_kernel,
        [((CHIPS - 1) * SOURCES, W, 2 * W), (W, W)],
        [near, far, pupil_gain, TABLES, real, imag, total],
        "others",
        5_000_000_000,
        smem=(0, 1),
    )
    other = swap_cores(mine)
    (wanted,) = call(wanted_kernel, [(W, W)], [target, TABLES], "wanted", 600_000_000)
    other, wanted = tied(other, wanted)
    residual, energies = call(
        residual_kernel, [(W, W), (8, K)], [mine, other, wanted, own_field, TABLES], "residual", 300_000_000
    )
    plane = pltpu.VMEM((2, W, K), F32)
    planes = (jnp.zeros((8, K), F32),) * 2
    for chip in range(CHIPS):
        arrived = tile_swap(energies, (3, 1, 4, 2)[chip])
        last = chip == CHIPS - 1
        outs = call(
            functools.partial(adjoint_kernel, chip),
            [(W, W)] if last else [(2, W, K), (2, W, K)],
            [(info, near, far, far)[chip], residual, field if chip else own_field, pupil_gain, TABLES, *planes],
            "adjoint",
            1_500_000_000,
            scratch=(plane, plane) if last else (),
            smem=(0,),
        )
        planes = outs
        *planes, energies = tied(*planes, energies + arrived)
    lines, rim = call(
        lines_kernel,
        [(K, W), (A, W)],
        [planes[0], TABLES],
        "lines",
        100_000_000,
    )
    from_rows = tile_move(rim, lambda source: (1, 0) if source < CHIPS else (-1, 0))
    (mine,) = call(rim_kernel, [(K + 8, W)], [lines, from_rows, energies], "rim", K * K)
    other = swap_cores(mine)
    inner, side = call(
        pixels_kernel,
        [(A, PIX), (A + 8, K)],
        [mine, other, TABLES],
        "pixels",
        100_000_000,
    )
    my_side = tile_move(side, lambda source: (0, -1) if source % 2 == 0 else (0, 1))
    other_side = swap_cores(my_side)
    mask_grad, weight_grad = call(
        join_kernel, [(1, A, PIX), (SOURCES,)], [inner, side, my_side, other_side], "join", A * PIX
    )
    return mask_grad, weight_grad


def solution(mesh):
    placed = (P("tile", None, None), P("tile", None, None), P(), P("src"), P("src", None, None))
    return jax.shard_map(
        body,
        mesh=mesh,
        in_specs=placed,
        out_specs=(P("tile", "src", None), P("src")),
        check_vma=False,
    )
```

```python
import functools
import math

import jax
import jax.numpy as jnp
import ml_dtypes
import numpy as np
from jax import lax
from jax.experimental import pallas as pl
from jax.experimental.pallas import tpu as pltpu
from jax.sharding import PartitionSpec as P

A = 64
TROWS = 4
TCOLS = 8
PIX = 512
N = PIX + 2 * A
K = 128
W = 256
SOURCES = 4
CHIPS = 4
BF = jnp.bfloat16
F32 = jnp.float32
BOTH = ("src", "tile")


def two_terms(table):
    first = table.astype(np.float32).astype(ml_dtypes.bfloat16)
    rest = (table - first.astype(np.float64)).astype(np.float32)
    return np.stack([first, rest.astype(ml_dtypes.bfloat16)])


def real_basis():
    angles = 2.0 * np.pi / N * np.mod(np.outer(np.arange(N), np.arange(K)), N)
    return np.concatenate([np.cos(angles), np.sin(angles)], axis=1) / math.sqrt(N)


def fold_table():
    ranks = np.arange(W) - K
    parts = np.arange(K)
    same = np.abs(ranks)[None, :] == parts[:, None]
    return np.concatenate([same * 1.0, same * np.sign(ranks)[None, :]], axis=0)


def coarse_table():
    ranks = np.arange(K) - K // 2
    angles = 2.0 * np.pi / W * np.mod(np.outer(ranks, np.arange(W)), W)
    down_real, down_imag = np.cos(angles) / math.sqrt(K), np.sin(angles) / math.sqrt(K)
    return np.block([[down_real, down_imag], [-down_imag, down_real]])


def interpolation():
    ranks = np.arange(1, K)
    shift = (np.arange(PIX) + A)[:, None] / N - np.arange(W)[None, :] / W
    return (1.0 + 2.0 * np.cos(2.0 * np.pi * shift[..., None] * ranks).sum(-1)) / W


ROWS = 64


def packed(entries):
    spots, pieces, at = {}, [], 0
    for name, tables in entries.items():
        spots[name] = []
        for table in tables:
            count = table.shape[0] // ROWS
            spots[name].append((at, count))
            pieces.append(table.reshape(count, ROWS, W))
            at += count
    return np.concatenate(pieces), spots


def two_halves(table):
    return [half for term in two_terms(table) for half in (term[:, :W], term[:, W:])]


def make_tables():
    basis = real_basis()
    coarse = coarse_table()
    spread = interpolation()
    fold = fold_table().astype(ml_dtypes.bfloat16)
    middle = basis[A : N - A]
    rims = np.concatenate([basis[:A], basis[N - A :]])
    sides = [two_terms(basis[:A].T), two_terms(basis[N - A :].T)]
    early = packed(
        {
            "mid": two_terms(middle),
            "mid_t": two_halves(middle.T),
            "rims": two_terms(rims),
            "rims_t": [np.concatenate(list(two_terms(rims.T)), axis=1)],
            "sides": [np.concatenate([term for pair in sides for term in pair], axis=1)],
        }
    )
    late = packed(
        {
            "coarse": two_halves(coarse),
            "coarse_t": two_terms(coarse.T),
            "fold": [fold],
            "fold_t": [np.ascontiguousarray(fold.T)],
            "spread": two_terms(spread),
            "spread_t": two_halves(spread.T),
            "gram": two_terms(spread.T @ spread),
        }
    )
    return early, late


(EARLY, EARLY_AT), (LATE, LATE_AT) = make_tables()
SPOTS = EARLY_AT | LATE_AT


def stored(ref, name, at=0):
    start, count = SPOTS[name][at]
    return ref[start : start + count].reshape(count * ROWS, W)


def narrow(ref, name):
    return stored(ref, name, 0), stored(ref, name, 1)


def wide(ref, name):
    return tuple(
        jnp.concatenate([stored(ref, name, at), stored(ref, name, at + 1)], axis=1) for at in (0, 2)
    )


def terms(value):
    first = value.astype(BF)
    return first, (value - first.astype(F32)).astype(BF)


def dot(first_op, second_op):
    return jnp.dot(first_op, second_op, preferred_element_type=F32)


def product(first_op, second_op):
    first_hi, first_lo = first_op
    second_hi, second_lo = second_op
    return dot(
        jnp.concatenate([first_hi, first_hi, first_lo], axis=1),
        jnp.concatenate([second_hi, second_lo, second_hi], axis=0),
    )


def exact_left(table, value):
    high, low = terms(value)
    return dot(table, high) + dot(table, low)


def exact_right(value, table):
    high, low = terms(value)
    return dot(high, table) + dot(low, table)


def call(kernel, outs, ins, name, flops, scratch=(), smem=(), bf16=(), grant=20):
    specs = [
        pl.BlockSpec(memory_space=pltpu.SMEM if at in smem else pltpu.VMEM) for at in range(len(ins))
    ]
    shapes = [jax.ShapeDtypeStruct(shape, BF if at in bf16 else F32) for at, shape in enumerate(outs)]
    moved = 4 * sum(math.prod(shape) for shape in outs) + sum(one.size * one.dtype.itemsize for one in ins)
    return pl.pallas_call(
        kernel,
        out_shape=shapes,
        in_specs=specs,
        out_specs=[pl.BlockSpec(memory_space=pltpu.VMEM) for _ in outs],
        scratch_shapes=list(scratch),
        compiler_params=pltpu.CompilerParams(vmem_limit_bytes=40 * 1024 * 1024),
        cost_estimate=pl.CostEstimate(flops=flops, bytes_accessed=moved, transcendentals=0),
        name=name,
    )(*ins)


def my_place():
    group = lax.axis_index("src")
    return group // 2, group % 2


def my_tile():
    tile = lax.axis_index("tile")
    return tile // TCOLS, lax.rem(tile, TCOLS)


def own_kernel(tile_ref, table_ref, rows_ref, rims_ref):
    rows_ref[...] = product(wide(table_ref, "mid_t"), terms(tile_ref[0]))
    rims_ref[...] = stored(table_ref, "rims_t")


def wanted_kernel(target_ref, table_ref, wanted_ref):
    upper = product(terms(target_ref[0]), narrow(table_ref, "spread"))
    wanted_ref[...] = product(wide(table_ref, "spread_t"), terms(upper)).T


def rows_kernel(rows_ref, mine_ref, other_ref, table_ref, all_ref, side_ref):
    _, core = my_place()
    first = core == 0
    mine, other = mine_ref[...], other_ref[...]
    row, _ = my_tile()
    upper = jnp.where(row > 0, jnp.where(first, mine, other), 0.0)
    lower = jnp.where(row < TROWS - 1, jnp.where(first, other, mine), 0.0)
    rim = jnp.concatenate([upper, lower], axis=0)
    table = table_ref[...]
    rows = rows_ref[...] + product((table[:, :K], table[:, K:]), terms(rim))
    all_ref[...] = rows
    side = jnp.where(first, rows[:, PIX - A :], rows[:, :A])
    side_ref[...] = jnp.concatenate([side[:K], side[K:]], axis=1)


def columns_kernel(rows_ref, table_ref, _, basis_ref):
    basis_ref[...] = product(terms(rows_ref[...]), narrow(table_ref, "mid"))


def disc_of(gain):
    rows = lax.broadcasted_iota(jnp.int32, (K, K), 0) - K // 2
    columns = lax.broadcasted_iota(jnp.int32, (K, K), 1) - K // 2
    return jnp.where(rows * rows + columns * columns <= (K // 2) ** 2, gain, 0.0)


def window_starts(info_refs, source):
    ref = info_refs[min(source // SOURCES, 2)]
    at = source % SOURCES + (SOURCES if source // SOURCES == 3 else 0)

    def start(coordinate):
        index = ref[at, coordinate, 0].astype(jnp.int32)
        return jnp.clip(lax.rem(index + K, N), 0, K)

    return start(0), start(1)


def weight_of(info_refs, source):
    ref = info_refs[min(source // SOURCES, 2)]
    return ref[source % SOURCES + (SOURCES if source // SOURCES == 3 else 0), 0, 1]


def image_of(info_refs, chips, planes, disc, table_ref, field_ref):
    coarse = wide(table_ref, "coarse")
    total = jnp.zeros((W, W), F32)
    for chip in chips:
        specs = []
        for source in range(chip * SOURCES, chip * SOURCES + SOURCES):
            row, column = window_starts(info_refs, source)

            def window(ref):
                rows = jnp.concatenate([ref[0, pl.ds(row, K), :], ref[1, pl.ds(row, K), :]], axis=1)
                return pltpu.roll(rows, lax.rem(W - column, W), 1)[:, :K] * disc

            specs.append(jnp.concatenate([window(ref) for ref in planes], axis=1))
        stacked = product(terms(jnp.concatenate(specs, axis=0)), coarse)
        for at in range(SOURCES):
            half = stacked[at * K : at * K + K].T
            half = jnp.concatenate([half[:W], half[W:]], axis=1)
            field = product(terms(half), coarse)
            field_ref[(chip - chips[0]) * SOURCES + at] = field
            real, imag = field[:, :W], field[:, W:]
            weight = weight_of(info_refs, chip * SOURCES + at)
            total = total + weight * (real * real + imag * imag)
    return total


def image_kernel(
    info_ref,
    basis_ref,
    mine_ref,
    other_ref,
    gain_ref,
    early_ref,
    table_ref,
    field_ref,
    total_ref,
    real_ref,
    imag_ref,
):
    _, core = my_place()
    first = core == 0
    mine, other = mine_ref[...], other_ref[...]
    _, column = my_tile()
    left = jnp.where(column > 0, jnp.where(first, mine, other), 0.0)
    right = jnp.where(column < TCOLS - 1, jnp.where(first, other, mine), 0.0)
    rim = jnp.concatenate(
        [
            jnp.concatenate([left[:, :A], right[:, :A]], axis=1),
            jnp.concatenate([left[:, A:], right[:, A:]], axis=1),
        ],
        axis=0,
    )
    basis = basis_ref[...] + product(terms(rim), narrow(early_ref, "rims"))
    zero = jnp.zeros((K, K), F32)
    even = jnp.concatenate(
        [
            jnp.concatenate([basis[:K, :K], zero], axis=1),
            jnp.concatenate([zero, -basis[K:, K:]], axis=1),
        ],
        axis=0,
    )
    odd = jnp.concatenate(
        [
            jnp.concatenate([zero, -basis[:K, K:]], axis=1),
            jnp.concatenate([-basis[K:, :K], zero], axis=1),
        ],
        axis=0,
    )
    fold, fold_t = stored(table_ref, "fold"), stored(table_ref, "fold_t")
    for ref, part in ((real_ref, even), (imag_ref, odd)):
        plane = exact_right(exact_left(fold_t, part), fold)
        ref[0] = plane[:, :K]
        ref[1] = plane[:, K:]
    disc = disc_of(gain_ref[...])
    total_ref[...] = image_of((info_ref,), (0,), (real_ref, imag_ref), disc, table_ref, field_ref)


def others_kernel(
    near_ref, far_ref, gain_ref, table_ref, real_ref, imag_ref, before_ref, field_ref, total_ref
):
    info_refs = (None, near_ref, far_ref)
    disc = disc_of(gain_ref[...])
    total_ref[...] = before_ref[...] + image_of(
        info_refs, (1, 2, 3), (real_ref, imag_ref), disc, table_ref, field_ref
    )


def residual_kernel(mine_ref, other_ref, wanted_ref, field_ref, table_ref, residual_ref, energy_ref):
    bright = mine_ref[...] + other_ref[...]
    gram = narrow(table_ref, "gram")
    value = product(terms(product(gram, terms(bright))), gram)
    residual = value * (1.0 / (8 * SOURCES)) - wanted_ref[...]
    residual_ref[...] = residual
    lanes = lax.broadcasted_iota(jnp.int32, (8, K), 1)
    energies = jnp.zeros((8, K), F32)
    for source in range(SOURCES):
        real, imag = field_ref[source, :, :W], field_ref[source, :, W:]
        energy = jnp.sum(residual * (real * real + imag * imag))
        energies = jnp.where(lanes == source, energy, energies)
    energy_ref[...] = energies


def adjoint_kernel(
    chip,
    info_ref,
    residual_ref,
    field_ref,
    gain_ref,
    table_ref,
    early_ref,
    real_in,
    imag_in,
    *outs,
):
    info_refs = (info_ref,) * 3
    first_field = SOURCES if chip else 0
    coarse_t = narrow(table_ref, "coarse_t")
    last = chip == CHIPS - 1
    real_ref, imag_ref = outs[2:] if last else outs
    residual = residual_ref[...]
    disc = disc_of(gain_ref[...])
    real_ref[...] = jnp.zeros((2, W, K), F32) if chip == 0 else real_in[...]
    imag_ref[...] = jnp.zeros((2, W, K), F32) if chip == 0 else imag_in[...]
    pad = jnp.zeros((K, K), F32)
    first = chip * SOURCES
    halves = []
    for source in range(first, first + SOURCES):
        field = field_ref.at[source - first_field]
        scaled = jnp.concatenate([residual * field[:, :W], residual * field[:, W:]], axis=1)
        half = product(terms(scaled), coarse_t).T
        halves.append(jnp.concatenate([half[:K], half[K:]], axis=1))
    spec = product(terms(jnp.concatenate(halves, axis=0)), coarse_t)
    for source in range(first, first + SOURCES):
        row, column = window_starts(info_refs, source)
        scale = disc * (2.0 * weight_of(info_refs, source))
        own = spec[(source - first) * K : (source - first) * K + K]
        for ref, part in ((real_ref, own[:, :K]), (imag_ref, own[:, K:])):
            spread = pltpu.roll(jnp.concatenate([part * scale, pad], axis=1), column, 1)
            for side in range(2):
                ref[side, pl.ds(row, K), :] += spread[:, side * K : side * K + K]
    if not last:
        return
    fold, fold_t = stored(table_ref, "fold"), stored(table_ref, "fold_t")
    real, imag = (
        exact_left(fold, jnp.concatenate([ref[0], ref[1]], axis=1)) for ref in (real_ref, imag_ref)
    )
    cosines = exact_right(jnp.concatenate([real[:K], -imag[K:]], axis=0), fold_t[:, :K])
    sines = exact_right(jnp.concatenate([-imag[:K], -real[K:]], axis=0), fold_t[:, K:])
    spectrum = terms(jnp.concatenate([cosines, sines], axis=1))
    lines_ref, rim_ref = outs[:2]
    place, _ = my_place()
    lines = [early_ref[pl.ds(SPOTS["mid"][at][0] + 2 * place, 2)].reshape(K, W) for at in range(2)]
    lines_ref[...] = product(lines, spectrum)
    outer = [early_ref[SPOTS["rims"][at][0] + 1 - place // 2] for at in range(2)]
    rim_ref[...] = product(outer, spectrum)


def rim_kernel(lines_ref, rim_ref, energy_ref, out_ref):
    chip, core = my_place()
    row, _ = my_tile()
    rim = rim_ref[...]
    out_ref[:A] = lines_ref[:A] + jnp.where((chip == 0) & (row > 0), rim, 0.0)
    out_ref[A:K] = lines_ref[A:] + jnp.where((chip == 3) & (row < TROWS - 1), rim, 0.0)
    energy = energy_ref[...]
    out_ref[K:] = jnp.concatenate([jnp.where(core == at, energy, 0.0) for at in range(2)], axis=1)


def pixels_kernel(mine_ref, other_ref, table_ref, inner_ref, side_ref):
    _, core = my_place()
    first = core == 0
    lines = mine_ref[...] + other_ref[...]
    top, bottom = lines[:A], lines[A:K]
    table = stored(table_ref, "sides")
    table = jnp.where(first, table[:, :K], table[:, K:])
    table = (table[:, :A], table[:, A:])
    side_ref[:A] = jnp.concatenate([product(terms(top), table), product(terms(bottom), table)], axis=1)
    lanes = lax.broadcasted_iota(jnp.int32, (8, K), 1)
    side_ref[A:] = jnp.where(lanes < A, lines[K:, :K], pltpu.roll(lines[K:, K:], A, 1))
    own = jnp.where(first, top, bottom)
    inner_ref[...] = product(terms(own), wide(table_ref, "mid_t"))


def join_kernel(inner_ref, before_ref, mine_ref, other_ref, out_ref, energy_ref):
    _, core = my_place()
    first = core == 0
    mine, other = mine_ref[...], other_ref[...]
    _, column = my_tile()
    left = jnp.where(column > 0, jnp.where(first, other[:A, :A], mine[:A, A:]), 0.0)
    right = jnp.where(column < TCOLS - 1, jnp.where(first, mine[:A, :A], other[:A, A:]), 0.0)
    inner = inner_ref[...]
    pad = jnp.zeros((A, A), F32)
    out_ref[0, :, :K] = inner[:, :K] + jnp.concatenate([left, pad], axis=1)
    out_ref[0, :, K : PIX - K] = inner[:, K : PIX - K]
    out_ref[0, :, PIX - K :] = inner[:, PIX - K :] + jnp.concatenate([pad, right], axis=1)
    odd = lax.rem(column, 2)
    total = before_ref[A : A + 1] + jnp.where(core == odd, mine[A : A + 1], other[A : A + 1])
    total = pltpu.roll(total, core * A, 1) * (16.0 / (TROWS * TCOLS * PIX * PIX))
    energy_ref[...] = total[0, :SOURCES]


def swap_cores(value):
    return lax.ppermute(value, "src", [(at, at ^ 1) for at in range(8)])


def chip_swap(value, low):
    pairs = []
    for source in range(2 * CHIPS):
        for tile in range(TROWS * TCOLS):
            step = 1 if tile % 2 == low else -1
            partner = (source // 2 + step) % CHIPS * 2 + source % 2
            pairs.append((source * 32 + tile, partner * 32 + (tile ^ 1)))
    return lax.ppermute(value, BOTH, pairs)


def tile_move(value, shift_of):
    pairs = []
    for source in range(2 * CHIPS):
        down, right = shift_of(source)
        turns = shift_of(source ^ 1) == (-down, -right)
        for row in range(TROWS):
            for column in range(TCOLS):
                to_row, to_column = row + down, column + right
                inside = 0 <= to_row < TROWS and 0 <= to_column < TCOLS
                to = to_row % TROWS * TCOLS + to_column % TCOLS
                to = source * 32 + to if inside or not turns else (source ^ 1) * 32 + row * TCOLS + column
                pairs.append((source * 32 + row * TCOLS + column, to))
    return lax.ppermute(value, BOTH, pairs)


def tile_swap(value, step):
    def partner(at):
        y, x, z = at // TCOLS, at // 2 % 4, at % 2
        if step == 0:
            z = 1 - z
        elif step < 3:
            x = x ^ 1 if step == 1 else 3 - x
        else:
            y = y ^ 1 if step == 3 else 3 - y
        return y * TCOLS + x * 2 + z

    return lax.ppermute(value, "tile", [(at, partner(at)) for at in range(TROWS * TCOLS)])


def tied(*values):
    return lax.optimization_barrier(values)


def body(mask_tiles, target, pupil_gain, weights, freq_index):
    core = lax.axis_index("src") % 2
    edge = jnp.where(core == 0, mask_tiles[0, PIX - A :], mask_tiles[0, :A])
    mine = tile_move(edge, lambda source: (1, 0) if source % 2 == 0 else (-1, 0))
    rows, rim_table = call(own_kernel, [(W, PIX), (W, W)], [mask_tiles, EARLY], "own", 400_000_000, bf16=(1,))
    rows, weights, freq_index = tied(rows, weights, freq_index)
    mine, rows = tied(mine, rows)
    other = swap_cores(mine)
    lanes = lax.broadcasted_iota(jnp.int32, freq_index.shape, 2)
    info = jnp.where(lanes == 1, weights[:, None, None], freq_index.astype(F32))
    near = chip_swap(info, 1)
    rows, side = call(
        rows_kernel, [(W, PIX), (K, K)], [rows, mine, other, rim_table], "rows", 100_000_000
    )
    my_side = tile_move(side, lambda source: (0, 1) if source % 2 == 0 else (0, -1))
    (basis,) = call(columns_kernel, [(W, W)], [rows, EARLY, LATE], "columns", 200_000_000)
    far = chip_swap(jnp.concatenate([info, near]), 0)
    my_side, basis = tied(my_side, basis)
    other_side = swap_cores(my_side)
    own_field, total, real, imag = call(
        image_kernel,
        [(SOURCES, W, 2 * W), (W, W), (2, W, K), (2, W, K)],
        [info, basis, my_side, other_side, pupil_gain, EARLY, LATE],
        "image",
        2_000_000_000,
        smem=(0,),
    )
    field, mine = call(
        others_kernel,
        [((CHIPS - 1) * SOURCES, W, 2 * W), (W, W)],
        [near, far, pupil_gain, LATE, real, imag, total],
        "others",
        5_000_000_000,
        smem=(0, 1),
    )
    other = swap_cores(mine)
    (wanted,) = call(wanted_kernel, [(W, W)], [target, LATE], "wanted", 600_000_000)
    other, wanted = tied(other, wanted)
    residual, energies = call(
        residual_kernel, [(W, W), (8, K)], [mine, other, wanted, own_field, LATE], "residual", 300_000_000
    )
    plane = pltpu.VMEM((2, W, K), F32)
    planes = (jnp.zeros((8, K), F32),) * 2
    for chip in range(CHIPS):
        arrived = tile_swap(energies, (3, 1, 4, 2)[chip])
        last = chip == CHIPS - 1
        outs = call(
            functools.partial(adjoint_kernel, chip),
            [(K, W), (A, W)] if last else [(2, W, K), (2, W, K)],
            [(info, near, far, far)[chip], residual, field if chip else own_field, pupil_gain, LATE, EARLY, *planes],
            "adjoint",
            1_500_000_000,
            scratch=(plane, plane) if last else (),
            smem=(0,),
        )
        planes = outs
        *planes, energies = tied(*planes, energies + arrived)
    lines, rim = planes
    from_rows = tile_move(rim, lambda source: (1, 0) if source < CHIPS else (-1, 0))
    (mine,) = call(rim_kernel, [(K + 8, W)], [lines, from_rows, energies], "rim", K * K)
    other = swap_cores(mine)
    inner, side = call(
        pixels_kernel,
        [(A, PIX), (A + 8, K)],
        [mine, other, EARLY],
        "pixels",
        100_000_000,
    )
    my_side = tile_move(side, lambda source: (0, -1) if source % 2 == 0 else (0, 1))
    other_side = swap_cores(my_side)
    mask_grad, weight_grad = call(
        join_kernel, [(1, A, PIX), (SOURCES,)], [inner, side, my_side, other_side], "join", A * PIX
    )
    return mask_grad, weight_grad


def solution(mesh):
    placed = (P("tile", None, None), P("tile", None, None), P(), P("src"), P("src", None, None))
    return jax.shard_map(
        body,
        mesh=mesh,
        in_specs=placed,
        out_specs=(P("tile", "src", None), P("src")),
        check_vma=False,
    )
```

```python
import functools
import math

import jax
import jax.numpy as jnp
import ml_dtypes
import numpy as np
from jax import lax
from jax.experimental import pallas as pl
from jax.experimental.pallas import tpu as pltpu
from jax.sharding import PartitionSpec as P

A = 64
TROWS = 4
TCOLS = 8
PIX = 512
N = PIX + 2 * A
K = 128
W = 256
SOURCES = 4
CHIPS = 4
BF = jnp.bfloat16
F32 = jnp.float32
BOTH = ("src", "tile")


def two_terms(table):
    first = table.astype(np.float32).astype(ml_dtypes.bfloat16)
    rest = (table - first.astype(np.float64)).astype(np.float32)
    return np.stack([first, rest.astype(ml_dtypes.bfloat16)])


def real_basis():
    angles = 2.0 * np.pi / N * np.mod(np.outer(np.arange(N), np.arange(K)), N)
    return np.concatenate([np.cos(angles), np.sin(angles)], axis=1) / math.sqrt(N)


def fold_table():
    ranks = np.arange(W) - K
    parts = np.arange(K)
    same = np.abs(ranks)[None, :] == parts[:, None]
    return np.concatenate([same * 1.0, same * np.sign(ranks)[None, :]], axis=0)


def coarse_table():
    ranks = np.arange(K) - K // 2
    angles = 2.0 * np.pi / W * np.mod(np.outer(ranks, np.arange(W)), W)
    down_real, down_imag = np.cos(angles) / math.sqrt(K), np.sin(angles) / math.sqrt(K)
    return np.block([[down_real, down_imag], [-down_imag, down_real]])


def interpolation():
    ranks = np.arange(1, K)
    shift = (np.arange(PIX) + A)[:, None] / N - np.arange(W)[None, :] / W
    return (1.0 + 2.0 * np.cos(2.0 * np.pi * shift[..., None] * ranks).sum(-1)) / W


ROWS = 64


def packed(entries):
    spots, pieces, at = {}, [], 0
    for name, tables in entries.items():
        spots[name] = []
        for table in tables:
            count = table.shape[0] // ROWS
            spots[name].append((at, count))
            pieces.append(table.reshape(count, ROWS, W))
            at += count
    return np.concatenate(pieces), spots


def two_halves(table):
    return [half for term in two_terms(table) for half in (term[:, :W], term[:, W:])]


def make_tables():
    basis = real_basis()
    coarse = coarse_table()
    spread = interpolation()
    fold = fold_table().astype(ml_dtypes.bfloat16)
    middle = basis[A : N - A]
    rims = np.concatenate([basis[:A], basis[N - A :]])
    sides = [two_terms(basis[:A].T), two_terms(basis[N - A :].T)]
    early = packed(
        {
            "mid": two_terms(middle),
            "mid_t": two_halves(middle.T),
            "rims": two_terms(rims),
            "rims_t": [np.concatenate(list(two_terms(rims.T)), axis=1)],
            "sides": [np.concatenate([term for pair in sides for term in pair], axis=1)],
        }
    )
    late = packed(
        {
            "coarse": two_halves(coarse),
            "coarse_t": two_terms(coarse.T),
            "fold": [fold],
            "fold_t": [np.ascontiguousarray(fold.T)],
            "spread": two_terms(spread),
            "spread_t": two_halves(spread.T),
            "gram": two_terms(spread.T @ spread),
        }
    )
    return early, late


(EARLY, EARLY_AT), (LATE, LATE_AT) = make_tables()
SPOTS = EARLY_AT | LATE_AT


def stored(ref, name, at=0):
    start, count = SPOTS[name][at]
    return ref[start : start + count].reshape(count * ROWS, W)


def narrow(ref, name):
    return stored(ref, name, 0), stored(ref, name, 1)


def wide(ref, name):
    return tuple(
        jnp.concatenate([stored(ref, name, at), stored(ref, name, at + 1)], axis=1) for at in (0, 2)
    )


def terms(value):
    first = value.astype(BF)
    return first, (value - first.astype(F32)).astype(BF)


def dot(first_op, second_op):
    return jnp.dot(first_op, second_op, preferred_element_type=F32)


def product(first_op, second_op):
    first_hi, first_lo = first_op
    second_hi, second_lo = second_op
    return dot(
        jnp.concatenate([first_hi, first_hi, first_lo], axis=1),
        jnp.concatenate([second_hi, second_lo, second_hi], axis=0),
    )


def exact_left(table, value):
    high, low = terms(value)
    return dot(table, high) + dot(table, low)


def exact_right(value, table):
    high, low = terms(value)
    return dot(high, table) + dot(low, table)


def call(kernel, outs, ins, name, flops, scratch=(), smem=(), bf16=(), grant=20):
    specs = [
        pl.BlockSpec(memory_space=pltpu.SMEM if at in smem else pltpu.VMEM) for at in range(len(ins))
    ]
    shapes = [jax.ShapeDtypeStruct(shape, BF if at in bf16 else F32) for at, shape in enumerate(outs)]
    moved = 4 * sum(math.prod(shape) for shape in outs) + sum(one.size * one.dtype.itemsize for one in ins)
    return pl.pallas_call(
        kernel,
        out_shape=shapes,
        in_specs=specs,
        out_specs=[pl.BlockSpec(memory_space=pltpu.VMEM) for _ in outs],
        scratch_shapes=list(scratch),
        compiler_params=pltpu.CompilerParams(vmem_limit_bytes=40 * 1024 * 1024),
        cost_estimate=pl.CostEstimate(flops=flops, bytes_accessed=moved, transcendentals=0),
        name=name,
    )(*ins)


def my_place():
    group = lax.axis_index("src")
    return group // 2, group % 2


def my_tile():
    tile = lax.axis_index("tile")
    return tile // TCOLS, lax.rem(tile, TCOLS)


def own_kernel(tile_ref, table_ref, rows_ref, rims_ref):
    rows_ref[...] = product(wide(table_ref, "mid_t"), terms(tile_ref[0]))
    rims_ref[...] = stored(table_ref, "rims_t")


def wanted_kernel(target_ref, table_ref, wanted_ref):
    upper = product(terms(target_ref[0]), narrow(table_ref, "spread"))
    wanted_ref[...] = product(wide(table_ref, "spread_t"), terms(upper)).T


def rows_kernel(rows_ref, mine_ref, other_ref, table_ref, all_ref, side_ref):
    _, core = my_place()
    first = core == 0
    mine, other = mine_ref[...], other_ref[...]
    row, _ = my_tile()
    upper = jnp.where(row > 0, jnp.where(first, mine, other), 0.0)
    lower = jnp.where(row < TROWS - 1, jnp.where(first, other, mine), 0.0)
    rim = jnp.concatenate([upper, lower], axis=0)
    table = table_ref[...]
    rows = rows_ref[...] + product((table[:, :K], table[:, K:]), terms(rim))
    all_ref[...] = rows
    side = jnp.where(first, rows[:, PIX - A :], rows[:, :A])
    side_ref[...] = jnp.concatenate([side[:K], side[K:]], axis=1)


def columns_kernel(rows_ref, table_ref, _, basis_ref):
    basis_ref[...] = product(terms(rows_ref[...]), narrow(table_ref, "mid"))


def disc_of(gain):
    rows = lax.broadcasted_iota(jnp.int32, (K, K), 0) - K // 2
    columns = lax.broadcasted_iota(jnp.int32, (K, K), 1) - K // 2
    return jnp.where(rows * rows + columns * columns <= (K // 2) ** 2, gain, 0.0)


def window_starts(info_refs, source):
    ref = info_refs[min(source // SOURCES, 2)]
    at = source % SOURCES + (SOURCES if source // SOURCES == 3 else 0)

    def start(coordinate):
        index = ref[at, coordinate, 0].astype(jnp.int32)
        return jnp.clip(lax.rem(index + K, N), 0, K)

    return start(0), start(1)


def weight_of(info_refs, source):
    ref = info_refs[min(source // SOURCES, 2)]
    return ref[source % SOURCES + (SOURCES if source // SOURCES == 3 else 0), 0, 1]


def image_of(info_refs, chips, planes, disc, table_ref, field_ref):
    coarse = wide(table_ref, "coarse")
    total = jnp.zeros((W, W), F32)
    for chip in chips:
        specs = []
        for source in range(chip * SOURCES, chip * SOURCES + SOURCES):
            row, column = window_starts(info_refs, source)

            def window(ref):
                rows = jnp.concatenate([ref[0, pl.ds(row, K), :], ref[1, pl.ds(row, K), :]], axis=1)
                return pltpu.roll(rows, lax.rem(W - column, W), 1)[:, :K] * disc

            specs.append(jnp.concatenate([window(ref) for ref in planes], axis=1))
        stacked = product(terms(jnp.concatenate(specs, axis=0)), coarse)
        for at in range(SOURCES):
            half = stacked[at * K : at * K + K].T
            half = jnp.concatenate([half[:W], half[W:]], axis=1)
            field = product(terms(half), coarse)
            field_ref[(chip - chips[0]) * SOURCES + at] = field
            real, imag = field[:, :W], field[:, W:]
            weight = weight_of(info_refs, chip * SOURCES + at)
            total = total + weight * (real * real + imag * imag)
    return total


def image_kernel(
    info_ref,
    basis_ref,
    mine_ref,
    other_ref,
    gain_ref,
    early_ref,
    table_ref,
    field_ref,
    total_ref,
    real_ref,
    imag_ref,
):
    _, core = my_place()
    first = core == 0
    mine, other = mine_ref[...], other_ref[...]
    _, column = my_tile()
    left = jnp.where(column > 0, jnp.where(first, mine, other), 0.0)
    right = jnp.where(column < TCOLS - 1, jnp.where(first, other, mine), 0.0)
    rim = jnp.concatenate(
        [
            jnp.concatenate([left[:, :A], right[:, :A]], axis=1),
            jnp.concatenate([left[:, A:], right[:, A:]], axis=1),
        ],
        axis=0,
    )
    basis = basis_ref[...] + product(terms(rim), narrow(early_ref, "rims"))
    zero = jnp.zeros((K, K), F32)
    even = jnp.concatenate(
        [
            jnp.concatenate([basis[:K, :K], zero], axis=1),
            jnp.concatenate([zero, -basis[K:, K:]], axis=1),
        ],
        axis=0,
    )
    odd = jnp.concatenate(
        [
            jnp.concatenate([zero, -basis[:K, K:]], axis=1),
            jnp.concatenate([-basis[K:, :K], zero], axis=1),
        ],
        axis=0,
    )
    fold, fold_t = stored(table_ref, "fold"), stored(table_ref, "fold_t")
    for ref, part in ((real_ref, even), (imag_ref, odd)):
        plane = exact_right(exact_left(fold_t, part), fold)
        ref[0] = plane[:, :K]
        ref[1] = plane[:, K:]
    disc = disc_of(gain_ref[...])
    total_ref[...] = image_of((info_ref,), (0,), (real_ref, imag_ref), disc, table_ref, field_ref)


def others_kernel(
    near_ref, far_ref, gain_ref, table_ref, real_ref, imag_ref, before_ref, field_ref, total_ref
):
    info_refs = (None, near_ref, far_ref)
    disc = disc_of(gain_ref[...])
    total_ref[...] = before_ref[...] + image_of(
        info_refs, (1, 2, 3), (real_ref, imag_ref), disc, table_ref, field_ref
    )


def residual_kernel(mine_ref, other_ref, wanted_ref, field_ref, table_ref, residual_ref, energy_ref):
    bright = mine_ref[...] + other_ref[...]
    gram = narrow(table_ref, "gram")
    value = product(terms(product(gram, terms(bright))), gram)
    residual = value * (1.0 / (8 * SOURCES)) - wanted_ref[...]
    residual_ref[...] = residual
    lanes = lax.broadcasted_iota(jnp.int32, (8, K), 1)
    energies = jnp.zeros((8, K), F32)
    for source in range(SOURCES):
        real, imag = field_ref[source, :, :W], field_ref[source, :, W:]
        energy = jnp.sum(residual * (real * real + imag * imag))
        energies = jnp.where(lanes == source, energy, energies)
    energy_ref[...] = energies


def adjoint_kernel(
    chip,
    info_ref,
    residual_ref,
    field_ref,
    gain_ref,
    table_ref,
    early_ref,
    real_in,
    imag_in,
    *outs,
):
    info_refs = (info_ref,) * 3
    first_field = SOURCES if chip else 0
    coarse_t = narrow(table_ref, "coarse_t")
    last = chip == CHIPS - 1
    real_ref, imag_ref = outs[2:] if last else outs
    residual = residual_ref[...]
    disc = disc_of(gain_ref[...])
    real_ref[...] = jnp.zeros((2, W, K), F32) if chip == 0 else real_in[...]
    imag_ref[...] = jnp.zeros((2, W, K), F32) if chip == 0 else imag_in[...]
    pad = jnp.zeros((K, K), F32)
    first = chip * SOURCES
    halves = []
    for source in range(first, first + SOURCES):
        field = field_ref.at[source - first_field]
        scaled = jnp.concatenate([residual * field[:, :W], residual * field[:, W:]], axis=1)
        half = product(terms(scaled), coarse_t).T
        halves.append(jnp.concatenate([half[:K], half[K:]], axis=1))
    spec = product(terms(jnp.concatenate(halves, axis=0)), coarse_t)
    for source in range(first, first + SOURCES):
        row, column = window_starts(info_refs, source)
        scale = disc * (2.0 * weight_of(info_refs, source))
        own = spec[(source - first) * K : (source - first) * K + K]
        for ref, part in ((real_ref, own[:, :K]), (imag_ref, own[:, K:])):
            spread = pltpu.roll(jnp.concatenate([part * scale, pad], axis=1), column, 1)
            for side in range(2):
                ref[side, pl.ds(row, K), :] += spread[:, side * K : side * K + K]
    if not last:
        return
    fold, fold_t = stored(table_ref, "fold"), stored(table_ref, "fold_t")
    real, imag = (
        exact_left(fold, jnp.concatenate([ref[0], ref[1]], axis=1)) for ref in (real_ref, imag_ref)
    )
    cosines = exact_right(jnp.concatenate([real[:K], -imag[K:]], axis=0), fold_t[:, :K])
    sines = exact_right(jnp.concatenate([-imag[:K], -real[K:]], axis=0), fold_t[:, K:])
    spectrum = terms(jnp.concatenate([cosines, sines], axis=1))
    lines_ref, rim_ref = outs[:2]
    place, _ = my_place()
    lines = [early_ref[pl.ds(SPOTS["mid"][at][0] + 2 * place, 2)].reshape(K, W) for at in range(2)]
    lines_ref[...] = product(lines, spectrum)
    outer = [early_ref[SPOTS["rims"][at][0] + 1 - place // 2] for at in range(2)]
    rim_ref[...] = product(outer, spectrum)


def rim_kernel(lines_ref, rim_ref, energy_ref, out_ref):
    chip, core = my_place()
    row, _ = my_tile()
    rim = rim_ref[...]
    out_ref[:A] = lines_ref[:A] + jnp.where((chip == 0) & (row > 0), rim, 0.0)
    out_ref[A:K] = lines_ref[A:] + jnp.where((chip == 3) & (row < TROWS - 1), rim, 0.0)
    energy = energy_ref[...]
    out_ref[K:] = jnp.concatenate([jnp.where(core == at, energy, 0.0) for at in range(2)], axis=1)


def pixels_kernel(mine_ref, other_ref, table_ref, inner_ref, side_ref):
    _, core = my_place()
    first = core == 0
    lines = mine_ref[...] + other_ref[...]
    top, bottom = lines[:A], lines[A:K]
    table = stored(table_ref, "sides")
    table = jnp.where(first, table[:, :K], table[:, K:])
    table = (table[:, :A], table[:, A:])
    side_ref[:A] = jnp.concatenate([product(terms(top), table), product(terms(bottom), table)], axis=1)
    lanes = lax.broadcasted_iota(jnp.int32, (8, K), 1)
    side_ref[A:] = jnp.where(lanes < A, lines[K:, :K], pltpu.roll(lines[K:, K:], A, 1))
    own = jnp.where(first, top, bottom)
    inner_ref[...] = product(terms(own), wide(table_ref, "mid_t"))


def join_kernel(inner_ref, before_ref, mine_ref, other_ref, out_ref, energy_ref):
    _, core = my_place()
    first = core == 0
    mine, other = mine_ref[...], other_ref[...]
    _, column = my_tile()
    left = jnp.where(column > 0, jnp.where(first, other[:A, :A], mine[:A, A:]), 0.0)
    right = jnp.where(column < TCOLS - 1, jnp.where(first, mine[:A, :A], other[:A, A:]), 0.0)
    inner = inner_ref[...]
    pad = jnp.zeros((A, A), F32)
    out_ref[0, :, :K] = inner[:, :K] + jnp.concatenate([left, pad], axis=1)
    out_ref[0, :, K : PIX - K] = inner[:, K : PIX - K]
    out_ref[0, :, PIX - K :] = inner[:, PIX - K :] + jnp.concatenate([pad, right], axis=1)
    odd = lax.rem(column, 2)
    total = before_ref[A : A + 1] + jnp.where(core == odd, mine[A : A + 1], other[A : A + 1])
    total = pltpu.roll(total, core * A, 1) * (16.0 / (TROWS * TCOLS * PIX * PIX))
    energy_ref[...] = total[0, :SOURCES]


def swap_cores(value):
    return lax.ppermute(value, "src", [(at, at ^ 1) for at in range(8)])


def chip_swap(value, low):
    pairs = []
    for source in range(2 * CHIPS):
        for tile in range(TROWS * TCOLS):
            step = 1 if tile % 2 == low else -1
            partner = (source // 2 + step) % CHIPS * 2 + source % 2
            pairs.append((source * 32 + tile, partner * 32 + (tile ^ 1)))
    return lax.ppermute(value, BOTH, pairs)


def tile_move(value, shift_of):
    pairs = []
    for source in range(2 * CHIPS):
        down, right = shift_of(source)
        turns = shift_of(source ^ 1) == (-down, -right)
        for row in range(TROWS):
            for column in range(TCOLS):
                to_row, to_column = row + down, column + right
                inside = 0 <= to_row < TROWS and 0 <= to_column < TCOLS
                to = to_row % TROWS * TCOLS + to_column % TCOLS
                to = source * 32 + to if inside or not turns else (source ^ 1) * 32 + row * TCOLS + column
                pairs.append((source * 32 + row * TCOLS + column, to))
    return lax.ppermute(value, BOTH, pairs)


def line_move(value):
    pairs = []
    for source in range(2 * CHIPS):
        down = 1 if source // 2 % 2 == 0 else -1
        for tile in range(TROWS * TCOLS):
            to = tile + down * TCOLS
            inside = 0 <= to < TROWS * TCOLS
            pairs.append((source * 32 + tile, source * 32 + to if inside else (source ^ 2) * 32 + tile))
    return lax.ppermute(value, BOTH, pairs)


def tile_swap(value, step):
    def partner(at):
        y, x, z = at // TCOLS, at // 2 % 4, at % 2
        if step == 0:
            z = 1 - z
        elif step < 3:
            x = x ^ 1 if step == 1 else 3 - x
        else:
            y = y ^ 1 if step == 3 else 3 - y
        return y * TCOLS + x * 2 + z

    return lax.ppermute(value, "tile", [(at, partner(at)) for at in range(TROWS * TCOLS)])


def tied(*values):
    return lax.optimization_barrier(values)


def body(mask_tiles, target, pupil_gain, weights, freq_index):
    core = lax.axis_index("src") % 2
    edge = jnp.where(core == 0, mask_tiles[0, PIX - A :], mask_tiles[0, :A])
    mine = tile_move(edge, lambda source: (1, 0) if source % 2 == 0 else (-1, 0))
    rows, rim_table = call(own_kernel, [(W, PIX), (W, W)], [mask_tiles, EARLY], "own", 400_000_000, bf16=(1,))
    rows, weights, freq_index = tied(rows, weights, freq_index)
    mine, rows = tied(mine, rows)
    other = swap_cores(mine)
    lanes = lax.broadcasted_iota(jnp.int32, freq_index.shape, 2)
    info = jnp.where(lanes == 1, weights[:, None, None], freq_index.astype(F32))
    near = chip_swap(info, 1)
    rows, side = call(
        rows_kernel, [(W, PIX), (K, K)], [rows, mine, other, rim_table], "rows", 100_000_000
    )
    my_side = tile_move(side, lambda source: (0, 1) if source % 2 == 0 else (0, -1))
    (basis,) = call(columns_kernel, [(W, W)], [rows, EARLY, LATE], "columns", 200_000_000)
    far = chip_swap(jnp.concatenate([info, near]), 0)
    my_side, basis = tied(my_side, basis)
    other_side = swap_cores(my_side)
    own_field, total, real, imag = call(
        image_kernel,
        [(SOURCES, W, 2 * W), (W, W), (2, W, K), (2, W, K)],
        [info, basis, my_side, other_side, pupil_gain, EARLY, LATE],
        "image",
        2_000_000_000,
        smem=(0,),
    )
    field, mine = call(
        others_kernel,
        [((CHIPS - 1) * SOURCES, W, 2 * W), (W, W)],
        [near, far, pupil_gain, LATE, real, imag, total],
        "others",
        5_000_000_000,
        smem=(0, 1),
    )
    other = swap_cores(mine)
    (wanted,) = call(wanted_kernel, [(W, W)], [target, LATE], "wanted", 600_000_000)
    other, wanted = tied(other, wanted)
    residual, energies = call(
        residual_kernel, [(W, W), (8, K)], [mine, other, wanted, own_field, LATE], "residual", 300_000_000
    )
    plane = pltpu.VMEM((2, W, K), F32)
    planes = (jnp.zeros((8, K), F32),) * 2
    for chip in range(CHIPS):
        arrived = tile_swap(energies, (4, 2, 3, 1)[chip])
        last = chip == CHIPS - 1
        outs = call(
            functools.partial(adjoint_kernel, chip),
            [(K, W), (A, W)] if last else [(2, W, K), (2, W, K)],
            [(info, near, far, far)[chip], residual, field if chip else own_field, pupil_gain, LATE, EARLY, *planes],
            "adjoint",
            1_500_000_000,
            scratch=(plane, plane) if last else (),
            smem=(0,),
        )
        planes = outs
        *planes, energies = tied(*planes, energies + arrived)
    lines, rim = planes
    from_rows = line_move(rim)
    (mine,) = call(rim_kernel, [(K + 8, W)], [lines, from_rows, energies], "rim", K * K)
    other = swap_cores(mine)
    inner, side = call(
        pixels_kernel,
        [(A, PIX), (A + 8, K)],
        [mine, other, EARLY],
        "pixels",
        100_000_000,
    )
    my_side = tile_move(side, lambda source: (0, -1) if source % 2 == 0 else (0, 1))
    other_side = swap_cores(my_side)
    mask_grad, weight_grad = call(
        join_kernel, [(1, A, PIX), (SOURCES,)], [inner, side, my_side, other_side], "join", A * PIX
    )
    return mask_grad, weight_grad


def solution(mesh):
    placed = (P("tile", None, None), P("tile", None, None), P(), P("src"), P("src", None, None))
    return jax.shard_map(
        body,
        mesh=mesh,
        in_specs=placed,
        out_specs=(P("tile", "src", None), P("src")),
        check_vma=False,
    )
```

```python
import functools
import math

import jax
import jax.numpy as jnp
import ml_dtypes
import numpy as np
from jax import lax
from jax.experimental import pallas as pl
from jax.experimental.pallas import tpu as pltpu
from jax.sharding import PartitionSpec as P

A = 64
TROWS = 4
TCOLS = 8
PIX = 512
N = PIX + 2 * A
K = 128
W = 256
SOURCES = 4
CHIPS = 4
BF = jnp.bfloat16
F32 = jnp.float32
BOTH = ("src", "tile")


def two_terms(table):
    first = table.astype(np.float32).astype(ml_dtypes.bfloat16)
    rest = (table - first.astype(np.float64)).astype(np.float32)
    return np.stack([first, rest.astype(ml_dtypes.bfloat16)])


def real_basis():
    angles = 2.0 * np.pi / N * np.mod(np.outer(np.arange(N), np.arange(K)), N)
    return np.concatenate([np.cos(angles), np.sin(angles)], axis=1) / math.sqrt(N)


def fold_table():
    ranks = np.arange(W) - K
    parts = np.arange(K)
    same = np.abs(ranks)[None, :] == parts[:, None]
    return np.concatenate([same * 1.0, same * np.sign(ranks)[None, :]], axis=0)


def coarse_table():
    ranks = np.arange(K) - K // 2
    angles = 2.0 * np.pi / W * np.mod(np.outer(ranks, np.arange(W)), W)
    down_real, down_imag = np.cos(angles) / math.sqrt(K), np.sin(angles) / math.sqrt(K)
    return np.block([[down_real, down_imag], [-down_imag, down_real]])


def interpolation():
    ranks = np.arange(1, K)
    shift = (np.arange(PIX) + A)[:, None] / N - np.arange(W)[None, :] / W
    return (1.0 + 2.0 * np.cos(2.0 * np.pi * shift[..., None] * ranks).sum(-1)) / W


ROWS = 64


def packed(entries):
    spots, pieces, at = {}, [], 0
    for name, tables in entries.items():
        spots[name] = []
        for table in tables:
            count = table.shape[0] // ROWS
            spots[name].append((at, count))
            pieces.append(table.reshape(count, ROWS, W))
            at += count
    return np.concatenate(pieces), spots


def two_halves(table):
    return [half for term in two_terms(table) for half in (term[:, :W], term[:, W:])]


def make_tables():
    basis = real_basis()
    coarse = coarse_table()
    spread = interpolation()
    fold = fold_table().astype(ml_dtypes.bfloat16)
    middle = basis[A : N - A]
    rims = np.concatenate([basis[:A], basis[N - A :]])
    sides = [two_terms(basis[:A].T), two_terms(basis[N - A :].T)]
    early = packed(
        {
            "mid": two_terms(middle),
            "mid_t": two_halves(middle.T),
            "rims": two_terms(rims),
            "rims_t": [np.concatenate(list(two_terms(rims.T)), axis=1)],
            "sides": [np.concatenate([term for pair in sides for term in pair], axis=1)],
        }
    )
    late = packed(
        {
            "coarse": two_halves(coarse),
            "coarse_t": two_terms(coarse.T),
            "fold": [fold],
            "fold_t": [np.ascontiguousarray(fold.T)],
            "spread": two_terms(spread),
            "spread_t": two_halves(spread.T),
            "gram": two_terms(spread.T @ spread),
        }
    )
    return early, late


(EARLY, EARLY_AT), (LATE, LATE_AT) = make_tables()
SPOTS = EARLY_AT | LATE_AT


def stored(ref, name, at=0):
    start, count = SPOTS[name][at]
    return ref[start : start + count].reshape(count * ROWS, W)


def narrow(ref, name):
    return stored(ref, name, 0), stored(ref, name, 1)


def wide(ref, name):
    return tuple(
        jnp.concatenate([stored(ref, name, at), stored(ref, name, at + 1)], axis=1) for at in (0, 2)
    )


def terms(value):
    first = value.astype(BF)
    return first, (value - first.astype(F32)).astype(BF)


def dot(first_op, second_op):
    return jnp.dot(first_op, second_op, preferred_element_type=F32)


def product(first_op, second_op):
    first_hi, first_lo = first_op
    second_hi, second_lo = second_op
    return dot(
        jnp.concatenate([first_hi, first_hi, first_lo], axis=1),
        jnp.concatenate([second_hi, second_lo, second_hi], axis=0),
    )


def exact_left(table, value):
    high, low = terms(value)
    return dot(table, high) + dot(table, low)


def exact_right(value, table):
    high, low = terms(value)
    return dot(high, table) + dot(low, table)


def call(kernel, outs, ins, name, flops, scratch=(), smem=(), bf16=(), grant=20):
    specs = [
        pl.BlockSpec(memory_space=pltpu.SMEM if at in smem else pltpu.VMEM) for at in range(len(ins))
    ]
    shapes = [jax.ShapeDtypeStruct(shape, BF if at in bf16 else F32) for at, shape in enumerate(outs)]
    moved = 4 * sum(math.prod(shape) for shape in outs) + sum(one.size * one.dtype.itemsize for one in ins)
    return pl.pallas_call(
        kernel,
        out_shape=shapes,
        in_specs=specs,
        out_specs=[pl.BlockSpec(memory_space=pltpu.VMEM) for _ in outs],
        scratch_shapes=list(scratch),
        compiler_params=pltpu.CompilerParams(vmem_limit_bytes=40 * 1024 * 1024),
        cost_estimate=pl.CostEstimate(flops=flops, bytes_accessed=moved, transcendentals=0),
        name=name,
    )(*ins)


def my_place():
    group = lax.axis_index("src")
    return group // 2, group % 2


def my_tile():
    tile = lax.axis_index("tile")
    return tile // TCOLS, lax.rem(tile, TCOLS)


def own_kernel(tile_ref, table_ref, rows_ref, rims_ref):
    rows_ref[...] = product(wide(table_ref, "mid_t"), terms(tile_ref[0]))
    rims_ref[...] = stored(table_ref, "rims_t")


def wanted_kernel(target_ref, table_ref, wanted_ref):
    upper = product(terms(target_ref[0]), narrow(table_ref, "spread"))
    wanted_ref[...] = product(wide(table_ref, "spread_t"), terms(upper)).T


def rows_kernel(rows_ref, mine_ref, other_ref, table_ref, all_ref, side_ref):
    _, core = my_place()
    first = core == 0
    mine, other = mine_ref[...], other_ref[...]
    row, _ = my_tile()
    upper = jnp.where(row > 0, jnp.where(first, mine, other), 0.0)
    lower = jnp.where(row < TROWS - 1, jnp.where(first, other, mine), 0.0)
    rim = jnp.concatenate([upper, lower], axis=0)
    table = table_ref[...]
    rows = rows_ref[...] + product((table[:, :K], table[:, K:]), terms(rim))
    all_ref[...] = rows
    side = jnp.where(first, rows[:, PIX - A :], rows[:, :A])
    side_ref[...] = jnp.concatenate([side[:K], side[K:]], axis=1)


def columns_kernel(rows_ref, table_ref, _, basis_ref):
    basis_ref[...] = product(terms(rows_ref[...]), narrow(table_ref, "mid"))


def disc_of(gain):
    rows = lax.broadcasted_iota(jnp.int32, (K, K), 0) - K // 2
    columns = lax.broadcasted_iota(jnp.int32, (K, K), 1) - K // 2
    return jnp.where(rows * rows + columns * columns <= (K // 2) ** 2, gain, 0.0)


def window_starts(info_refs, source):
    ref = info_refs[min(source // SOURCES, 2)]
    at = source % SOURCES + (SOURCES if source // SOURCES == 3 else 0)

    def start(coordinate):
        index = ref[at, coordinate, 0].astype(jnp.int32)
        return jnp.clip(lax.rem(index + K, N), 0, K)

    return start(0), start(1)


def weight_of(info_refs, source):
    ref = info_refs[min(source // SOURCES, 2)]
    return ref[source % SOURCES + (SOURCES if source // SOURCES == 3 else 0), 0, 1]


def image_of(info_refs, chips, planes, disc, table_ref, field_ref):
    coarse = wide(table_ref, "coarse")
    total = jnp.zeros((W, W), F32)
    for chip in chips:
        specs = []
        for source in range(chip * SOURCES, chip * SOURCES + SOURCES):
            row, column = window_starts(info_refs, source)

            def window(ref):
                rows = jnp.concatenate([ref[0, pl.ds(row, K), :], ref[1, pl.ds(row, K), :]], axis=1)
                return pltpu.roll(rows, lax.rem(W - column, W), 1)[:, :K] * disc

            specs.append(jnp.concatenate([window(ref) for ref in planes], axis=1))
        stacked = product(terms(jnp.concatenate(specs, axis=0)), coarse)
        for at in range(SOURCES):
            half = stacked[at * K : at * K + K].T
            half = jnp.concatenate([half[:W], half[W:]], axis=1)
            field = product(terms(half), coarse)
            field_ref[(chip - chips[0]) * SOURCES + at] = field
            real, imag = field[:, :W], field[:, W:]
            weight = weight_of(info_refs, chip * SOURCES + at)
            total = total + weight * (real * real + imag * imag)
    return total


def image_kernel(
    info_ref,
    basis_ref,
    mine_ref,
    other_ref,
    gain_ref,
    early_ref,
    table_ref,
    field_ref,
    total_ref,
    real_ref,
    imag_ref,
):
    _, core = my_place()
    first = core == 0
    mine, other = mine_ref[...], other_ref[...]
    _, column = my_tile()
    left = jnp.where(column > 0, jnp.where(first, mine, other), 0.0)
    right = jnp.where(column < TCOLS - 1, jnp.where(first, other, mine), 0.0)
    rim = jnp.concatenate(
        [
            jnp.concatenate([left[:, :A], right[:, :A]], axis=1),
            jnp.concatenate([left[:, A:], right[:, A:]], axis=1),
        ],
        axis=0,
    )
    basis = basis_ref[...] + product(terms(rim), narrow(early_ref, "rims"))
    zero = jnp.zeros((K, K), F32)
    even = jnp.concatenate(
        [
            jnp.concatenate([basis[:K, :K], zero], axis=1),
            jnp.concatenate([zero, -basis[K:, K:]], axis=1),
        ],
        axis=0,
    )
    odd = jnp.concatenate(
        [
            jnp.concatenate([zero, -basis[:K, K:]], axis=1),
            jnp.concatenate([-basis[K:, :K], zero], axis=1),
        ],
        axis=0,
    )
    fold, fold_t = stored(table_ref, "fold"), stored(table_ref, "fold_t")
    for ref, part in ((real_ref, even), (imag_ref, odd)):
        plane = exact_right(exact_left(fold_t, part), fold)
        ref[0] = plane[:, :K]
        ref[1] = plane[:, K:]
    disc = disc_of(gain_ref[...])
    total_ref[...] = image_of((info_ref,), (0,), (real_ref, imag_ref), disc, table_ref, field_ref)


def others_kernel(
    near_ref, far_ref, gain_ref, table_ref, real_ref, imag_ref, before_ref, field_ref, total_ref
):
    info_refs = (None, near_ref, far_ref)
    disc = disc_of(gain_ref[...])
    total_ref[...] = before_ref[...] + image_of(
        info_refs, (1, 2, 3), (real_ref, imag_ref), disc, table_ref, field_ref
    )


def residual_kernel(mine_ref, other_ref, wanted_ref, field_ref, table_ref, residual_ref, energy_ref):
    bright = mine_ref[...] + other_ref[...]
    gram = narrow(table_ref, "gram")
    value = product(terms(product(gram, terms(bright))), gram)
    residual = value * (1.0 / (8 * SOURCES)) - wanted_ref[...]
    residual_ref[...] = residual
    lanes = lax.broadcasted_iota(jnp.int32, (8, K), 1)
    energies = jnp.zeros((8, K), F32)
    for source in range(SOURCES):
        real, imag = field_ref[source, :, :W], field_ref[source, :, W:]
        energy = jnp.sum(residual * (real * real + imag * imag))
        energies = jnp.where(lanes == source, energy, energies)
    energy_ref[...] = energies


def adjoint_kernel(
    chip,
    info_ref,
    residual_ref,
    field_ref,
    gain_ref,
    table_ref,
    early_ref,
    real_in,
    imag_in,
    *outs,
):
    info_refs = (info_ref,) * 3
    first_field = SOURCES if chip else 0
    coarse_t = narrow(table_ref, "coarse_t")
    last = chip == CHIPS - 1
    real_ref, imag_ref = outs[2:] if last else outs
    residual = residual_ref[...]
    disc = disc_of(gain_ref[...])
    real_ref[...] = jnp.zeros((2, W, K), F32) if chip == 0 else real_in[...]
    imag_ref[...] = jnp.zeros((2, W, K), F32) if chip == 0 else imag_in[...]
    pad = jnp.zeros((K, K), F32)
    first = chip * SOURCES
    halves = []
    for source in range(first, first + SOURCES):
        field = field_ref.at[source - first_field]
        scaled = jnp.concatenate([residual * field[:, :W], residual * field[:, W:]], axis=1)
        half = product(terms(scaled), coarse_t).T
        halves.append(jnp.concatenate([half[:K], half[K:]], axis=1))
    spec = product(terms(jnp.concatenate(halves, axis=0)), coarse_t)
    for source in range(first, first + SOURCES):
        row, column = window_starts(info_refs, source)
        scale = disc * (2.0 * weight_of(info_refs, source))
        own = spec[(source - first) * K : (source - first) * K + K]
        for ref, part in ((real_ref, own[:, :K]), (imag_ref, own[:, K:])):
            spread = pltpu.roll(jnp.concatenate([part * scale, pad], axis=1), column, 1)
            for side in range(2):
                ref[side, pl.ds(row, K), :] += spread[:, side * K : side * K + K]
    if not last:
        return
    fold, fold_t = stored(table_ref, "fold"), stored(table_ref, "fold_t")
    real, imag = (
        exact_left(fold, jnp.concatenate([ref[0], ref[1]], axis=1)) for ref in (real_ref, imag_ref)
    )
    cosines = exact_right(jnp.concatenate([real[:K], -imag[K:]], axis=0), fold_t[:, :K])
    sines = exact_right(jnp.concatenate([-imag[:K], -real[K:]], axis=0), fold_t[:, K:])
    spectrum = terms(jnp.concatenate([cosines, sines], axis=1))
    lines_ref, rim_ref = outs[:2]
    place, _ = my_place()
    lines = [early_ref[pl.ds(SPOTS["mid"][at][0] + 2 * place, 2)].reshape(K, W) for at in range(2)]
    lines_ref[...] = product(lines, spectrum)
    outer = [early_ref[SPOTS["rims"][at][0] + 1 - place // 2] for at in range(2)]
    rim_ref[...] = product(outer, spectrum)


def rim_kernel(lines_ref, rim_ref, energy_ref, out_ref):
    chip, core = my_place()
    row, _ = my_tile()
    rim = rim_ref[...]
    out_ref[:A] = lines_ref[:A] + jnp.where((chip == 0) & (row > 0), rim, 0.0)
    out_ref[A:K] = lines_ref[A:] + jnp.where((chip == 3) & (row < TROWS - 1), rim, 0.0)
    energy = energy_ref[...]
    out_ref[K:] = jnp.concatenate([jnp.where(core == at, energy, 0.0) for at in range(2)], axis=1)


def pixels_kernel(mine_ref, other_ref, table_ref, inner_ref, side_ref):
    _, core = my_place()
    first = core == 0
    lines = mine_ref[...] + other_ref[...]
    top, bottom = lines[:A], lines[A:K]
    table = stored(table_ref, "sides")
    table = jnp.where(first, table[:, :K], table[:, K:])
    table = (table[:, :A], table[:, A:])
    side_ref[:A] = jnp.concatenate([product(terms(top), table), product(terms(bottom), table)], axis=1)
    lanes = lax.broadcasted_iota(jnp.int32, (8, K), 1)
    side_ref[A:] = jnp.where(lanes < A, lines[K:, :K], pltpu.roll(lines[K:, K:], A, 1))
    own = jnp.where(first, top, bottom)
    inner_ref[...] = product(terms(own), wide(table_ref, "mid_t"))


def join_kernel(inner_ref, before_ref, mine_ref, other_ref, out_ref, energy_ref):
    _, core = my_place()
    first = core == 0
    mine, other = mine_ref[...], other_ref[...]
    _, column = my_tile()
    left = jnp.where(column > 0, jnp.where(first, other[:A, :A], mine[:A, A:]), 0.0)
    right = jnp.where(column < TCOLS - 1, jnp.where(first, mine[:A, :A], other[:A, A:]), 0.0)
    inner = inner_ref[...]
    pad = jnp.zeros((A, A), F32)
    out_ref[0, :, :K] = inner[:, :K] + jnp.concatenate([left, pad], axis=1)
    out_ref[0, :, K : PIX - K] = inner[:, K : PIX - K]
    out_ref[0, :, PIX - K :] = inner[:, PIX - K :] + jnp.concatenate([pad, right], axis=1)
    odd = lax.rem(column, 2)
    total = before_ref[A : A + 1] + jnp.where(core == odd, mine[A : A + 1], other[A : A + 1])
    total = pltpu.roll(total, core * A, 1) * (16.0 / (TROWS * TCOLS * PIX * PIX))
    energy_ref[...] = total[0, :SOURCES]


def swap_cores(value):
    return lax.ppermute(value, "src", [(at, at ^ 1) for at in range(8)])


def chip_swap(value, low):
    pairs = []
    for source in range(2 * CHIPS):
        for tile in range(TROWS * TCOLS):
            step = 1 if tile % 2 == low else -1
            partner = (source // 2 + step) % CHIPS * 2 + source % 2
            pairs.append((source * 32 + tile, partner * 32 + (tile ^ 1)))
    return lax.ppermute(value, BOTH, pairs)


def tile_move(value, shift_of):
    pairs = []
    for source in range(2 * CHIPS):
        down, right = shift_of(source)
        turns = shift_of(source ^ 1) == (-down, -right)
        for row in range(TROWS):
            for column in range(TCOLS):
                to_row, to_column = row + down, column + right
                inside = 0 <= to_row < TROWS and 0 <= to_column < TCOLS
                to = to_row % TROWS * TCOLS + to_column % TCOLS
                to = source * 32 + to if inside or not turns else (source ^ 1) * 32 + row * TCOLS + column
                pairs.append((source * 32 + row * TCOLS + column, to))
    return lax.ppermute(value, BOTH, pairs)


def tile_swap(value, step):
    def partner(at):
        y, x, z = at // TCOLS, at // 2 % 4, at % 2
        if step == 0:
            z = 1 - z
        elif step < 3:
            x = x ^ 1 if step == 1 else 3 - x
        else:
            y = y ^ 1 if step == 3 else 3 - y
        return y * TCOLS + x * 2 + z

    return lax.ppermute(value, "tile", [(at, partner(at)) for at in range(TROWS * TCOLS)])


def tied(*values):
    return lax.optimization_barrier(values)


def body(mask_tiles, target, pupil_gain, weights, freq_index):
    core = lax.axis_index("src") % 2
    edge = jnp.where(core == 0, mask_tiles[0, PIX - A :], mask_tiles[0, :A])
    mine = tile_move(edge, lambda source: (1, 0) if source % 2 == 0 else (-1, 0))
    rows, rim_table = call(own_kernel, [(W, PIX), (W, W)], [mask_tiles, EARLY], "own", 400_000_000, bf16=(1,))
    rows, weights, freq_index = tied(rows, weights, freq_index)
    mine, rows = tied(mine, rows)
    other = swap_cores(mine)
    lanes = lax.broadcasted_iota(jnp.int32, freq_index.shape, 2)
    info = jnp.where(lanes == 1, weights[:, None, None], freq_index.astype(F32))
    near = chip_swap(info, 1)
    rows, side = call(
        rows_kernel, [(W, PIX), (K, K)], [rows, mine, other, rim_table], "rows", 100_000_000
    )
    my_side = tile_move(side, lambda source: (0, 1) if source % 2 == 0 else (0, -1))
    (basis,) = call(columns_kernel, [(W, W)], [rows, EARLY, LATE], "columns", 200_000_000)
    far = chip_swap(jnp.concatenate([info, near]), 0)
    my_side, basis = tied(my_side, basis)
    other_side = swap_cores(my_side)
    own_field, total, real, imag = call(
        image_kernel,
        [(SOURCES, W, 2 * W), (W, W), (2, W, K), (2, W, K)],
        [info, basis, my_side, other_side, pupil_gain, EARLY, LATE],
        "image",
        2_000_000_000,
        smem=(0,),
    )
    field, mine = call(
        others_kernel,
        [((CHIPS - 1) * SOURCES, W, 2 * W), (W, W)],
        [near, far, pupil_gain, LATE, real, imag, total],
        "others",
        5_000_000_000,
        smem=(0, 1),
    )
    other = swap_cores(mine)
    (wanted,) = call(wanted_kernel, [(W, W)], [target, LATE], "wanted", 600_000_000)
    other, wanted = tied(other, wanted)
    residual, energies = call(
        residual_kernel, [(W, W), (8, K)], [mine, other, wanted, own_field, LATE], "residual", 300_000_000
    )
    plane = pltpu.VMEM((2, W, K), F32)
    planes = (jnp.zeros((8, K), F32),) * 2
    for chip in range(CHIPS):
        arrived = tile_swap(energies, (4, 2, 3, 1)[chip])
        last = chip == CHIPS - 1
        outs = call(
            functools.partial(adjoint_kernel, chip),
            [(K, W), (A, W)] if last else [(2, W, K), (2, W, K)],
            [(info, near, far, far)[chip], residual, field if chip else own_field, pupil_gain, LATE, EARLY, *planes],
            "adjoint",
            1_500_000_000,
            scratch=(plane, plane) if last else (),
            smem=(0,),
        )
        planes = outs
        *planes, energies = tied(*planes, energies + arrived)
    lines, rim = planes
    from_rows = tile_move(rim, lambda source: (1, 0) if source < CHIPS else (-1, 0))
    (mine,) = call(rim_kernel, [(K + 8, W)], [lines, from_rows, energies], "rim", K * K)
    other = swap_cores(mine)
    inner, side = call(
        pixels_kernel,
        [(A, PIX), (A + 8, K)],
        [mine, other, EARLY],
        "pixels",
        100_000_000,
    )
    my_side = tile_move(side, lambda source: (0, -1) if source % 2 == 0 else (0, 1))
    other_side = swap_cores(my_side)
    mask_grad, weight_grad = call(
        join_kernel, [(1, A, PIX), (SOURCES,)], [inner, side, my_side, other_side], "join", A * PIX
    )
    return mask_grad, weight_grad


def solution(mesh):
    placed = (P("tile", None, None), P("tile", None, None), P(), P("src"), P("src", None, None))
    return jax.shard_map(
        body,
        mesh=mesh,
        in_specs=placed,
        out_specs=(P("tile", "src", None), P("src")),
        check_vma=False,
    )
```

```python
import functools
import math

import jax
import jax.numpy as jnp
import ml_dtypes
import numpy as np
from jax import lax
from jax.experimental import pallas as pl
from jax.experimental.pallas import tpu as pltpu
from jax.sharding import PartitionSpec as P

A = 64
TROWS = 4
TCOLS = 8
PIX = 512
N = PIX + 2 * A
K = 128
W = 256
SOURCES = 4
CHIPS = 4
BF = jnp.bfloat16
F32 = jnp.float32
BOTH = ("src", "tile")


def two_terms(table):
    first = table.astype(np.float32).astype(ml_dtypes.bfloat16)
    rest = (table - first.astype(np.float64)).astype(np.float32)
    return np.stack([first, rest.astype(ml_dtypes.bfloat16)])


def real_basis():
    angles = 2.0 * np.pi / N * np.mod(np.outer(np.arange(N), np.arange(K)), N)
    return np.concatenate([np.cos(angles), np.sin(angles)], axis=1) / math.sqrt(N)


def fold_table():
    ranks = np.arange(W) - K
    parts = np.arange(K)
    same = np.abs(ranks)[None, :] == parts[:, None]
    return np.concatenate([same * 1.0, same * np.sign(ranks)[None, :]], axis=0)


def coarse_table():
    ranks = np.arange(K) - K // 2
    angles = 2.0 * np.pi / W * np.mod(np.outer(ranks, np.arange(W)), W)
    down_real, down_imag = np.cos(angles) / math.sqrt(K), np.sin(angles) / math.sqrt(K)
    return np.block([[down_real, down_imag], [-down_imag, down_real]])


def interpolation():
    ranks = np.arange(1, K)
    shift = (np.arange(PIX) + A)[:, None] / N - np.arange(W)[None, :] / W
    return (1.0 + 2.0 * np.cos(2.0 * np.pi * shift[..., None] * ranks).sum(-1)) / W


ROWS = 64


def packed(entries):
    spots, pieces, at = {}, [], 0
    for name, tables in entries.items():
        spots[name] = []
        for table in tables:
            count = table.shape[0] // ROWS
            spots[name].append((at, count))
            pieces.append(table.reshape(count, ROWS, W))
            at += count
    return np.concatenate(pieces), spots


def two_halves(table):
    return [half for term in two_terms(table) for half in (term[:, :W], term[:, W:])]


def make_tables():
    basis = real_basis()
    coarse = coarse_table()
    spread = interpolation()
    fold = fold_table().astype(ml_dtypes.bfloat16)
    middle = basis[A : N - A]
    rims = np.concatenate([basis[:A], basis[N - A :]])
    sides = [two_terms(basis[:A].T), two_terms(basis[N - A :].T)]
    early = packed(
        {
            "mid": two_terms(middle),
            "mid_t": two_halves(middle.T),
            "rims": two_terms(rims),
            "rims_t": [np.concatenate(list(two_terms(rims.T)), axis=1)],
            "sides": [np.concatenate([term for pair in sides for term in pair], axis=1)],
        }
    )
    late = packed(
        {
            "coarse": two_halves(coarse),
            "coarse_t": two_terms(coarse.T),
            "fold": [fold],
            "fold_t": [np.ascontiguousarray(fold.T)],
            "spread": two_terms(spread),
            "spread_t": two_halves(spread.T),
            "gram": two_terms(spread.T @ spread),
        }
    )
    return early, late


(EARLY, EARLY_AT), (LATE, LATE_AT) = make_tables()
SPOTS = EARLY_AT | LATE_AT


def stored(ref, name, at=0):
    start, count = SPOTS[name][at]
    return ref[start : start + count].reshape(count * ROWS, W)


def narrow(ref, name):
    return stored(ref, name, 0), stored(ref, name, 1)


def wide(ref, name):
    return tuple(
        jnp.concatenate([stored(ref, name, at), stored(ref, name, at + 1)], axis=1) for at in (0, 2)
    )


def terms(value):
    first = value.astype(BF)
    return first, (value - first.astype(F32)).astype(BF)


def dot(first_op, second_op):
    return jnp.dot(first_op, second_op, preferred_element_type=F32)


def product(first_op, second_op):
    first_hi, first_lo = first_op
    second_hi, second_lo = second_op
    return dot(
        jnp.concatenate([first_hi, first_hi, first_lo], axis=1),
        jnp.concatenate([second_hi, second_lo, second_hi], axis=0),
    )


def exact_left(table, value):
    high, low = terms(value)
    return dot(table, high) + dot(table, low)


def exact_right(value, table):
    high, low = terms(value)
    return dot(high, table) + dot(low, table)


def call(kernel, outs, ins, name, flops, scratch=(), smem=(), bf16=(), grant=20):
    specs = [
        pl.BlockSpec(memory_space=pltpu.SMEM if at in smem else pltpu.VMEM) for at in range(len(ins))
    ]
    shapes = [jax.ShapeDtypeStruct(shape, BF if at in bf16 else F32) for at, shape in enumerate(outs)]
    moved = 4 * sum(math.prod(shape) for shape in outs) + sum(one.size * one.dtype.itemsize for one in ins)
    return pl.pallas_call(
        kernel,
        out_shape=shapes,
        in_specs=specs,
        out_specs=[pl.BlockSpec(memory_space=pltpu.VMEM) for _ in outs],
        scratch_shapes=list(scratch),
        compiler_params=pltpu.CompilerParams(vmem_limit_bytes=40 * 1024 * 1024),
        cost_estimate=pl.CostEstimate(flops=flops, bytes_accessed=moved, transcendentals=0),
        name=name,
    )(*ins)


def my_place():
    group = lax.axis_index("src")
    return group // 2, group % 2


def my_tile():
    tile = lax.axis_index("tile")
    return tile // TCOLS, lax.rem(tile, TCOLS)


def own_kernel(tile_ref, table_ref, rows_ref, rims_ref):
    rows_ref[...] = product(wide(table_ref, "mid_t"), terms(tile_ref[0]))
    rims_ref[...] = stored(table_ref, "rims_t")


def wanted_kernel(target_ref, table_ref, wanted_ref):
    upper = product(terms(target_ref[0]), narrow(table_ref, "spread"))
    wanted_ref[...] = product(wide(table_ref, "spread_t"), terms(upper)).T


def rows_kernel(rows_ref, mine_ref, other_ref, table_ref, all_ref, side_ref):
    _, core = my_place()
    first = core == 0
    mine, other = mine_ref[...], other_ref[...]
    row, _ = my_tile()
    upper = jnp.where(row > 0, jnp.where(first, mine, other), 0.0)
    lower = jnp.where(row < TROWS - 1, jnp.where(first, other, mine), 0.0)
    rim = jnp.concatenate([upper, lower], axis=0)
    table = table_ref[...]
    rows = rows_ref[...] + product((table[:, :K], table[:, K:]), terms(rim))
    all_ref[...] = rows
    side = jnp.where(first, rows[:, PIX - A :], rows[:, :A])
    side_ref[...] = jnp.concatenate([side[:K], side[K:]], axis=1)


def columns_kernel(rows_ref, table_ref, _, basis_ref):
    basis_ref[...] = product(terms(rows_ref[...]), narrow(table_ref, "mid"))


def disc_of(gain):
    rows = lax.broadcasted_iota(jnp.int32, (K, K), 0) - K // 2
    columns = lax.broadcasted_iota(jnp.int32, (K, K), 1) - K // 2
    return jnp.where(rows * rows + columns * columns <= (K // 2) ** 2, gain, 0.0)


def window_starts(info_refs, source):
    ref = info_refs[min(source // SOURCES, 2)]
    at = source % SOURCES + (SOURCES if source // SOURCES == 3 else 0)

    def start(coordinate):
        index = ref[at, coordinate, 0].astype(jnp.int32)
        return jnp.clip(lax.rem(index + K, N), 0, K)

    return start(0), start(1)


def weight_of(info_refs, source):
    ref = info_refs[min(source // SOURCES, 2)]
    return ref[source % SOURCES + (SOURCES if source // SOURCES == 3 else 0), 0, 1]


def image_of(info_refs, chips, planes, disc, table_ref, field_ref):
    coarse = wide(table_ref, "coarse")
    total = jnp.zeros((W, W), F32)
    for chip in chips:
        specs = []
        for source in range(chip * SOURCES, chip * SOURCES + SOURCES):
            row, column = window_starts(info_refs, source)

            def window(ref):
                rows = jnp.concatenate([ref[0, pl.ds(row, K), :], ref[1, pl.ds(row, K), :]], axis=1)
                return pltpu.roll(rows, lax.rem(W - column, W), 1)[:, :K] * disc

            specs.append(jnp.concatenate([window(ref) for ref in planes], axis=1))
        stacked = product(terms(jnp.concatenate(specs, axis=0)), coarse)
        for at in range(SOURCES):
            half = stacked[at * K : at * K + K].T
            half = jnp.concatenate([half[:W], half[W:]], axis=1)
            field = product(terms(half), coarse)
            field_ref[(chip - chips[0]) * SOURCES + at] = field
            real, imag = field[:, :W], field[:, W:]
            weight = weight_of(info_refs, chip * SOURCES + at)
            total = total + weight * (real * real + imag * imag)
    return total


def image_kernel(
    info_ref,
    basis_ref,
    mine_ref,
    other_ref,
    gain_ref,
    early_ref,
    table_ref,
    field_ref,
    total_ref,
    real_ref,
    imag_ref,
):
    _, core = my_place()
    first = core == 0
    mine, other = mine_ref[...], other_ref[...]
    _, column = my_tile()
    left = jnp.where(column > 0, jnp.where(first, mine, other), 0.0)
    right = jnp.where(column < TCOLS - 1, jnp.where(first, other, mine), 0.0)
    rim = jnp.concatenate(
        [
            jnp.concatenate([left[:, :A], right[:, :A]], axis=1),
            jnp.concatenate([left[:, A:], right[:, A:]], axis=1),
        ],
        axis=0,
    )
    basis = basis_ref[...] + product(terms(rim), narrow(early_ref, "rims"))
    zero = jnp.zeros((K, K), F32)
    even = jnp.concatenate(
        [
            jnp.concatenate([basis[:K, :K], zero], axis=1),
            jnp.concatenate([zero, -basis[K:, K:]], axis=1),
        ],
        axis=0,
    )
    odd = jnp.concatenate(
        [
            jnp.concatenate([zero, -basis[:K, K:]], axis=1),
            jnp.concatenate([-basis[K:, :K], zero], axis=1),
        ],
        axis=0,
    )
    fold, fold_t = stored(table_ref, "fold"), stored(table_ref, "fold_t")
    for ref, part in ((real_ref, even), (imag_ref, odd)):
        plane = exact_right(exact_left(fold_t, part), fold)
        ref[0] = plane[:, :K]
        ref[1] = plane[:, K:]
    disc = disc_of(gain_ref[...])
    total_ref[...] = image_of((info_ref,), (0,), (real_ref, imag_ref), disc, table_ref, field_ref)


def others_kernel(
    near_ref, far_ref, gain_ref, table_ref, real_ref, imag_ref, before_ref, field_ref, total_ref
):
    info_refs = (None, near_ref, far_ref)
    disc = disc_of(gain_ref[...])
    total_ref[...] = before_ref[...] + image_of(
        info_refs, (1, 2, 3), (real_ref, imag_ref), disc, table_ref, field_ref
    )


def residual_kernel(mine_ref, other_ref, wanted_ref, field_ref, table_ref, residual_ref, energy_ref):
    bright = mine_ref[...] + other_ref[...]
    gram = narrow(table_ref, "gram")
    value = product(terms(product(gram, terms(bright))), gram)
    residual = value * (1.0 / (8 * SOURCES)) - wanted_ref[...]
    residual_ref[...] = residual
    lanes = lax.broadcasted_iota(jnp.int32, (8, K), 1)
    energies = jnp.zeros((8, K), F32)
    for source in range(SOURCES):
        real, imag = field_ref[source, :, :W], field_ref[source, :, W:]
        energy = jnp.sum(residual * (real * real + imag * imag))
        energies = jnp.where(lanes == source, energy, energies)
    energy_ref[...] = energies


def adjoint_kernel(
    chip,
    info_ref,
    residual_ref,
    field_ref,
    gain_ref,
    table_ref,
    early_ref,
    real_in,
    imag_in,
    *outs,
):
    info_refs = (info_ref,) * 3
    first_field = SOURCES if chip else 0
    coarse_t = narrow(table_ref, "coarse_t")
    last = chip == CHIPS - 1
    real_ref, imag_ref = outs[2:] if last else outs
    residual = residual_ref[...]
    disc = disc_of(gain_ref[...])
    real_ref[...] = jnp.zeros((2, W, K), F32) if chip == 0 else real_in[...]
    imag_ref[...] = jnp.zeros((2, W, K), F32) if chip == 0 else imag_in[...]
    pad = jnp.zeros((K, K), F32)
    first = chip * SOURCES
    halves = []
    for source in range(first, first + SOURCES):
        field = field_ref.at[source - first_field]
        scaled = jnp.concatenate([residual * field[:, :W], residual * field[:, W:]], axis=1)
        half = product(terms(scaled), coarse_t).T
        halves.append(jnp.concatenate([half[:K], half[K:]], axis=1))
    spec = product(terms(jnp.concatenate(halves, axis=0)), coarse_t)
    for source in range(first, first + SOURCES):
        row, column = window_starts(info_refs, source)
        scale = disc * (2.0 * weight_of(info_refs, source))
        own = spec[(source - first) * K : (source - first) * K + K]
        for ref, part in ((real_ref, own[:, :K]), (imag_ref, own[:, K:])):
            spread = pltpu.roll(jnp.concatenate([part * scale, pad], axis=1), column, 1)
            for side in range(2):
                ref[side, pl.ds(row, K), :] += spread[:, side * K : side * K + K]
    if not last:
        return
    fold, fold_t = stored(table_ref, "fold"), stored(table_ref, "fold_t")
    real, imag = (
        exact_left(fold, jnp.concatenate([ref[0], ref[1]], axis=1)) for ref in (real_ref, imag_ref)
    )
    cosines = exact_right(jnp.concatenate([real[:K], -imag[K:]], axis=0), fold_t[:, :K])
    sines = exact_right(jnp.concatenate([-imag[:K], -real[K:]], axis=0), fold_t[:, K:])
    spectrum = terms(jnp.concatenate([cosines, sines], axis=1))
    lines_ref, rim_ref = outs[:2]
    place, _ = my_place()
    lines = [early_ref[pl.ds(SPOTS["mid"][at][0] + 2 * place, 2)].reshape(K, W) for at in range(2)]
    lines_ref[...] = product(lines, spectrum)
    outer = [early_ref[SPOTS["rims"][at][0] + 1 - place // 2] for at in range(2)]
    rim_ref[...] = product(outer, spectrum)


def rim_kernel(lines_ref, rim_ref, energy_ref, out_ref):
    chip, core = my_place()
    row, _ = my_tile()
    rim = rim_ref[...]
    out_ref[:A] = lines_ref[:A] + jnp.where((chip == 0) & (row > 0), rim, 0.0)
    out_ref[A:K] = lines_ref[A:] + jnp.where((chip == 3) & (row < TROWS - 1), rim, 0.0)
    energy = energy_ref[...]
    out_ref[K:] = jnp.concatenate([jnp.where(core == at, energy, 0.0) for at in range(2)], axis=1)


def pixels_kernel(mine_ref, other_ref, table_ref, inner_ref, side_ref):
    _, core = my_place()
    first = core == 0
    lines = mine_ref[...] + other_ref[...]
    top, bottom = lines[:A], lines[A:K]
    table = stored(table_ref, "sides")
    table = jnp.where(first, table[:, :K], table[:, K:])
    table = (table[:, :A], table[:, A:])
    side_ref[:A] = jnp.concatenate([product(terms(top), table), product(terms(bottom), table)], axis=1)
    lanes = lax.broadcasted_iota(jnp.int32, (8, K), 1)
    side_ref[A:] = jnp.where(lanes < A, lines[K:, :K], pltpu.roll(lines[K:, K:], A, 1))
    own = jnp.where(first, top, bottom)
    inner_ref[...] = product(terms(own), wide(table_ref, "mid_t"))


def join_kernel(inner_ref, before_ref, mine_ref, other_ref, out_ref, energy_ref):
    _, core = my_place()
    first = core == 0
    mine, other = mine_ref[...], other_ref[...]
    _, column = my_tile()
    left = jnp.where(column > 0, jnp.where(first, other[:A, :A], mine[:A, A:]), 0.0)
    right = jnp.where(column < TCOLS - 1, jnp.where(first, mine[:A, :A], other[:A, A:]), 0.0)
    inner = inner_ref[...]
    pad = jnp.zeros((A, A), F32)
    out_ref[0, :, :K] = inner[:, :K] + jnp.concatenate([left, pad], axis=1)
    out_ref[0, :, K : PIX - K] = inner[:, K : PIX - K]
    out_ref[0, :, PIX - K :] = inner[:, PIX - K :] + jnp.concatenate([pad, right], axis=1)
    odd = lax.rem(column, 2)
    total = before_ref[A : A + 1] + jnp.where(core == odd, mine[A : A + 1], other[A : A + 1])
    total = pltpu.roll(total, core * A, 1) * (16.0 / (TROWS * TCOLS * PIX * PIX))
    energy_ref[...] = total[0, :SOURCES]


def swap_cores(value):
    return lax.ppermute(value, "src", [(at, at ^ 1) for at in range(8)])


def chip_swap(value, low):
    pairs = []
    for source in range(2 * CHIPS):
        for tile in range(TROWS * TCOLS):
            step = 1 if tile % 2 == low else -1
            partner = (source // 2 + step) % CHIPS * 2 + source % 2
            pairs.append((source * 32 + tile, partner * 32 + (tile ^ 1)))
    return lax.ppermute(value, BOTH, pairs)


def tile_move(value, shift_of):
    pairs = []
    for source in range(2 * CHIPS):
        down, right = shift_of(source)
        turns = shift_of(source ^ 1) == (-down, -right)
        for row in range(TROWS):
            for column in range(TCOLS):
                to_row, to_column = row + down, column + right
                inside = 0 <= to_row < TROWS and 0 <= to_column < TCOLS
                to = to_row % TROWS * TCOLS + to_column % TCOLS
                to = source * 32 + to if inside or not turns else (source ^ 1) * 32 + row * TCOLS + column
                pairs.append((source * 32 + row * TCOLS + column, to))
    return lax.ppermute(value, BOTH, pairs)


def tile_swap(value, step):
    def partner(at):
        y, x, z = at // TCOLS, at // 2 % 4, at % 2
        if step == 0:
            z = 1 - z
        elif step < 3:
            x = x ^ 1 if step == 1 else 3 - x
        else:
            y = y ^ 1 if step == 3 else 3 - y
        return y * TCOLS + x * 2 + z

    return lax.ppermute(value, "tile", [(at, partner(at)) for at in range(TROWS * TCOLS)])


def tied(*values):
    return lax.optimization_barrier(values)


def body(mask_tiles, target, pupil_gain, weights, freq_index):
    core = lax.axis_index("src") % 2
    edge = jnp.where(core == 0, mask_tiles[0, PIX - A :], mask_tiles[0, :A])
    mine = tile_move(edge, lambda source: (1, 0) if source % 2 == 0 else (-1, 0))
    rows, rim_table = call(own_kernel, [(W, PIX), (W, W)], [mask_tiles, EARLY], "own", 400_000_000, bf16=(1,))
    rows, weights, freq_index = tied(rows, weights, freq_index)
    mine, rows = tied(mine, rows)
    other = swap_cores(mine)
    lanes = lax.broadcasted_iota(jnp.int32, freq_index.shape, 2)
    info = jnp.where(lanes == 1, weights[:, None, None], freq_index.astype(F32))
    near = chip_swap(info, 1)
    rows, side = call(
        rows_kernel, [(W, PIX), (K, K)], [rows, mine, other, rim_table], "rows", 100_000_000
    )
    my_side = tile_move(side, lambda source: (0, 1) if source % 2 == 0 else (0, -1))
    (basis,) = call(columns_kernel, [(W, W)], [rows, EARLY, LATE], "columns", 200_000_000)
    far = chip_swap(jnp.concatenate([info, near]), 0)
    my_side, basis = tied(my_side, basis)
    other_side = swap_cores(my_side)
    own_field, total, real, imag = call(
        image_kernel,
        [(SOURCES, W, 2 * W), (W, W), (2, W, K), (2, W, K)],
        [info, basis, my_side, other_side, pupil_gain, EARLY, LATE],
        "image",
        2_000_000_000,
        smem=(0,),
    )
    field, mine = call(
        others_kernel,
        [((CHIPS - 1) * SOURCES, W, 2 * W), (W, W)],
        [near, far, pupil_gain, LATE, real, imag, total],
        "others",
        5_000_000_000,
        smem=(0, 1),
    )
    other = swap_cores(mine)
    (wanted,) = call(wanted_kernel, [(W, W)], [target, LATE], "wanted", 600_000_000)
    other, wanted = tied(other, wanted)
    residual, energies = call(
        residual_kernel, [(W, W), (8, K)], [mine, other, wanted, own_field, LATE], "residual", 300_000_000
    )
    plane = pltpu.VMEM((2, W, K), F32)
    planes = (jnp.zeros((8, K), F32),) * 2
    for chip in range(CHIPS):
        arrived = tile_swap(energies, (2, 4, 1, 3)[chip])
        last = chip == CHIPS - 1
        outs = call(
            functools.partial(adjoint_kernel, chip),
            [(K, W), (A, W)] if last else [(2, W, K), (2, W, K)],
            [(info, near, far, far)[chip], residual, field if chip else own_field, pupil_gain, LATE, EARLY, *planes],
            "adjoint",
            1_500_000_000,
            scratch=(plane, plane) if last else (),
            smem=(0,),
        )
        planes = outs
        *planes, energies = tied(*planes, energies + arrived)
    lines, rim = planes
    from_rows = tile_move(rim, lambda source: (1, 0) if source < CHIPS else (-1, 0))
    (mine,) = call(rim_kernel, [(K + 8, W)], [lines, from_rows, energies], "rim", K * K)
    other = swap_cores(mine)
    inner, side = call(
        pixels_kernel,
        [(A, PIX), (A + 8, K)],
        [mine, other, EARLY],
        "pixels",
        100_000_000,
    )
    my_side = tile_move(side, lambda source: (0, -1) if source % 2 == 0 else (0, 1))
    other_side = swap_cores(my_side)
    mask_grad, weight_grad = call(
        join_kernel, [(1, A, PIX), (SOURCES,)], [inner, side, my_side, other_side], "join", A * PIX
    )
    return mask_grad, weight_grad


def solution(mesh):
    placed = (P("tile", None, None), P("tile", None, None), P(), P("src"), P("src", None, None))
    return jax.shard_map(
        body,
        mesh=mesh,
        in_specs=placed,
        out_specs=(P("tile", "src", None), P("src")),
        check_vma=False,
    )
```
